32 devices in a mesh: row: 4 (over z), col: 8 (over y, x, core).
Axes of the slice: x: 2, y: 2, z: 4, core: 2. Of those that a mesh axis runs over, the one named last changes fastest.
Arguments:
- tile_data: bfloat16 [4, 8, 32, 256, 256], P('row', 'col'), may hold values from -0.125 to 0.125
- tile_row_block: int32 [4, 8, 32], P('row', 'col'), may hold values from 0 to 63
- tile_column_block: int32 [4, 8, 32], P('row', 'col'), may hold values from 0 to 63
- tile_count: int32 [4, 8], P('row', 'col'), may hold values from 1 to 32, as said below
- saved_primal: float32 [3, 131072], P(None, 'col'), may hold values from 0 to 1
- saved_dual: float32 [3, 65536], P(None, 'row'), may hold values from 0 to 1
- primal_mask: int32 [3, 131072], P(None, 'col'), may hold values 0 or 1
- dual_mask: int32 [3, 65536], P(None, 'row'), may hold values 0 or 1
- cost_vector: float32 [131072], P('col'), may hold values from -6 to 6
- demand: float32 [65536], P('row'), may hold values from -6 to 6
- upper_bound: float32 [131072], P('col'), may hold values from 0.5 to 1.5
- step_sizes: float32 [2], replicated, may hold values from 0.2 to 0.4
- primal_cotangent: float32 [131072], P('col'), may hold values from -6 to 6
- dual_cotangent: float32 [65536], P('row'), may hold values from -6 to 6
Outputs:
- primal_adjoint: float32 [131072], P('col')
- dual_adjoint: float32 [65536], P(('row', 'col'))
- step_gradients: float32 [2], replicated
The draws below stay inside these ranges and needn't reach their ends.
Inputs may be any that keep to these rules, and one draw needn't show every extreme that they name: `tile_count`: block positions may repeat, and tiles at one position add; slots at and beyond a device's count are ignored. In every index of row some device has 32 live slots.
All inputs are finite; a program needn't handle non-finite values. No bound on the sum of `primal_mask` or of `dual_mask` on one device may be relied on, other than what follows from the above.
Results may differ from the reference program's by a relative error of at most 0.00071.
Values may be sent and summed in bfloat16 or wider, within the bound.
No kernel may reach another device: no remote copies, remote signals or barrier semaphores. Data moves between devices by JAX's collectives and lax.ppermute only.
A program may use at most 64 MiB of HBM per device.

```python
import math
import jax
import jax.numpy as jnp
from jax import lax

TILE = 256
RB_DEV = 64
CB_DEV = 64
TILES_DEV = 32
ITERS = 3
ROWS_DEV = 16384
COLS_DEV = 16384
NROW = 65536
NCOL = 131072
N_ROW = 4
N_COL = 8


def draw_tile_count(key, part):
    light_counts = jax.random.randint(key, (N_ROW, N_COL), 1, TILES_DEV // 2 + 1)
    heavy_place = jax.random.randint(jax.random.fold_in(key, 7), (N_ROW, 1), 0, N_COL)
    places = jnp.arange(N_COL)[None, :]
    return jnp.where(places == heavy_place, TILES_DEV, light_counts).astype(jnp.int32)


def plant(array, own_key, smallest, largest):
    spot = [jax.random.randint(jax.random.fold_in(own_key, axis), (), 0, length) for axis, length in enumerate(array.shape)]
    main_axis = array.shape.index(max(array.shape))
    beside = spot[:main_axis] + [(spot[main_axis] + 1) % array.shape[main_axis]] + spot[main_axis + 1:]
    return array.at[tuple(spot)].set(smallest).at[tuple(beside)].set(largest)


def levels(stream_key, dims, shards, smallest, largest):
    def one(axis_at, blocks):
        steps = jax.random.uniform(jax.random.fold_in(jax.random.fold_in(stream_key, 6), axis_at), (blocks,), jnp.float32, smallest / len(shards), largest / len(shards))
        return jnp.repeat(jnp.exp(steps), dims[axis_at] // blocks).reshape((-1,) + (1,) * (len(dims) - axis_at - 1))

    level = one(*shards[0])
    for cut in shards[1:]:
        level = level * one(*cut)
    return level


def centred(stream_key, extent, deviation, reach, shards=(), kind=jnp.bfloat16):
    factor_of = levels(stream_key, extent, shards, -0.22, 0.18) if shards else 1.0
    entries = jax.random.normal(stream_key, extent, jnp.float32) * deviation * factor_of
    return jnp.minimum(jnp.maximum(entries, -reach), reach).astype(kind)


def setup_inputs(seed: int = 0) -> dict:
    key_list = jax.random.split(jax.random.key(seed), 15)
    return {
        "tile_data": centred(key_list[0], (N_ROW, N_COL, TILES_DEV, TILE, TILE), (8 * TILE) ** -0.5, 0.125, ((0, 4), (1, 8))),
        "tile_row_block": plant(jax.random.randint(key_list[1], (N_ROW, N_COL, TILES_DEV), 0, RB_DEV), jax.random.fold_in(key_list[1], 1), 0, RB_DEV - 1).astype(jnp.int32),
        "tile_column_block": plant(jax.random.randint(key_list[2], (N_ROW, N_COL, TILES_DEV), 0, CB_DEV), jax.random.fold_in(key_list[2], 1), 0, CB_DEV - 1).astype(jnp.int32),
        "tile_count": draw_tile_count(jax.random.fold_in(key_list[14], 71), 0),
        "saved_primal": jnp.clip(1.0 * jax.random.uniform(key_list[4], (ITERS, NCOL), jnp.float32) ** levels(key_list[4], (ITERS, NCOL), ((1, 8),), -0.2, 0.2), 0.0, 1.0),
        "saved_dual": jnp.clip(1.0 * jax.random.uniform(key_list[5], (ITERS, NROW), jnp.float32) ** levels(key_list[5], (ITERS, NROW), ((1, 4),), -0.2, 0.2), 0.0, 1.0),
        "primal_mask": plant((jax.random.randint(key_list[6], (ITERS, NCOL), 0, 4) < 3).astype(jnp.int32), jax.random.fold_in(key_list[6], 1), 0, 1),
        "dual_mask": plant((jax.random.randint(key_list[7], (ITERS, NROW), 0, 2) < 1).astype(jnp.int32), jax.random.fold_in(key_list[7], 1), 0, 1),
        "cost_vector": centred(key_list[8], (NCOL,), 1.0, 6.0, ((0, 8),), jnp.float32),
        "demand": centred(key_list[9], (NROW,), 1.0, 6.0, ((0, 4),), jnp.float32),
        "upper_bound": jnp.clip(0.5 + 1.0 * jax.random.uniform(key_list[10], (NCOL,), jnp.float32) ** levels(key_list[10], (NCOL,), ((0, 8),), -0.2, 0.2), 0.5, 1.5),
        "step_sizes": jnp.clip(jnp.exp(jax.random.uniform(key_list[11], (2,), jnp.float32, math.log(0.2), math.log(0.4))), 0.2, 0.4),
        "primal_cotangent": centred(key_list[12], (NCOL,), 1.0, 6.0, ((0, 8),), jnp.float32),
        "dual_cotangent": centred(key_list[13], (NROW,), 1.0, 6.0, ((0, 4),), jnp.float32),
    }


def apply_tiles(tile_data, tile_row_block, tile_column_block, tile_count, vectors, transpose):
    devices = N_ROW * N_COL
    stacked = tile_data.reshape(devices, TILES_DEV, TILE, TILE)
    rows_flat = tile_row_block.reshape(devices, TILES_DEV)
    cols_flat = tile_column_block.reshape(devices, TILES_DEV)
    counts = tile_count.reshape(devices)
    batch = vectors.shape[0]

    def device_term(inputs):
        tiles_here, rows_here, cols_here, count_here, device = inputs
        grid_row = device // N_COL
        grid_column = device % N_COL
        if transpose:
            piece = lax.dynamic_slice_in_dim(vectors, (grid_row * ROWS_DEV).astype(jnp.int32), ROWS_DEV, 1)
            in_index, out_index, out_blocks = (rows_here, cols_here, CB_DEV)
            einsum_form = 'sij,bsi->bsj'
        else:
            piece = lax.dynamic_slice_in_dim(vectors, (grid_column * COLS_DEV).astype(jnp.int32), COLS_DEV, 1)
            in_index, out_index, out_blocks = (cols_here, rows_here, RB_DEV)
            einsum_form = 'sij,bsj->bsi'
        blocks = piece.reshape(batch, -1, TILE).astype(jnp.float32)
        picked = jnp.take(blocks, in_index, axis=1)
        products = jnp.einsum(einsum_form, tiles_here.astype(jnp.float32), picked, precision=lax.Precision.HIGHEST)
        live_slots = (jnp.arange(TILES_DEV, dtype=jnp.int32) < count_here).astype(jnp.float32)
        products = products * live_slots[None, :, None]
        selector = (out_index[:, None] == jnp.arange(out_blocks, dtype=jnp.int32)[None, :]).astype(jnp.float32)
        summed = jnp.einsum('sn,bsi->bni', selector, products, precision=lax.Precision.HIGHEST)
        return summed.reshape(batch, out_blocks * TILE)
    terms = lax.map(device_term, (stacked, rows_flat, cols_flat, counts, jnp.arange(devices, dtype=jnp.int32)))
    if transpose:
        summed = terms.reshape(N_ROW, N_COL, batch, COLS_DEV).sum(axis=0)
        return jnp.transpose(summed, (1, 0, 2)).reshape(batch, NCOL)
    summed = terms.reshape(N_ROW, N_COL, batch, ROWS_DEV).sum(axis=1)
    return jnp.transpose(summed, (1, 0, 2)).reshape(batch, NROW)

def reference(tile_data, tile_row_block, tile_column_block, tile_count, saved_primal, saved_dual, primal_mask, dual_mask, cost_vector, demand, upper_bound, step_sizes, primal_cotangent, dual_cotangent):
    tau = step_sizes[0]
    sigma = step_sizes[1]
    grid = (tile_data, tile_row_block, tile_column_block, tile_count)
    masks_x = primal_mask.astype(jnp.float32)
    masks_y = dual_mask.astype(jnp.float32)
    reduced = cost_vector[None, :] - apply_tiles(*grid, saved_dual.astype(jnp.bfloat16), True)
    half = jnp.clip(saved_primal - tau * reduced, 0.0, upper_bound[None, :])
    extrapolated = (2.0 * half - saved_primal).astype(jnp.bfloat16)
    residual = demand[None, :] - apply_tiles(*grid, extrapolated, False)
    adjoint_x = primal_cotangent
    adjoint_y = dual_cotangent
    anchor_x = jnp.zeros_like(adjoint_x)
    anchor_y = jnp.zeros_like(adjoint_y)
    tau_sum = jnp.zeros((), jnp.float32)
    sigma_sum = jnp.zeros((), jnp.float32)
    for step in reversed(range(ITERS)):
        weight = (step + 1.0) / (step + 2.0)
        anchor_x = anchor_x + (1.0 - weight) * adjoint_x
        anchor_y = anchor_y + (1.0 - weight) * adjoint_y
        dual_term = masks_y[step] * weight * adjoint_y
        sigma_sum = sigma_sum + jnp.sum(dual_term * residual[step])
        back = apply_tiles(*grid, dual_term.astype(jnp.bfloat16)[None, :], True)[0]
        primal_term = masks_x[step] * (weight * adjoint_x - 2.0 * sigma * back)
        tau_sum = tau_sum + jnp.sum(-primal_term * reduced[step])
        adjoint_x = primal_term + sigma * back
        image = apply_tiles(*grid, primal_term.astype(jnp.bfloat16)[None, :], False)[0]
        adjoint_y = dual_term + tau * image
    gradients = jnp.stack([tau_sum / math.sqrt(NCOL), sigma_sum / math.sqrt(NROW)])
    return (adjoint_x + anchor_x, adjoint_y + anchor_y, gradients)
```

```python
import functools
import math

import jax
import jax.numpy as jnp
from jax import lax
from jax.experimental import pallas as pl
from jax.experimental.pallas import tpu as pltpu
from jax.sharding import PartitionSpec as P

LANES = 128
VMEM = pl.BlockSpec(memory_space=pltpu.VMEM)
SMEM = pl.BlockSpec(memory_space=pltpu.SMEM)
GRANT = 32 * 1024 * 1024


def accumulate(transpose, in_index, out_index, count, tiles, source, slot_of, total):
    slots, width, _ = tiles.shape
    per_block = width // LANES
    vectors = total.shape[0]
    total[...] = jnp.zeros_like(total)
    live_count = count[0, 0]
    rows = max(8, vectors)
    for slot in range(slots):
        start = slot_of(in_index[0, 0, slot] * per_block)
        place = out_index[0, 0, slot] * per_block
        live = (live_count > slot).astype(jnp.float32)
        halves = []
        for half in range(per_block):
            if vectors == 1:
                halves.append(source[0, pl.ds(start + half, 1), :])
            else:
                which = lax.broadcasted_iota(jnp.int32, (rows, LANES), 0)
                stacked = jnp.zeros((rows, LANES), jnp.float32)
                for vector in range(vectors):
                    line = source[vector, pl.ds(start + half, 1), :]
                    stacked = jnp.where(which == vector, line, stacked)
                halves.append(stacked)
        block = (jnp.concatenate(halves, axis=1) * live).astype(jnp.bfloat16)
        contract = ((1,), (0,)) if transpose else ((1,), (1,))
        product = lax.dot_general(
            block, tiles[slot], (contract, ((), ())), preferred_element_type=jnp.float32
        )
        for vector in range(vectors):
            for half in range(per_block):
                at = pl.ds(place + half, 1)
                total[vector, at, :] += product[
                    vector : vector + 1, half * LANES : (half + 1) * LANES
                ]


def apply_body(transpose, parts_in, parts_out, vectors, *refs):
    in_index, out_index, count, place_in, place_out, tiles = refs[:6]
    parts = refs[6 : 6 + parts_in]
    outs = refs[6 + parts_in : 6 + parts_in + parts_out]
    source, total = refs[6 + parts_in + parts_out :]
    length = source.shape[1] // parts_in
    for part in range(parts_in):
        source[:, part * length : (part + 1) * length, :] = (
            parts[part][...].astype(jnp.float32).reshape(vectors, length, LANES)
        )

    def slot_of(row):
        if parts_in == 1:
            return row
        owner = row // length
        return (owner ^ place_in[0]) * length + (row - owner * length)

    accumulate(transpose, in_index, out_index, count, tiles, source, slot_of, total)
    size = total.shape[1] // parts_out
    for part in range(parts_out):
        first = pl.multiple_of((place_out[0] ^ part) * size, size)
        outs[part][...] = total[:, pl.ds(first, size), :].reshape(outs[part].shape)


def apply_tiles(transpose, grid, place_in, place_out, parts, out_rows, parts_out, vectors, name):
    tiles, row_blocks, column_blocks, count = grid
    in_rows = sum(part.size for part in parts) // (vectors * LANES)
    size = out_rows // parts_out
    shape = (size, LANES) if vectors == 1 else (vectors, size, LANES)
    order = (row_blocks, column_blocks) if transpose else (column_blocks, row_blocks)
    return pl.pallas_call(
        functools.partial(apply_body, transpose, len(parts), parts_out, vectors),
        out_shape=[jax.ShapeDtypeStruct(shape, jnp.float32)] * parts_out,
        in_specs=[SMEM] * 5 + [VMEM] * (1 + len(parts)),
        out_specs=[VMEM] * parts_out,
        scratch_shapes=[
            pltpu.VMEM((vectors, in_rows, LANES), jnp.float32),
            pltpu.VMEM((vectors, out_rows, LANES), jnp.float32),
        ],
        compiler_params=pltpu.CompilerParams(vmem_limit_bytes=GRANT),
        cost_estimate=pl.CostEstimate(
            flops=2 * tiles.size * vectors, bytes_accessed=2 * tiles.size, transcendentals=0
        ),
        name=name,
    )(*order, count, place_in, place_out, tiles, *parts)


def exchange(parts, axis):
    size = len(parts)
    return [parts[0]] + [
        lax.ppermute(parts[k], axis, [(i, i ^ k) for i in range(size)]) for k in range(1, size)
    ]


def tree_sum(parts):
    while len(parts) > 1:
        parts = [parts[i] + parts[i + 1] for i in range(0, len(parts), 2)]
    return parts[0]


def local(
    tile_data,
    tile_row_block,
    tile_column_block,
    tile_count,
    saved_primal,
    saved_dual,
    primal_mask,
    dual_mask,
    cost_vector,
    demand,
    upper_bound,
    step_sizes,
    primal_cotangent,
    dual_cotangent,
):
    slot_count = tile_data.shape[2]
    tile_width = tile_data.shape[-1]
    tiles = tile_data.reshape(slot_count, tile_width, tile_width)
    grid = (tiles, tile_row_block, tile_column_block, tile_count)
    iterations = saved_primal.shape[0]
    row_length = saved_dual.shape[1]
    column_length = saved_primal.shape[1]
    n_row = lax.axis_size("row")
    n_col = lax.axis_size("col")
    me_row = lax.axis_index("row")
    me_col = lax.axis_index("col")
    at_row = me_row.reshape(1).astype(jnp.int32)
    at_col = me_col.reshape(1).astype(jnp.int32)
    lines_y = row_length // LANES
    lines_x = column_length // LANES
    share_y = lines_y // n_col
    share_x = lines_x // n_row
    tau = step_sizes[0]
    sigma = step_sizes[1]

    def own_y(array):
        lead = array.shape[:-1]
        array = array.reshape(lead + (lines_y, LANES))
        return lax.dynamic_slice_in_dim(array, me_col * share_y, share_y, len(lead))

    def own_x(array):
        lead = array.shape[:-1]
        array = array.reshape(lead + (lines_x, LANES))
        return lax.dynamic_slice_in_dim(array, me_row * share_x, share_x, len(lead))

    def weight_of(step):
        return (step + 1.0) / (step + 2.0)

    last = iterations - 1
    first_term = (
        dual_mask[last].astype(jnp.float32) * weight_of(last) * dual_cotangent
    ).reshape(lines_y, LANES)
    first_parts = [first_term.astype(jnp.bfloat16)]
    back_parts = apply_tiles(
        True, grid, at_col, at_row, first_parts, lines_x, n_row, 1, "back_first"
    )

    saved = saved_dual.astype(jnp.bfloat16).reshape(iterations, lines_y, LANES)
    saved_parts = apply_tiles(
        True, grid, at_col, at_row, [saved], lines_x, n_row, iterations, "back_saved"
    )

    adjoint_x = own_x(primal_cotangent)
    adjoint_y = own_y(dual_cotangent)
    masks_x = own_x(primal_mask).astype(jnp.float32)
    masks_y = own_y(dual_mask).astype(jnp.float32)
    anchor_x = jnp.zeros_like(adjoint_x)
    anchor_y = jnp.zeros_like(adjoint_y)
    tau_terms = []
    sigma_terms = []
    reduced = None
    for step in reversed(range(iterations)):
        weight = weight_of(step)
        anchor_x = anchor_x + (1.0 - weight) * adjoint_x
        anchor_y = anchor_y + (1.0 - weight) * adjoint_y
        dual_term = masks_y[step] * weight * adjoint_y
        sigma_terms.append((step, dual_term))
        if back_parts is None:
            gathered = exchange([dual_term.astype(jnp.bfloat16)] * n_col, "col")
            back_parts = apply_tiles(
                True, grid, at_col, at_row, gathered, lines_x, n_row, 1, f"back_{step}"
            )
        back = tree_sum(exchange(back_parts, "row"))
        back_parts = None
        primal_term = masks_x[step] * (weight * adjoint_x - 2.0 * sigma * back)
        tau_terms.append((step, primal_term))
        adjoint_x = primal_term + sigma * back
        gathered = exchange([primal_term.astype(jnp.bfloat16)] * n_row, "row")
        image_parts = apply_tiles(
            False, grid, at_row, at_col, gathered, lines_y, n_col, 1, f"image_{step}"
        )
        if reduced is None:
            reduced = own_x(cost_vector) - tree_sum(exchange(saved_parts, "row"))
            primal = own_x(saved_primal)
            half = jnp.clip(primal - tau * reduced, 0.0, own_x(upper_bound))
            extrapolated = (2.0 * half - primal).astype(jnp.bfloat16)
            extrapolated = exchange([extrapolated] * n_row, "row")
            residual_parts = apply_tiles(
                False,
                grid,
                at_row,
                at_col,
                extrapolated,
                lines_y,
                n_col,
                iterations,
                "image_saved",
            )
        image = tree_sum(exchange(image_parts, "col"))
        adjoint_y = dual_term + tau * image
    residual = own_y(demand) - tree_sum(exchange(residual_parts, "col"))

    tau_sum = -sum(jnp.sum(term * reduced[step]) for step, term in tau_terms)
    sigma_sum = sum(jnp.sum(term * residual[step]) for step, term in sigma_terms)
    sums = jnp.stack([tau_sum, sigma_sum])
    spots = lax.broadcasted_iota(jnp.int32, (8, LANES), 1)
    packed = jnp.where(spots == 0, sums[0], jnp.where(spots == 1, sums[1], 0.0))
    packed = tree_sum(exchange([packed] * n_row, "row"))
    packed = tree_sum(exchange([packed] * n_col, "col"))
    total_columns = column_length * n_col
    total_rows = row_length * n_row
    scales = jnp.array(
        [1.0 / math.sqrt(total_columns), 1.0 / math.sqrt(total_rows)], jnp.float32
    )
    gradients = packed[0, :2] * scales

    final_x = exchange([adjoint_x + anchor_x] * n_row, "row")
    primal_adjoint = jnp.zeros((n_row, share_x, LANES), jnp.float32)
    for part in range(n_row):
        primal_adjoint = lax.dynamic_update_index_in_dim(
            primal_adjoint, final_x[part], me_row ^ part, 0
        )
    primal_adjoint = primal_adjoint.reshape(column_length)
    dual_adjoint = (adjoint_y + anchor_y).reshape(row_length // n_col)
    return (primal_adjoint, dual_adjoint, gradients)


def solution(mesh):
    placed = (
        P("row", "col", None, None, None),
        P("row", "col", None),
        P("row", "col", None),
        P("row", "col"),
        P(None, "col"),
        P(None, "row"),
        P(None, "col"),
        P(None, "row"),
        P("col"),
        P("row"),
        P("col"),
        P(),
        P("col"),
        P("row"),
    )
    return jax.shard_map(
        local,
        mesh=mesh,
        in_specs=placed,
        out_specs=(P("col"), P(("row", "col")), P()),
        check_vma=False,
    )
```

```python
import functools
import math

import jax
import jax.numpy as jnp
from jax import lax
from jax.experimental import pallas as pl
from jax.experimental.pallas import tpu as pltpu
from jax.sharding import PartitionSpec as P

LANES = 128
VMEM = pl.BlockSpec(memory_space=pltpu.VMEM)
SMEM = pl.BlockSpec(memory_space=pltpu.SMEM)
GRANT = 32 * 1024 * 1024


def accumulate(transpose, in_index, out_index, count, tiles, source, total):
    slots, width, _ = tiles.shape
    per_block = width // LANES
    vectors = total.shape[0]
    total[...] = jnp.zeros_like(total)
    live_count = count[0, 0]
    rows = max(8, vectors)
    for slot in range(slots):
        start = in_index[0, 0, slot] * per_block
        place = out_index[0, 0, slot] * per_block
        live = (live_count > slot).astype(jnp.float32)
        halves = []
        for half in range(per_block):
            if vectors == 1:
                halves.append(source[0, pl.ds(start + half, 1), :])
            else:
                which = lax.broadcasted_iota(jnp.int32, (rows, LANES), 0)
                stacked = jnp.zeros((rows, LANES), jnp.float32)
                for vector in range(vectors):
                    line = source[vector, pl.ds(start + half, 1), :]
                    stacked = jnp.where(which == vector, line, stacked)
                halves.append(stacked)
        block = (jnp.concatenate(halves, axis=1) * live).astype(jnp.bfloat16)
        contract = ((1,), (0,)) if transpose else ((1,), (1,))
        product = lax.dot_general(
            block, tiles[slot], (contract, ((), ())), preferred_element_type=jnp.float32
        )
        for vector in range(vectors):
            for half in range(per_block):
                at = pl.ds(place + half, 1)
                total[vector, at, :] += product[
                    vector : vector + 1, half * LANES : (half + 1) * LANES
                ]


def apply_body(transpose, in_index, out_index, count, tiles, parts, out, source, total):
    for part in range(parts.shape[0]):
        length = parts.shape[2]
        source[:, part * length : (part + 1) * length, :] = parts[part].astype(jnp.float32)
    accumulate(transpose, in_index, out_index, count, tiles, source, total)
    size = out.shape[2]
    for part in range(out.shape[0]):
        out[part] = total[:, part * size : (part + 1) * size, :]


def apply_tiles(transpose, grid, parts, out_rows, parts_out, name):
    tiles, row_blocks, column_blocks, count = grid
    parts_in, vectors, length, _ = parts.shape
    shape = (parts_out, vectors, out_rows // parts_out, LANES)
    order = (row_blocks, column_blocks) if transpose else (column_blocks, row_blocks)
    return pl.pallas_call(
        functools.partial(apply_body, transpose),
        out_shape=jax.ShapeDtypeStruct(shape, jnp.float32),
        in_specs=[SMEM] * 3 + [VMEM] * 2,
        out_specs=VMEM,
        scratch_shapes=[
            pltpu.VMEM((vectors, parts_in * length, LANES), jnp.float32),
            pltpu.VMEM((vectors, out_rows, LANES), jnp.float32),
        ],
        compiler_params=pltpu.CompilerParams(vmem_limit_bytes=GRANT),
        cost_estimate=pl.CostEstimate(
            flops=2 * tiles.size * vectors, bytes_accessed=2 * tiles.size, transcendentals=0
        ),
        name=name,
    )(*order, count, tiles, parts)


def scatter_sum(parts, axis):
    return lax.all_to_all(parts, axis, 0, 0).sum(axis=0)


def gather(part, axis):
    size = lax.axis_size(axis)
    return lax.all_to_all(jnp.broadcast_to(part, (size,) + part.shape), axis, 0, 0)


def local(
    tile_data,
    tile_row_block,
    tile_column_block,
    tile_count,
    saved_primal,
    saved_dual,
    primal_mask,
    dual_mask,
    cost_vector,
    demand,
    upper_bound,
    step_sizes,
    primal_cotangent,
    dual_cotangent,
):
    slot_count = tile_data.shape[2]
    tile_width = tile_data.shape[-1]
    tiles = tile_data.reshape(slot_count, tile_width, tile_width)
    grid = (tiles, tile_row_block, tile_column_block, tile_count)
    iterations = saved_primal.shape[0]
    row_length = saved_dual.shape[1]
    column_length = saved_primal.shape[1]
    n_row = lax.axis_size("row")
    n_col = lax.axis_size("col")
    me_row = lax.axis_index("row")
    me_col = lax.axis_index("col")
    lines_y = row_length // LANES
    lines_x = column_length // LANES
    share_y = lines_y // n_col
    share_x = lines_x // n_row
    tau = step_sizes[0]
    sigma = step_sizes[1]

    def own_y(array):
        lead = array.shape[:-1]
        array = array.reshape(lead + (lines_y, LANES))
        return lax.dynamic_slice_in_dim(array, me_col * share_y, share_y, len(lead))

    def own_x(array):
        lead = array.shape[:-1]
        array = array.reshape(lead + (lines_x, LANES))
        return lax.dynamic_slice_in_dim(array, me_row * share_x, share_x, len(lead))

    def weight_of(step):
        return (step + 1.0) / (step + 2.0)

    last = iterations - 1
    first_term = (
        dual_mask[last].astype(jnp.float32) * weight_of(last) * dual_cotangent
    ).reshape(1, 1, lines_y, LANES)
    first_part = first_term.astype(jnp.bfloat16)
    back_parts = apply_tiles(True, grid, first_part, lines_x, n_row, "back_first")

    saved = saved_dual.astype(jnp.bfloat16).reshape(1, iterations, lines_y, LANES)
    saved_parts = apply_tiles(True, grid, saved, lines_x, n_row, "back_saved")

    adjoint_x = own_x(primal_cotangent)
    adjoint_y = own_y(dual_cotangent)
    masks_x = own_x(primal_mask).astype(jnp.float32)
    masks_y = own_y(dual_mask).astype(jnp.float32)
    anchor_x = jnp.zeros_like(adjoint_x)
    anchor_y = jnp.zeros_like(adjoint_y)
    tau_terms = []
    sigma_terms = []
    reduced = None
    for step in reversed(range(iterations)):
        weight = weight_of(step)
        anchor_x = anchor_x + (1.0 - weight) * adjoint_x
        anchor_y = anchor_y + (1.0 - weight) * adjoint_y
        dual_term = masks_y[step] * weight * adjoint_y
        sigma_terms.append((step, dual_term))
        if back_parts is None:
            gathered = gather(dual_term.astype(jnp.bfloat16)[None], "col")
            back_parts = apply_tiles(True, grid, gathered, lines_x, n_row, f"back_{step}")
        back = scatter_sum(back_parts, "row")[0]
        back_parts = None
        primal_term = masks_x[step] * (weight * adjoint_x - 2.0 * sigma * back)
        tau_terms.append((step, primal_term))
        adjoint_x = primal_term + sigma * back
        gathered = gather(primal_term.astype(jnp.bfloat16)[None], "row")
        image_parts = apply_tiles(False, grid, gathered, lines_y, n_col, f"image_{step}")
        if reduced is None:
            reduced = own_x(cost_vector) - scatter_sum(saved_parts, "row")
            primal = own_x(saved_primal)
            half = jnp.clip(primal - tau * reduced, 0.0, own_x(upper_bound))
            extrapolated = (2.0 * half - primal).astype(jnp.bfloat16)
            extrapolated = gather(extrapolated, "row")
            residual_parts = apply_tiles(
                False, grid, extrapolated, lines_y, n_col, "image_saved"
            )
        image = scatter_sum(image_parts, "col")[0]
        adjoint_y = dual_term + tau * image
    residual = own_y(demand) - scatter_sum(residual_parts, "col")

    tau_sum = -sum(jnp.sum(term * reduced[step]) for step, term in tau_terms)
    sigma_sum = sum(jnp.sum(term * residual[step]) for step, term in sigma_terms)
    sums = jnp.stack([tau_sum, sigma_sum])
    spots = lax.broadcasted_iota(jnp.int32, (8, LANES), 1)
    packed = jnp.where(spots == 0, sums[0], jnp.where(spots == 1, sums[1], 0.0))
    packed = gather(packed, "row").sum(axis=0)
    packed = gather(packed, "col").sum(axis=0)
    total_columns = column_length * n_col
    total_rows = row_length * n_row
    scales = jnp.array(
        [1.0 / math.sqrt(total_columns), 1.0 / math.sqrt(total_rows)], jnp.float32
    )
    gradients = packed[0, :2] * scales

    primal_adjoint = gather(adjoint_x + anchor_x, "row").reshape(column_length)
    dual_adjoint = (adjoint_y + anchor_y).reshape(row_length // n_col)
    return (primal_adjoint, dual_adjoint, gradients)


def solution(mesh):
    placed = (
        P("row", "col", None, None, None),
        P("row", "col", None),
        P("row", "col", None),
        P("row", "col"),
        P(None, "col"),
        P(None, "row"),
        P(None, "col"),
        P(None, "row"),
        P("col"),
        P("row"),
        P("col"),
        P(),
        P("col"),
        P("row"),
    )
    return jax.shard_map(
        local,
        mesh=mesh,
        in_specs=placed,
        out_specs=(P("col"), P(("row", "col")), P()),
        check_vma=False,
    )
```

```python
import functools
import math

import jax
import jax.numpy as jnp
from jax import lax
from jax.experimental import pallas as pl
from jax.experimental.pallas import tpu as pltpu
from jax.sharding import PartitionSpec as P

LANES = 128
EXTRA = 16
CHUNKS = 4
VMEM = pl.BlockSpec(memory_space=pltpu.VMEM)
SMEM = pl.BlockSpec(memory_space=pltpu.SMEM)
ANY = pl.BlockSpec(memory_space=pl.ANY)
GRANT = 32 * 1024 * 1024


def weight_of(step):
    return (step + 1.0) / (step + 2.0)


def tree_sum(parts):
    while len(parts) > 1:
        parts = [parts[i] + parts[i + 1] for i in range(0, len(parts), 2)]
    return parts[0]


def fold(lines):
    return lines.reshape(-1, 8, LANES).sum(axis=0)


def rounded(values):
    return values.astype(jnp.bfloat16).astype(jnp.float32)


def add_products(transpose, in_index, out_index, count, tiles, slots, source, total):
    per_block = tiles.shape[-1] // LANES
    several = len(total.shape) == 3
    live_count = count[0, 0]
    for slot in slots:
        start = in_index[0, 0, slot] * per_block
        place = out_index[0, 0, slot] * per_block
        live = (live_count > slot).astype(jnp.float32)
        halves = []
        for half in range(per_block):
            if not several:
                halves.append(source[pl.ds(start + half, 1), :])
                continue
            vectors = source.shape[0]
            rows = -(-vectors // 8) * 8
            which = lax.broadcasted_iota(jnp.int32, (rows, LANES), 0)
            stacked = jnp.zeros((rows, LANES), jnp.float32)
            for vector in range(vectors):
                line = source[vector, pl.ds(start + half, 1), :]
                stacked = jnp.where(which == vector, line, stacked)
            halves.append(stacked)
        block = (jnp.concatenate(halves, axis=1) * live).astype(jnp.bfloat16)
        contract = ((1,), (0,)) if transpose else ((1,), (1,))
        product = lax.dot_general(
            block, tiles[slot], (contract, ((), ())), preferred_element_type=jnp.float32
        )
        for half in range(per_block):
            at = pl.ds(place + half, 1)
            lanes = slice(half * LANES, (half + 1) * LANES)
            if several:
                for vector in range(total.shape[0]):
                    total[vector, at, :] += product[vector : vector + 1, lanes]
            else:
                total[at, :] += product[:, lanes]


def first_body(
    step, rows, columns, count, tile_data, mask, cotangent, tiles, term, anchor, out, source, arrived
):
    slots = tiles.shape[0]
    chunk = slots // CHUNKS

    def fetch(part):
        span = pl.ds(part * chunk, chunk)
        return pltpu.make_async_copy(tile_data.at[0, 0, span], tiles.at[span], arrived.at[part])

    for part in range(CHUNKS):
        fetch(part).start()
    weight = weight_of(step)
    adjoint = cotangent[...]
    anchor[...] = (1.0 - weight) * adjoint
    value = mask[:, step, :].astype(jnp.float32) * weight * adjoint
    term[...] = value
    source[...] = rounded(value)
    out[...] = jnp.zeros_like(out)
    for part in range(CHUNKS):
        fetch(part).wait()
        span = range(part * chunk, (part + 1) * chunk)
        add_products(True, rows, columns, count, tiles, span, source, out)


def dual_body(step, n_col, rows, columns, count, sizes, tiles, mask, parts, before, anchor, *refs):
    last = step == 0
    if last:
        demand, images, terms, term, anchor_out, out, source = refs
    else:
        term, anchor_out, out, source = refs
    weight = weight_of(step)
    image = tree_sum([part[...] for part in parts])
    adjoint = before[...] + sizes[0] * image
    anchor_out[...] = anchor[...] + (1.0 - weight) * adjoint
    value = mask[:, step, :].astype(jnp.float32) * weight * adjoint
    term[...] = value
    source[...] = rounded(value)
    lines = source.shape[0]
    total = out.at[pl.ds(0, lines)] if last else out
    total[...] = jnp.zeros(total.shape, jnp.float32)
    add_products(True, rows, columns, count, tiles, range(tiles.shape[0]), source, total)
    if last:
        share = demand[...] * (1.0 / n_col)
        found = value * (share - images[0])
        for other, earlier in enumerate(terms):
            found += earlier[...] * (share - images[other + 1])
        out[lines : lines + 8, :] = fold(found)
        out[lines + 8 : lines + 16, :] = jnp.zeros((8, LANES), jnp.float32)


def primal_body(step, n_col, rows, columns, count, sizes, tiles, mask, parts, before, anchor, *refs):
    last = step == 0
    if last:
        place, reduced, terms, final, mine, other, source, out = refs
    else:
        term, adjoint_out, anchor_out, out, source = refs
    sigma = sizes[1]
    weight = weight_of(step)
    lines = source.shape[0]
    back = tree_sum([part[...] for part in parts])
    if last:
        sums = back[lines : lines + 8]
        back = back[:lines]
    adjoint = before[...]
    anchored = (1.0 - weight) * adjoint
    if anchor is not None:
        anchored = anchor[...] + anchored
    value = mask[:, step, :].astype(jnp.float32) * (weight * adjoint - 2.0 * sigma * back)
    after = value + sigma * back
    if last:
        final[...] = after + anchored
    else:
        term[...] = value
        adjoint_out[...] = after
        anchor_out[...] = anchored
    source[...] = rounded(value)
    out[...] = jnp.zeros_like(out)
    add_products(False, columns, rows, count, tiles, range(tiles.shape[0]), source, out)
    if last:
        found = value * reduced[0]
        for other_step, later in enumerate(terms):
            found += later[...] * reduced[other_step + 1]
        tail = jnp.concatenate([sums, -fold(found)], axis=0)
        share = out.shape[0] // n_col
        core = place[0] % 2
        for chip in range(n_col // 2):
            span = slice(chip * share, (chip + 1) * share)
            mine[span, :] = out[pl.ds((2 * chip + core) * share, share), :]
            other[span, :] = out[pl.ds((2 * chip + 1 - core) * share, share), :]
        mine[n_col // 2 * share :, :] = tail
        other[n_col // 2 * share :, :] = tail


def split_body(n_chip, place, mine, received, *outs):
    share = (mine.shape[0] - EXTRA) // n_chip
    chip = place[0] // 2
    tail = mine[n_chip * share :, :] + received[n_chip * share :, :]
    for part, out in enumerate(outs):
        at = pl.ds((chip ^ part) * share, share)
        out[:share, :] = mine[at, :] + received[at, :]
        out[share:, :] = tail


def last_body(scales, place, sizes, parts, term, anchor, adjoint, gradients):
    share = adjoint.shape[0]
    total = tree_sum([part[...] for part in parts])
    at = pl.ds(place[0] * share, share)
    adjoint[...] = term[at, :] + sizes[0] * total[:share] + anchor[at, :]
    gradients[0] = jnp.sum(total[share + 8 : share + 16]) * scales[0]
    gradients[1] = jnp.sum(total[share : share + 8]) * scales[1]


def saved_back_body(rows, columns, count, place, tiles, saved, *refs):
    outs, (source, total) = refs[:-2], refs[-2:]
    for step in range(source.shape[0]):
        source[step] = rounded(saved[:, step, :])
    total[...] = jnp.zeros_like(total)
    add_products(True, rows, columns, count, tiles, range(tiles.shape[0]), source, total)
    share = total.shape[1] // len(outs)
    for part, out in enumerate(outs):
        out[...] = total[:, pl.ds((place[0] ^ part) * share, share), :]


def saved_image_body(
    rows, columns, count, place, sizes, tiles, parts, cost, upper, primal, reduced, images, source
):
    share = parts[0].shape[1]
    for part, held in enumerate(parts):
        at = pl.ds((place[0] ^ part) * share, share)
        reduced[:, at, :] = cost[at, :][None] - held[...]
    for step in range(source.shape[0]):
        saved = primal[:, step, :]
        half = jnp.minimum(jnp.maximum(saved - sizes[0] * reduced[step], 0.0), upper[...])
        source[step] = rounded(2.0 * half - saved)
    images[...] = jnp.zeros_like(images)
    add_products(False, columns, rows, count, tiles, range(tiles.shape[0]), source, images)


def run(body, out_shape, groups, scratch, name, cost=None):
    flat, specs, widths = [], [], []
    for spec, value in groups:
        if value is None:
            widths.append(None)
            continue
        many = isinstance(value, (list, tuple))
        widths.append(len(value) if many else 0)
        for array in value if many else [value]:
            flat.append(array)
            specs.append(spec)

    def kernel(*refs):
        given = list(refs)
        taken = []
        for width in widths:
            if width is None:
                taken.append(None)
            elif width == 0:
                taken.append(given.pop(0))
            else:
                taken.append([given.pop(0) for _ in range(width)])
        body(*taken, *given)

    in_smem = [isinstance(shape, tuple) for shape in out_shape]
    shapes = [shape[1] if isinstance(shape, tuple) else shape for shape in out_shape]
    return pl.pallas_call(
        kernel,
        out_shape=shapes,
        in_specs=specs,
        out_specs=[SMEM if smem else VMEM for smem in in_smem],
        scratch_shapes=scratch,
        compiler_params=pltpu.CompilerParams(vmem_limit_bytes=GRANT),
        cost_estimate=cost,
        name=name,
    )(*flat)


def exchange(parts, axis, stride=1):
    size = lax.axis_size(axis)
    return [parts[0]] + [
        lax.ppermute(parts[k], axis, [(i, i ^ (k * stride)) for i in range(size)])
        for k in range(1, size // stride)
    ]


def local(
    tile_data,
    tile_row_block,
    tile_column_block,
    tile_count,
    saved_primal,
    saved_dual,
    primal_mask,
    dual_mask,
    cost_vector,
    demand,
    upper_bound,
    step_sizes,
    primal_cotangent,
    dual_cotangent,
):
    slots, width = tile_data.shape[2], tile_data.shape[-1]
    iterations, row_length = saved_dual.shape
    column_length = saved_primal.shape[1]
    n_row, n_col = lax.axis_size("row"), lax.axis_size("col")
    n_chip = n_col // 2
    at_row = lax.axis_index("row").reshape(1).astype(jnp.int32)
    at_col = lax.axis_index("col").reshape(1).astype(jnp.int32)
    lines_y, lines_x = row_length // LANES, column_length // LANES
    share_y, share_x = lines_y // n_col, lines_x // n_row
    last = iterations - 1
    cost = pl.CostEstimate(
        flops=2 * tile_data.size, bytes_accessed=2 * tile_data.size, transcendentals=0
    )

    def lines(array):
        if array.ndim == 1:
            return array.reshape(-1, LANES)
        return array.reshape(iterations, -1, LANES).transpose(1, 0, 2)

    def f32(*shape):
        return jax.ShapeDtypeStruct(shape, jnp.float32)

    def scratch(*shape):
        return pltpu.VMEM(shape, jnp.float32)

    mask_x, mask_y = lines(primal_mask), lines(dual_mask)
    full_x, full_y = f32(lines_x, LANES), f32(lines_y, LANES)
    where = [(SMEM, tile_row_block), (SMEM, tile_column_block), (SMEM, tile_count)]

    tiles, term_y, anchor_y, partial = run(
        functools.partial(first_body, last),
        [pltpu.VMEM((slots, width, width), jnp.bfloat16), full_y, full_y, full_x],
        where + [(ANY, tile_data), (VMEM, mask_y), (VMEM, lines(dual_cotangent))],
        [scratch(lines_y, LANES), pltpu.SemaphoreType.DMA((CHUNKS,))],
        "first",
        cost,
    )
    common = where + [(SMEM, step_sizes), (VMEM, tiles)]
    adjoint_x, anchor_x = lines(primal_cotangent), None
    terms_x, terms_y = [], [term_y]
    reduced = images = None
    for step in reversed(range(iterations)):
        parts = exchange([partial] * n_row, "row")
        if reduced is None:
            saved_parts = run(
                saved_back_body,
                [f32(iterations, share_x, LANES)] * n_row,
                where + [(SMEM, at_row), (VMEM, tiles), (VMEM, lines(saved_dual))],
                [scratch(iterations, lines_y, LANES), scratch(iterations, lines_x, LANES)],
                "saved_back",
                cost,
            )
        body = functools.partial(primal_body, step, n_col)
        groups = common + [(VMEM, mask_x), (VMEM, parts), (VMEM, adjoint_x), (VMEM, anchor_x)]
        if step > 0:
            term_x, adjoint_x, anchor_x, partial = run(
                body,
                [full_x, full_x, full_x, full_y],
                groups,
                [scratch(lines_x, LANES)],
                f"primal_{step}",
                cost,
            )
            terms_x.insert(0, term_x)
            partial = sum_pair(partial)
            if reduced is None:
                summed = tree_sum(exchange(saved_parts, "row"))
                gathered = exchange([summed] * n_row, "row")
                reduced, images = run(
                    saved_image_body,
                    [f32(iterations, lines_x, LANES), f32(iterations, lines_y, LANES)],
                    where
                    + [(SMEM, at_row), (SMEM, step_sizes), (VMEM, tiles), (VMEM, gathered)]
                    + [(VMEM, lines(cost_vector)), (VMEM, lines(upper_bound))]
                    + [(VMEM, lines(saved_primal))],
                    [scratch(iterations, lines_x, LANES)],
                    "saved_image",
                    cost,
                )
            parts = exchange([partial] * n_chip, "col", 2)
            final_step = step == 1
            groups = common + [(VMEM, mask_y), (VMEM, parts), (VMEM, term_y), (VMEM, anchor_y)]
            if final_step:
                groups += [(VMEM, lines(demand)), (VMEM, images), (VMEM, list(terms_y))]
            term_y, anchor_y, partial = run(
                functools.partial(dual_body, step - 1, n_col),
                [full_y, full_y, f32(lines_x + (EXTRA if final_step else 0), LANES)],
                groups,
                [scratch(lines_y, LANES)],
                f"dual_{step - 1}",
                cost,
            )
            terms_y.insert(0, term_y)
    half_y = f32(n_chip * share_y + EXTRA, LANES)
    primal_adjoint, mine, other = run(
        body,
        [full_x, half_y, half_y],
        groups + [(SMEM, at_col), (VMEM, reduced), (VMEM, terms_x)],
        [scratch(lines_x, LANES), scratch(lines_y, LANES)],
        "primal_0",
        cost,
    )
    received = lax.ppermute(other, "col", [(i, i ^ 1) for i in range(n_col)])
    parts = run(
        functools.partial(split_body, n_chip),
        [f32(share_y + EXTRA, LANES)] * n_chip,
        [(SMEM, at_col), (VMEM, mine), (VMEM, received)],
        [],
        "split",
    )
    parts = exchange(parts, "col", 2)
    scales = (1.0 / math.sqrt(column_length * n_col), 1.0 / math.sqrt(row_length * n_row))
    dual_adjoint, gradients = run(
        functools.partial(last_body, scales),
        [f32(share_y, LANES), ("smem", f32(2))],
        [(SMEM, at_col), (SMEM, step_sizes), (VMEM, parts), (VMEM, term_y), (VMEM, anchor_y)],
        [],
        "last",
    )
    return (primal_adjoint.reshape(-1), dual_adjoint.reshape(-1), gradients)


def sum_pair(partial):
    size = lax.axis_size("col")
    return partial + lax.ppermute(partial, "col", [(i, i ^ 1) for i in range(size)])


def solution(mesh):
    placed = (
        P("row", "col", None, None, None),
        P("row", "col", None),
        P("row", "col", None),
        P("row", "col"),
        P(None, "col"),
        P(None, "row"),
        P(None, "col"),
        P(None, "row"),
        P("col"),
        P("row"),
        P("col"),
        P(),
        P("col"),
        P("row"),
    )
    return jax.shard_map(
        local,
        mesh=mesh,
        in_specs=placed,
        out_specs=(P("col"), P(("row", "col")), P()),
        check_vma=False,
    )
```

```python
import functools
import math

import jax
import jax.numpy as jnp
from jax import lax
from jax.experimental import pallas as pl
from jax.experimental.pallas import tpu as pltpu
from jax.sharding import PartitionSpec as P

LANES = 128
EXTRA = 16
CHUNKS = 4
VMEM = pl.BlockSpec(memory_space=pltpu.VMEM)
SMEM = pl.BlockSpec(memory_space=pltpu.SMEM)
ANY = pl.BlockSpec(memory_space=pl.ANY)
GRANT = 32 * 1024 * 1024


def weight_of(step):
    return (step + 1.0) / (step + 2.0)


def tree_sum(parts):
    while len(parts) > 1:
        parts = [parts[i] + parts[i + 1] for i in range(0, len(parts), 2)]
    return parts[0]


def fold(lines):
    return lines.reshape(-1, 8, LANES).sum(axis=0)


def rounded(values):
    return values.astype(jnp.bfloat16).astype(jnp.float32)


def add_products(transpose, in_index, out_index, count, tiles, slots, source, total):
    per_block = tiles.shape[-1] // LANES
    several = len(total.shape) == 3
    live_count = count[0, 0]
    for slot in slots:
        start = in_index[0, 0, slot] * per_block
        place = out_index[0, 0, slot] * per_block
        live = (live_count > slot).astype(jnp.float32)
        halves = []
        for half in range(per_block):
            if not several:
                halves.append(source[pl.ds(start + half, 1), :])
                continue
            vectors = source.shape[0]
            rows = -(-vectors // 8) * 8
            which = lax.broadcasted_iota(jnp.int32, (rows, LANES), 0)
            stacked = jnp.zeros((rows, LANES), jnp.float32)
            for vector in range(vectors):
                line = source[vector, pl.ds(start + half, 1), :]
                stacked = jnp.where(which == vector, line, stacked)
            halves.append(stacked)
        block = (jnp.concatenate(halves, axis=1) * live).astype(jnp.bfloat16)
        contract = ((1,), (0,)) if transpose else ((1,), (1,))
        product = lax.dot_general(
            block, tiles[slot], (contract, ((), ())), preferred_element_type=jnp.float32
        )
        for half in range(per_block):
            at = pl.ds(place + half, 1)
            lanes = slice(half * LANES, (half + 1) * LANES)
            if several:
                for vector in range(total.shape[0]):
                    total[vector, at, :] += product[vector : vector + 1, lanes]
            else:
                total[at, :] += product[:, lanes]


def first_body(
    step, rows_far, columns_far, count, tile_data, mask_far, cotangent_far,
    tiles, term, anchor, out, source, rows, columns, mask, cotangent, arrived, ready,
):
    slots = tiles.shape[0]
    chunk = slots // CHUNKS
    small = [
        pltpu.make_async_copy(far, near, ready.at[spot])
        for spot, (far, near) in enumerate(
            [(mask_far, mask), (cotangent_far, cotangent), (rows_far, rows), (columns_far, columns)]
        )
    ]
    for copy in small:
        copy.start()

    def fetch(part):
        span = pl.ds(part * chunk, chunk)
        return pltpu.make_async_copy(tile_data.at[0, 0, span], tiles.at[span], arrived.at[part])

    for part in range(CHUNKS):
        fetch(part).start()
    out[...] = jnp.zeros_like(out)
    for copy in small:
        copy.wait()
    weight = weight_of(step)
    adjoint = cotangent[...]
    anchor[...] = (1.0 - weight) * adjoint
    value = mask[:, step, :].astype(jnp.float32) * weight * adjoint
    term[...] = value
    source[...] = rounded(value)
    for part in range(CHUNKS):
        fetch(part).wait()
        span = range(part * chunk, (part + 1) * chunk)
        add_products(True, rows, columns, count, tiles, span, source, out)


def dual_body(step, n_col, rows, columns, count, sizes, tiles, mask, parts, before, anchor, *refs):
    last = step == 0
    if last:
        demand, images, terms, term, anchor_out, out, source = refs
    else:
        term, anchor_out, out, source = refs
    weight = weight_of(step)
    image = tree_sum([part[...] for part in parts])
    adjoint = before[...] + sizes[0] * image
    anchor_out[...] = anchor[...] + (1.0 - weight) * adjoint
    value = mask[:, step, :].astype(jnp.float32) * weight * adjoint
    term[...] = value
    source[...] = rounded(value)
    lines = source.shape[0]
    total = out.at[pl.ds(0, lines)] if last else out
    total[...] = jnp.zeros(total.shape, jnp.float32)
    add_products(True, rows, columns, count, tiles, range(tiles.shape[0]), source, total)
    if last:
        share = demand[...] * (1.0 / n_col)
        found = value * (share - images[0])
        for other, earlier in enumerate(terms):
            found += earlier[...] * (share - images[other + 1])
        out[lines : lines + 8, :] = fold(found)
        out[lines + 8 : lines + 16, :] = jnp.zeros((8, LANES), jnp.float32)


def primal_body(step, n_col, rows, columns, count, sizes, tiles, mask, parts, before, anchor, *refs):
    last = step == 0
    if last:
        place, reduced, terms, final, mine, other, source, out = refs
    else:
        term, adjoint_out, anchor_out, out, source = refs
    sigma = sizes[1]
    weight = weight_of(step)
    lines = source.shape[0]
    back = tree_sum([part[...] for part in parts])
    if last:
        sums = back[lines : lines + 8]
        back = back[:lines]
    adjoint = before[...]
    anchored = (1.0 - weight) * adjoint
    if anchor is not None:
        anchored = anchor[...] + anchored
    value = mask[:, step, :].astype(jnp.float32) * (weight * adjoint - 2.0 * sigma * back)
    after = value + sigma * back
    if last:
        final[...] = after + anchored
    else:
        term[...] = value
        adjoint_out[...] = after
        anchor_out[...] = anchored
    source[...] = rounded(value)
    out[...] = jnp.zeros_like(out)
    add_products(False, columns, rows, count, tiles, range(tiles.shape[0]), source, out)
    if last:
        found = value * reduced[0]
        for other_step, later in enumerate(terms):
            found += later[...] * reduced[other_step + 1]
        tail = jnp.concatenate([sums, -fold(found)], axis=0)
        share = out.shape[0] // n_col
        core = place[0] % 2
        for chip in range(n_col // 2):
            span = slice(chip * share, (chip + 1) * share)
            mine[span, :] = out[pl.ds((2 * chip + core) * share, share), :]
            other[span, :] = out[pl.ds((2 * chip + 1 - core) * share, share), :]
        mine[n_col // 2 * share :, :] = tail
        other[n_col // 2 * share :, :] = tail


def split_body(n_chip, place, mine, received, *outs):
    share = (mine.shape[0] - EXTRA) // n_chip
    chip = place[0] // 2
    tail = mine[n_chip * share :, :] + received[n_chip * share :, :]
    for part, out in enumerate(outs):
        at = pl.ds((chip ^ part) * share, share)
        out[:share, :] = mine[at, :] + received[at, :]
        out[share:, :] = tail


def last_body(scales, place, sizes, parts, term, anchor, adjoint, gradients):
    share = adjoint.shape[0]
    total = tree_sum([part[...] for part in parts])
    at = pl.ds(place[0] * share, share)
    adjoint[...] = term[at, :] + sizes[0] * total[:share] + anchor[at, :]
    gradients[0] = jnp.sum(total[share + 8 : share + 16]) * scales[0]
    gradients[1] = jnp.sum(total[share : share + 8]) * scales[1]


def saved_back_body(rows, columns, count, place, tiles, saved, *refs):
    outs, (source, total) = refs[:-2], refs[-2:]
    for step in range(source.shape[0]):
        source[step] = rounded(saved[:, step, :])
    total[...] = jnp.zeros_like(total)
    add_products(True, rows, columns, count, tiles, range(tiles.shape[0]), source, total)
    share = total.shape[1] // len(outs)
    for part, out in enumerate(outs):
        out[...] = total[:, pl.ds((place[0] ^ part) * share, share), :]


def saved_image_body(
    rows, columns, count, place, sizes, tiles, parts, cost, upper, primal, reduced, images, source
):
    share = parts[0].shape[1]
    for part, held in enumerate(parts):
        at = pl.ds((place[0] ^ part) * share, share)
        reduced[:, at, :] = cost[at, :][None] - held[...]
    for step in range(source.shape[0]):
        saved = primal[:, step, :]
        half = jnp.minimum(jnp.maximum(saved - sizes[0] * reduced[step], 0.0), upper[...])
        source[step] = rounded(2.0 * half - saved)
    images[...] = jnp.zeros_like(images)
    add_products(False, columns, rows, count, tiles, range(tiles.shape[0]), source, images)


def far(array):
    return pltpu.with_memory_space_constraint(array, pltpu.HBM)


def run(body, out_shape, groups, scratch, name, cost=None):
    flat, specs, widths = [], [], []
    for spec, value in groups:
        if value is None:
            widths.append(None)
            continue
        many = isinstance(value, (list, tuple))
        widths.append(len(value) if many else 0)
        for array in value if many else [value]:
            flat.append(array)
            specs.append(spec)

    def kernel(*refs):
        given = list(refs)
        taken = []
        for width in widths:
            if width is None:
                taken.append(None)
            elif width == 0:
                taken.append(given.pop(0))
            else:
                taken.append([given.pop(0) for _ in range(width)])
        body(*taken, *given)

    in_smem = [isinstance(shape, tuple) for shape in out_shape]
    shapes = [shape[1] if isinstance(shape, tuple) else shape for shape in out_shape]
    return pl.pallas_call(
        kernel,
        out_shape=shapes,
        in_specs=specs,
        out_specs=[SMEM if smem else VMEM for smem in in_smem],
        scratch_shapes=scratch,
        compiler_params=pltpu.CompilerParams(vmem_limit_bytes=GRANT),
        cost_estimate=cost,
        name=name,
    )(*flat)


def exchange(parts, axis, stride=1):
    size = lax.axis_size(axis)
    return [parts[0]] + [
        lax.ppermute(parts[k], axis, [(i, i ^ (k * stride)) for i in range(size)])
        for k in range(1, size // stride)
    ]


def local(
    tile_data,
    tile_row_block,
    tile_column_block,
    tile_count,
    saved_primal,
    saved_dual,
    primal_mask,
    dual_mask,
    cost_vector,
    demand,
    upper_bound,
    step_sizes,
    primal_cotangent,
    dual_cotangent,
):
    slots, width = tile_data.shape[2], tile_data.shape[-1]
    iterations, row_length = saved_dual.shape
    column_length = saved_primal.shape[1]
    n_row, n_col = lax.axis_size("row"), lax.axis_size("col")
    n_chip = n_col // 2
    at_row = lax.axis_index("row").reshape(1).astype(jnp.int32)
    at_col = lax.axis_index("col").reshape(1).astype(jnp.int32)
    lines_y, lines_x = row_length // LANES, column_length // LANES
    share_y, share_x = lines_y // n_col, lines_x // n_row
    last = iterations - 1
    cost = pl.CostEstimate(
        flops=2 * tile_data.size, bytes_accessed=2 * tile_data.size, transcendentals=0
    )

    def lines(array):
        if array.ndim == 1:
            return array.reshape(-1, LANES)
        return array.reshape(iterations, -1, LANES).transpose(1, 0, 2)

    def f32(*shape):
        return jax.ShapeDtypeStruct(shape, jnp.float32)

    def scratch(*shape):
        return pltpu.VMEM(shape, jnp.float32)

    mask_x, mask_y = lines(primal_mask), lines(dual_mask)
    full_x, full_y = f32(lines_x, LANES), f32(lines_y, LANES)
    where = [(SMEM, tile_row_block), (SMEM, tile_column_block), (SMEM, tile_count)]

    tiles, term_y, anchor_y, partial = run(
        functools.partial(first_body, last),
        [pltpu.VMEM((slots, width, width), jnp.bfloat16), full_y, full_y, full_x],
        [(ANY, far(tile_row_block)), (ANY, far(tile_column_block)), (SMEM, tile_count)]
        + [(ANY, far(tile_data)), (ANY, far(mask_y)), (ANY, far(lines(dual_cotangent)))],
        [
            scratch(lines_y, LANES),
            pltpu.SMEM(tile_row_block.shape, jnp.int32),
            pltpu.SMEM(tile_row_block.shape, jnp.int32),
            pltpu.VMEM(mask_y.shape, jnp.int32),
            scratch(lines_y, LANES),
            pltpu.SemaphoreType.DMA((CHUNKS,)),
            pltpu.SemaphoreType.DMA((4,)),
        ],
        "first",
        cost,
    )
    tiles = pltpu.with_memory_space_constraint(tiles, pltpu.VMEM)
    common = where + [(SMEM, step_sizes), (VMEM, tiles)]
    adjoint_x, anchor_x = lines(primal_cotangent), None
    terms_x, terms_y = [], [term_y]
    reduced = images = None
    for step in reversed(range(iterations)):
        parts = exchange([partial] * n_row, "row")
        if reduced is None:
            saved_parts = run(
                saved_back_body,
                [f32(iterations, share_x, LANES)] * n_row,
                where + [(SMEM, at_row), (VMEM, tiles), (VMEM, lines(saved_dual))],
                [scratch(iterations, lines_y, LANES), scratch(iterations, lines_x, LANES)],
                "saved_back",
                cost,
            )
        body = functools.partial(primal_body, step, n_col)
        groups = common + [(VMEM, mask_x), (VMEM, parts), (VMEM, adjoint_x), (VMEM, anchor_x)]
        if step > 0:
            term_x, adjoint_x, anchor_x, partial = run(
                body,
                [full_x, full_x, full_x, full_y],
                groups,
                [scratch(lines_x, LANES)],
                f"primal_{step}",
                cost,
            )
            terms_x.insert(0, term_x)
            partial = sum_pair(partial)
            if reduced is None:
                summed = tree_sum(exchange(saved_parts, "row"))
                gathered = exchange([summed] * n_row, "row")
                reduced, images = run(
                    saved_image_body,
                    [f32(iterations, lines_x, LANES), f32(iterations, lines_y, LANES)],
                    where
                    + [(SMEM, at_row), (SMEM, step_sizes), (VMEM, tiles), (VMEM, gathered)]
                    + [(VMEM, lines(cost_vector)), (VMEM, lines(upper_bound))]
                    + [(VMEM, lines(saved_primal))],
                    [scratch(iterations, lines_x, LANES)],
                    "saved_image",
                    cost,
                )
            parts = exchange([partial] * n_chip, "col", 2)
            final_step = step == 1
            groups = common + [(VMEM, mask_y), (VMEM, parts), (VMEM, term_y), (VMEM, anchor_y)]
            if final_step:
                groups += [(VMEM, lines(demand)), (VMEM, images), (VMEM, list(terms_y))]
            term_y, anchor_y, partial = run(
                functools.partial(dual_body, step - 1, n_col),
                [full_y, full_y, f32(lines_x + (EXTRA if final_step else 0), LANES)],
                groups,
                [scratch(lines_y, LANES)],
                f"dual_{step - 1}",
                cost,
            )
            terms_y.insert(0, term_y)
    half_y = f32(n_chip * share_y + EXTRA, LANES)
    primal_adjoint, mine, other = run(
        body,
        [full_x, half_y, half_y],
        groups + [(SMEM, at_col), (VMEM, reduced), (VMEM, terms_x)],
        [scratch(lines_x, LANES), scratch(lines_y, LANES)],
        "primal_0",
        cost,
    )
    received = lax.ppermute(other, "col", [(i, i ^ 1) for i in range(n_col)])
    parts = run(
        functools.partial(split_body, n_chip),
        [f32(share_y + EXTRA, LANES)] * n_chip,
        [(SMEM, at_col), (VMEM, mine), (VMEM, received)],
        [],
        "split",
    )
    parts = exchange(parts, "col", 2)
    scales = (1.0 / math.sqrt(column_length * n_col), 1.0 / math.sqrt(row_length * n_row))
    dual_adjoint, gradients = run(
        functools.partial(last_body, scales),
        [f32(share_y, LANES), ("smem", f32(2))],
        [(SMEM, at_col), (SMEM, step_sizes), (VMEM, parts), (VMEM, term_y), (VMEM, anchor_y)],
        [],
        "last",
    )
    return (primal_adjoint.reshape(-1), dual_adjoint.reshape(-1), gradients)


def sum_pair(partial):
    size = lax.axis_size("col")
    return partial + lax.ppermute(partial, "col", [(i, i ^ 1) for i in range(size)])


def solution(mesh):
    placed = (
        P("row", "col", None, None, None),
        P("row", "col", None),
        P("row", "col", None),
        P("row", "col"),
        P(None, "col"),
        P(None, "row"),
        P(None, "col"),
        P(None, "row"),
        P("col"),
        P("row"),
        P("col"),
        P(),
        P("col"),
        P("row"),
    )
    return jax.shard_map(
        local,
        mesh=mesh,
        in_specs=placed,
        out_specs=(P("col"), P(("row", "col")), P()),
        check_vma=False,
    )
```

```python
import functools
import math

import jax
import jax.numpy as jnp
from jax import lax
from jax.experimental import pallas as pl
from jax.experimental.pallas import tpu as pltpu
from jax.sharding import PartitionSpec as P

LANES = 128
EXTRA = 16
CHUNKS = 4
SCALES = 16
STEPS = 64.0
LIMIT = 32760.0
FINE = 65000.0
LN2 = math.log(2.0)
VMEM = pl.BlockSpec(memory_space=pltpu.VMEM)
SMEM = pl.BlockSpec(memory_space=pltpu.SMEM)
ANY = pl.BlockSpec(memory_space=pl.ANY)
GRANT = 16 * 1024 * 1024


def weight_of(step):
    return (step + 1.0) / (step + 2.0)


def tree_sum(parts):
    while len(parts) > 1:
        parts = [parts[i] + parts[i + 1] for i in range(0, len(parts), 2)]
    return parts[0]


def fold(lines):
    return lines.reshape(-1, 8, LANES).sum(axis=0)


def rounded(values):
    return values.astype(jnp.bfloat16).astype(jnp.float32)


def add_products(transpose, in_index, out_index, count, tiles, slots, source, total):
    per_block = tiles.shape[-1] // LANES
    several = len(total.shape) == 3
    live_count = count[0, 0]
    for slot in slots:
        start = in_index[0, 0, slot] * per_block
        place = out_index[0, 0, slot] * per_block
        live = (live_count > slot).astype(jnp.float32)
        halves = []
        for half in range(per_block):
            if not several:
                halves.append(source[pl.ds(start + half, 1), :])
                continue
            vectors = source.shape[0]
            rows = -(-vectors // 8) * 8
            which = lax.broadcasted_iota(jnp.int32, (rows, LANES), 0)
            stacked = jnp.zeros((rows, LANES), jnp.float32)
            for vector in range(vectors):
                line = source[vector, pl.ds(start + half, 1), :]
                stacked = jnp.where(which == vector, line, stacked)
            halves.append(stacked)
        block = (jnp.concatenate(halves, axis=1) * live).astype(jnp.bfloat16)
        contract = ((1,), (0,)) if transpose else ((1,), (1,))
        product = lax.dot_general(
            block, tiles[slot], (contract, ((), ())), preferred_element_type=jnp.float32
        )
        for half in range(per_block):
            at = pl.ds(place + half, 1)
            lanes = slice(half * LANES, (half + 1) * LANES)
            if several:
                for vector in range(total.shape[0]):
                    total[vector, at, :] += product[vector : vector + 1, lanes]
            else:
                total[at, :] += product[:, lanes]


def whole_scale(lines):
    largest = jnp.maximum(jnp.max(jnp.abs(lines), axis=0, keepdims=True), 1e-30)
    return jnp.floor(jnp.log(largest) * (STEPS / LN2) + 1.0)


def to_units(code):
    return jnp.exp(code * (-LN2 / STEPS)) * LIMIT


def from_units(code):
    return jnp.exp(code * (LN2 / STEPS)) * (1.0 / LIMIT)


def nearest(values):
    return jnp.floor(values + 0.5)


def short(values):
    return values.astype(jnp.int32).astype(jnp.int16)


def long(values):
    return values.astype(jnp.int32).astype(jnp.float32)


def encode(lines):
    code = whole_scale(lines)
    return nearest(lines * to_units(code)), code


def encode_fine(lines):
    code = whole_scale(lines)
    units = lines * to_units(code)
    coarse = nearest(units)
    return coarse, nearest((units - coarse) * FINE), code


def scale_rows(codes):
    which = lax.broadcasted_iota(jnp.int32, (SCALES, LANES), 0)
    rows = jnp.zeros((SCALES, LANES), jnp.float32)
    for spot, code in enumerate(codes):
        rows = jnp.where(which == spot, code, rows)
    return short(rows)


def scales_of(part):
    codes = long(part[part.shape[0] - SCALES :, :])
    return [from_units(codes[spot : spot + 1]) for spot in range(2)]


def first_body(
    step, n_row, rows_far, columns_far, count, tile_data, mask_far, cotangent_far, saved_far,
    tiles, term, anchor, *refs
):
    outs = refs[:n_row]
    source, total, rows, columns, mask, cotangent, saved, arrived, ready = refs[n_row:]
    slots = tiles.shape[0]
    chunk = slots // CHUNKS
    pairs = [(mask_far, mask), (cotangent_far, cotangent), (saved_far, saved)]
    pairs += [(rows_far, rows), (columns_far, columns)]
    small = [
        pltpu.make_async_copy(far_ref, near, ready.at[spot])
        for spot, (far_ref, near) in enumerate(pairs)
    ]
    for copy in small:
        copy.start()

    def fetch(part):
        span = pl.ds(part * chunk, chunk)
        return pltpu.make_async_copy(tile_data.at[0, 0, span], tiles.at[span], arrived.at[part])

    for part in range(CHUNKS):
        fetch(part).start()
    total[...] = jnp.zeros_like(total)
    for copy in small:
        copy.wait()
    weight = weight_of(step)
    adjoint = cotangent[...]
    anchor[...] = (1.0 - weight) * adjoint
    value = mask[:, step, :].astype(jnp.float32) * weight * adjoint
    term[...] = value
    source[0] = rounded(value)
    iterations = source.shape[0] - 1
    for vector in range(iterations):
        source[vector + 1] = rounded(saved[:, vector, :])
    for part in range(CHUNKS):
        fetch(part).wait()
        span = range(part * chunk, (part + 1) * chunk)
        add_products(True, rows, columns, count, tiles, span, source, total)
    lines = total.shape[1]
    share = lines // n_row
    me = lax.axis_index("row")
    units, code = encode(total[0])
    units = short(units)
    for part, out in enumerate(outs):
        at = pl.ds(pl.multiple_of((me ^ part) * share, share), share)
        out[:lines, :] = units
        saved_units, saved_code = encode(total[1:, at, :].reshape(iterations * share, LANES))
        out[lines : lines + iterations * share, :] = short(saved_units)
        out[lines + iterations * share :, :] = scale_rows([code, saved_code])


def dual_body(step, n_col, rows, columns, count, sizes, tiles, mask, parts, before, anchor, *refs):
    last = step == 0
    if last:
        demand, images, terms, term, anchor_out, out, _, source, total = refs
    else:
        saved, term, anchor_out, out, _, source, total = refs
    weight = weight_of(step)
    image = tree_sum([part[...] for part in parts])
    adjoint = before[...] + sizes[0] * image
    anchor_out[...] = anchor[...] + (1.0 - weight) * adjoint
    value = mask[:, step, :].astype(jnp.float32) * weight * adjoint
    term[...] = value
    source[...] = rounded(value)
    total[...] = jnp.zeros_like(total)
    add_products(True, rows, columns, count, tiles, range(tiles.shape[0]), source, total)
    lines = total.shape[0]
    units, code = encode(total[...])
    out[:lines, :] = short(units)
    if last:
        share = demand[...] * (1.0 / n_col)
        found = value * (share - images[0])
        for other, earlier in enumerate(terms):
            found += earlier[...] * (share - images[other + 1])
        coarse, fine, found_code = encode_fine(fold(found))
        out[lines : lines + EXTRA, :] = short(jnp.concatenate([coarse, fine], axis=0))
        out[lines + EXTRA :, :] = scale_rows([code, found_code])
    elif saved is None:
        out[lines:, :] = scale_rows([code])
    else:
        size = saved.shape[0]
        coarse, fine, saved_code = encode_fine(saved[...])
        out[lines : lines + size, :] = short(coarse)
        out[lines + size : lines + 2 * size, :] = short(fine)
        out[lines + 2 * size :, :] = scale_rows([code, saved_code])


def primal_body(kind, step, n_row, n_col, rows, columns, count, sizes, tiles, mask, parts, before, anchor, *refs):
    last = kind == "last"
    if last:
        reduced, terms, final, mine, other, _, source, out = refs
    elif kind == "sums":
        term, adjoint_out, anchor_out, out, saved, _, source = refs
    elif kind == "shares":
        cost, upper, primal, term, adjoint_out, anchor_out, out, reduced, images, _, source, total = refs
    else:
        term, adjoint_out, anchor_out, out, _, source = refs
    sigma = sizes[1]
    weight = weight_of(step)
    lines = mask.shape[0]
    scales = [scales_of(part) for part in parts]
    back = tree_sum([long(part[:lines, :]) * scale[0] for part, scale in zip(parts, scales)])
    adjoint = before[...]
    anchored = (1.0 - weight) * adjoint
    if anchor is not None:
        anchored = anchor[...] + anchored
    value = mask[:, step, :].astype(jnp.float32) * (weight * adjoint - 2.0 * sigma * back)
    after = value + sigma * back
    if last:
        final[...] = after + anchored
    else:
        term[...] = value
        adjoint_out[...] = after
        anchor_out[...] = anchored
    all_slots = range(tiles.shape[0])
    if kind == "shares":
        iterations = reduced.shape[0]
        share = lines // n_row
        size = iterations * share
        me = lax.axis_index("row")
        for part, (held, scale) in enumerate(zip(parts, scales)):
            at = pl.ds(pl.multiple_of((me ^ part) * share, share), share)
            units = long(held[lines : lines + size, :])
            units += long(held[lines + size : lines + 2 * size, :]) * (1.0 / FINE)
            sums = (units * scale[1]).reshape(iterations, share, LANES)
            reduced[:, at, :] = cost[at, :][None] - sums
        source[0] = rounded(value)
        for vector in range(iterations):
            saved = primal[:, vector, :]
            half = jnp.minimum(jnp.maximum(saved - sizes[0] * reduced[vector], 0.0), upper[...])
            source[vector + 1] = rounded(2.0 * half - saved)
        total[...] = jnp.zeros_like(total)
        add_products(False, columns, rows, count, tiles, all_slots, source, total)
        out[...] = total[0]
        images[...] = total[1:]
        return
    source[...] = rounded(value)
    out[...] = jnp.zeros_like(out)
    add_products(False, columns, rows, count, tiles, all_slots, source, out)
    if kind == "sums":
        size = saved.shape[0]
        saved[...] = tree_sum(
            [long(part[lines : lines + size, :]) * scale[1] for part, scale in zip(parts, scales)]
        )
    if last:
        sums = 0.0
        for part, scale in zip(parts, scales):
            units = long(part[lines : lines + EXTRA, :])
            sums += (units[:8] + units[8:] * (1.0 / FINE)) * scale[1]
        found = value * reduced[0]
        for other_step, later in enumerate(terms):
            found += later[...] * reduced[other_step + 1]
        tail = jnp.concatenate([sums, -fold(found)], axis=0)
        share = out.shape[0] // n_col
        core = lax.axis_index("col") % 2
        for chip in range(n_col // 2):
            span = slice(chip * share, (chip + 1) * share)
            mine[span, :] = out[pl.ds((2 * chip + core) * share, share), :]
            other[span, :] = out[pl.ds((2 * chip + 1 - core) * share, share), :]
        mine[n_col // 2 * share :, :] = tail
        other[n_col // 2 * share :, :] = tail


def split_body(n_chip, mine, received, *outs):
    share = (mine.shape[0] - EXTRA) // n_chip
    chip = lax.axis_index("col") // 2
    tail = mine[n_chip * share :, :] + received[n_chip * share :, :]
    for part, out in enumerate(outs):
        at = pl.ds((chip ^ part) * share, share)
        out[:share, :] = mine[at, :] + received[at, :]
        out[share:, :] = tail


def last_body(scales, sizes, parts, term, anchor, adjoint, gradients):
    share = adjoint.shape[0]
    total = tree_sum([part[...] for part in parts])
    at = pl.ds(lax.axis_index("col") * share, share)
    adjoint[...] = term[at, :] + sizes[0] * total[:share] + anchor[at, :]
    gradients[0] = jnp.sum(total[share + 8 : share + 16]) * scales[0]
    gradients[1] = jnp.sum(total[share : share + 8]) * scales[1]


def far(array):
    return pltpu.with_memory_space_constraint(array, pltpu.HBM)


def run(body, out_shape, groups, scratch, name, cost=None, tiles=None):
    flat, specs, widths, aliases = [], [], [], {}
    for spec, value in groups:
        if value is None:
            widths.append(None)
            continue
        many = isinstance(value, (list, tuple))
        widths.append(len(value) if many else 0)
        for array in value if many else [value]:
            if array is tiles:
                aliases[len(flat)] = len(out_shape)
                array = pltpu.with_memory_space_constraint(array, pltpu.VMEM)
            flat.append(array)
            specs.append(spec)

    def kernel(*refs):
        given = list(refs)
        taken = []
        for width in widths:
            if width is None:
                taken.append(None)
            elif width == 0:
                taken.append(given.pop(0))
            else:
                taken.append([given.pop(0) for _ in range(width)])
        body(*taken, *given)

    in_smem = [isinstance(shape, tuple) for shape in out_shape]
    shapes = [shape[1] if isinstance(shape, tuple) else shape for shape in out_shape]
    if tiles is not None:
        shapes.append(pltpu.VMEM(tiles.shape, tiles.dtype))
        in_smem.append(False)
    return pl.pallas_call(
        kernel,
        out_shape=shapes,
        in_specs=specs,
        out_specs=[SMEM if smem else VMEM for smem in in_smem],
        scratch_shapes=scratch,
        input_output_aliases=aliases,
        compiler_params=pltpu.CompilerParams(vmem_limit_bytes=GRANT),
        cost_estimate=cost,
        name=name,
    )(*flat)


def exchange(parts, axis, stride=1):
    size = lax.axis_size(axis)
    return [parts[0]] + [
        lax.ppermute(parts[k], axis, [(i, i ^ (k * stride)) for i in range(size)])
        for k in range(1, size // stride)
    ]


def local(
    tile_data,
    tile_row_block,
    tile_column_block,
    tile_count,
    saved_primal,
    saved_dual,
    primal_mask,
    dual_mask,
    cost_vector,
    demand,
    upper_bound,
    step_sizes,
    primal_cotangent,
    dual_cotangent,
):
    slots, width = tile_data.shape[2], tile_data.shape[-1]
    iterations, row_length = saved_dual.shape
    column_length = saved_primal.shape[1]
    n_row, n_col = lax.axis_size("row"), lax.axis_size("col")
    n_chip = n_col // 2
    lines_y, lines_x = row_length // LANES, column_length // LANES
    share_y, share_x = lines_y // n_col, lines_x // n_row
    saved_lines = iterations * share_x
    last = iterations - 1
    cost = pl.CostEstimate(
        flops=2 * tile_data.size, bytes_accessed=2 * tile_data.size, transcendentals=0
    )

    def lines(array):
        if array.ndim == 1:
            return array.reshape(-1, LANES)
        return array.reshape(iterations, -1, LANES).transpose(1, 0, 2)

    def f32(*shape):
        return jax.ShapeDtypeStruct(shape, jnp.float32)

    def row_part(more):
        return jax.ShapeDtypeStruct((lines_x + more + SCALES, LANES), jnp.int16)

    def scratch(*shape):
        return pltpu.VMEM(shape, jnp.float32)

    mask_x, mask_y = lines(primal_mask), lines(dual_mask)
    full_x, full_y = f32(lines_x, LANES), f32(lines_y, LANES)
    where = [(SMEM, tile_row_block), (SMEM, tile_column_block), (SMEM, tile_count)]
    saved = lines(saved_dual)
    tiles, term_y, anchor_y, *parts = run(
        functools.partial(first_body, last, n_row),
        [pltpu.VMEM((slots, width, width), jnp.bfloat16), full_y, full_y]
        + [row_part(saved_lines)] * n_row,
        [(ANY, far(tile_row_block)), (ANY, far(tile_column_block)), (SMEM, tile_count)]
        + [(ANY, far(tile_data)), (ANY, far(mask_y)), (ANY, far(lines(dual_cotangent)))]
        + [(ANY, far(saved))],
        [
            scratch(iterations + 1, lines_y, LANES),
            scratch(iterations + 1, lines_x, LANES),
            pltpu.SMEM(tile_row_block.shape, jnp.int32),
            pltpu.SMEM(tile_row_block.shape, jnp.int32),
            pltpu.VMEM(mask_y.shape, jnp.int32),
            scratch(lines_y, LANES),
            scratch(*saved.shape),
            pltpu.SemaphoreType.DMA((CHUNKS,)),
            pltpu.SemaphoreType.DMA((5,)),
        ],
        "first",
        cost,
    )
    adjoint_x, anchor_x = lines(primal_cotangent), None
    terms_x, terms_y = [], [term_y]
    reduced = images = saved_sums = None
    for step in reversed(range(iterations)):
        parts = exchange(parts, "row")
        kind = {0: "last", last: "sums", last - 1: "shares"}.get(step, "plain")
        groups = where + [(SMEM, step_sizes), (VMEM, tiles), (VMEM, mask_x), (VMEM, parts)]
        groups += [(VMEM, adjoint_x), (VMEM, anchor_x)]
        body = functools.partial(primal_body, kind, step, n_row, n_col)
        if step == 0:
            break
        outs = [full_x, full_x, full_x, full_y]
        extra = [scratch(lines_x, LANES)]
        if kind == "sums":
            outs.append(f32(saved_lines, LANES))
        if kind == "shares":
            outs += [f32(iterations, lines_x, LANES), f32(iterations, lines_y, LANES)]
            groups += [(VMEM, lines(cost_vector)), (VMEM, lines(upper_bound))]
            groups += [(VMEM, lines(saved_primal))]
            extra = [
                scratch(iterations + 1, lines_x, LANES),
                scratch(iterations + 1, lines_y, LANES),
            ]
        term_x, adjoint_x, anchor_x, partial, *more, tiles = run(
            body, outs, groups, extra, f"primal_{step}", cost, tiles
        )
        if kind == "sums":
            (saved_sums,) = more
        elif kind == "shares":
            reduced, images = more
            saved_sums = None
        terms_x.insert(0, term_x)
        partial = sum_pair(partial)
        parts = exchange([partial] * n_chip, "col", 2)
        groups = where + [(SMEM, step_sizes), (VMEM, tiles), (VMEM, mask_y), (VMEM, parts)]
        groups += [(VMEM, term_y), (VMEM, anchor_y)]
        if step == 1:
            groups += [(VMEM, lines(demand)), (VMEM, images), (VMEM, list(terms_y))]
            out = row_part(EXTRA)
        else:
            groups += [(VMEM, saved_sums)]
            out = row_part(2 * saved_lines if saved_sums is not None else 0)
        term_y, anchor_y, part, tiles = run(
            functools.partial(dual_body, step - 1, n_col),
            [full_y, full_y, out],
            groups,
            [scratch(lines_y, LANES), scratch(lines_x, LANES)],
            f"dual_{step - 1}",
            cost,
            tiles,
        )
        parts = [part] * n_row
        terms_y.insert(0, term_y)
    half_y = f32(n_chip * share_y + EXTRA, LANES)
    primal_adjoint, mine, other, tiles = run(
        body,
        [full_x, half_y, half_y],
        groups + [(VMEM, reduced), (VMEM, terms_x)],
        [scratch(lines_x, LANES), scratch(lines_y, LANES)],
        "primal_0",
        cost,
        tiles,
    )
    received = lax.ppermute(other, "col", [(i, i ^ 1) for i in range(n_col)])
    parts = run(
        functools.partial(split_body, n_chip),
        [f32(share_y + EXTRA, LANES)] * n_chip,
        [(VMEM, mine), (VMEM, received)],
        [],
        "split",
    )
    parts = exchange(parts, "col", 2)
    scales = (1.0 / math.sqrt(column_length * n_col), 1.0 / math.sqrt(row_length * n_row))
    dual_adjoint, gradients = run(
        functools.partial(last_body, scales),
        [f32(share_y, LANES), ("smem", f32(2))],
        [(SMEM, step_sizes), (VMEM, parts), (VMEM, term_y), (VMEM, anchor_y)],
        [],
        "last",
    )
    return (primal_adjoint.reshape(-1), dual_adjoint.reshape(-1), gradients)


def sum_pair(partial):
    size = lax.axis_size("col")
    return partial + lax.ppermute(partial, "col", [(i, i ^ 1) for i in range(size)])


def solution(mesh):
    placed = (
        P("row", "col", None, None, None),
        P("row", "col", None),
        P("row", "col", None),
        P("row", "col"),
        P(None, "col"),
        P(None, "row"),
        P(None, "col"),
        P(None, "row"),
        P("col"),
        P("row"),
        P("col"),
        P(),
        P("col"),
        P("row"),
    )
    return jax.shard_map(
        local,
        mesh=mesh,
        in_specs=placed,
        out_specs=(P("col"), P(("row", "col")), P()),
        check_vma=False,
    )
```

```python
import functools
import math

import jax
import jax.numpy as jnp
from jax import lax
from jax.experimental import pallas as pl
from jax.experimental.pallas import tpu as pltpu
from jax.sharding import PartitionSpec as P

LANES = 128
EXTRA = 16
CHUNKS = 4
SCALES = 16
STEPS = 64.0
LIMIT = 32760.0
FINE = 65000.0
LN2 = math.log(2.0)
VMEM = pl.BlockSpec(memory_space=pltpu.VMEM)
SMEM = pl.BlockSpec(memory_space=pltpu.SMEM)
ANY = pl.BlockSpec(memory_space=pl.ANY)
GRANT = 16 * 1024 * 1024


def weight_of(step):
    return (step + 1.0) / (step + 2.0)


def tree_sum(parts):
    while len(parts) > 1:
        parts = [parts[i] + parts[i + 1] for i in range(0, len(parts), 2)]
    return parts[0]


def fold(lines):
    return lines.reshape(-1, 8, LANES).sum(axis=0)


def rounded(values):
    return values.astype(jnp.bfloat16).astype(jnp.float32)


def add_products(transpose, in_index, out_index, count, tiles, slots, source, total):
    per_block = tiles.shape[-1] // LANES
    several = len(total.shape) == 3
    live_count = count[0, 0]
    for slot in slots:
        start = in_index[0, 0, slot] * per_block
        place = out_index[0, 0, slot] * per_block
        live = (live_count > slot).astype(jnp.float32)
        halves = []
        for half in range(per_block):
            if not several:
                halves.append(source[pl.ds(start + half, 1), :])
                continue
            vectors = source.shape[0]
            rows = -(-vectors // 8) * 8
            which = lax.broadcasted_iota(jnp.int32, (rows, LANES), 0)
            stacked = jnp.zeros((rows, LANES), jnp.float32)
            for vector in range(vectors):
                line = source[vector, pl.ds(start + half, 1), :]
                stacked = jnp.where(which == vector, line, stacked)
            halves.append(stacked)
        block = (jnp.concatenate(halves, axis=1) * live).astype(jnp.bfloat16)
        contract = ((1,), (0,)) if transpose else ((1,), (1,))
        product = lax.dot_general(
            block, tiles[slot], (contract, ((), ())), preferred_element_type=jnp.float32
        )
        for half in range(per_block):
            at = pl.ds(place + half, 1)
            lanes = slice(half * LANES, (half + 1) * LANES)
            if several:
                for vector in range(total.shape[0]):
                    total[vector, at, :] += product[vector : vector + 1, lanes]
            else:
                total[at, :] += product[:, lanes]


def whole_scale(lines):
    largest = jnp.maximum(jnp.max(jnp.abs(lines), axis=0, keepdims=True), 1e-30)
    return jnp.floor(jnp.log(largest) * (STEPS / LN2) + 1.0)


def to_units(code):
    return jnp.exp(code * (-LN2 / STEPS)) * LIMIT


def from_units(code):
    return jnp.exp(code * (LN2 / STEPS)) * (1.0 / LIMIT)


def nearest(values):
    return jnp.floor(values + 0.5)


def short(values):
    return values.astype(jnp.int32).astype(jnp.int16)


def long(values):
    return values.astype(jnp.int32).astype(jnp.float32)


def encode(lines):
    code = whole_scale(lines)
    return nearest(lines * to_units(code)), code


def encode_fine(lines):
    code = whole_scale(lines)
    units = lines * to_units(code)
    coarse = nearest(units)
    return coarse, nearest((units - coarse) * FINE), code


def scale_rows(codes):
    which = lax.broadcasted_iota(jnp.int32, (SCALES, LANES), 0)
    rows = jnp.zeros((SCALES, LANES), jnp.float32)
    for spot, code in enumerate(codes):
        rows = jnp.where(which == spot, code, rows)
    return short(rows)


def codes_of(part):
    return long(part[part.shape[0] - SCALES :, :])


def group(part, lines, size, spot):
    return part[lines + spot * size : lines + (spot + 1) * size, :]


def both(lines, mine, received):
    ours, theirs = codes_of(mine)[:1], codes_of(received)[:1]
    return long(mine[:lines, :]) * from_units(ours) + long(received[:lines, :]) * from_units(theirs)


def both_fine(lines, mine, received):
    sums = 0.0
    for part in (mine, received):
        units = long(group(part, lines, EXTRA, 0))
        sums += (units[:8] + units[8:] * (1.0 / FINE)) * from_units(codes_of(part)[1:2])
    return sums


def write_payload(out, lines, main, groups):
    units, code = encode(main)
    out[:lines, :] = short(units)
    codes = [code]
    row = lines
    for units, code in groups:
        out[row : row + units.shape[0], :] = units
        row += units.shape[0]
        codes.append(code)
    out[row:, :] = scale_rows(codes)


def coded(lines):
    units, code = encode(lines)
    return short(units), code


def coded_fine(lines):
    coarse, fine, code = encode_fine(lines)
    return short(jnp.concatenate([coarse, fine], axis=0)), code


def middle_body(kind, lines, size, mine, received, kept, *outs):
    main = both(lines, mine, received)
    groups = []
    if kind == "scatter":
        out, keep = outs
        codes = codes_of(received)
        for spot in range(kept.shape[0]):
            units = long(group(received, lines, size, spot))
            sums = kept[spot] + units * from_units(codes[spot + 1 : spot + 2])
            if spot % 2:
                groups.append(coded(sums))
            else:
                keep[spot // 2] = sums
    elif kind == "gather":
        (out,) = outs
        count = (mine.shape[0] - lines - SCALES) // size
        for part in (mine, received):
            codes = codes_of(part)
            for spot in range(count):
                groups.append((group(part, lines, size, spot), codes[spot + 1 : spot + 2]))
    elif kind == "sums":
        (out,) = outs
        groups.append(coded_fine(both_fine(lines, mine, received)))
    else:
        (out,) = outs
    write_payload(out, lines, main, groups)


def halve_body(kept, received, keep, send):
    count = kept.shape[0] - 1
    tail = kept[count] + received[count]
    for spot in range(count):
        (send if spot % 2 else keep)[spot // 2] = kept[spot] + received[spot]
    keep[count // 2] = tail
    send[count // 2] = tail


def first_body(
    step, n_row, rows_far, columns_far, count, tile_data, mask_far, cotangent_far, saved_far,
    tiles, term, anchor, *refs
):
    out, keep, source, total, rows, columns, mask, cotangent, saved, arrived, ready = refs
    slots = tiles.shape[0]
    chunk = slots // CHUNKS
    pairs = [(mask_far, mask), (cotangent_far, cotangent), (saved_far, saved)]
    pairs += [(rows_far, rows), (columns_far, columns)]
    small = [
        pltpu.make_async_copy(far_ref, near, ready.at[spot])
        for spot, (far_ref, near) in enumerate(pairs)
    ]
    for copy in small:
        copy.start()

    def fetch(part):
        span = pl.ds(part * chunk, chunk)
        return pltpu.make_async_copy(tile_data.at[0, 0, span], tiles.at[span], arrived.at[part])

    for part in range(CHUNKS):
        fetch(part).start()
    total[...] = jnp.zeros_like(total)
    for copy in small:
        copy.wait()
    weight = weight_of(step)
    adjoint = cotangent[...]
    anchor[...] = (1.0 - weight) * adjoint
    value = mask[:, step, :].astype(jnp.float32) * weight * adjoint
    term[...] = value
    source[0] = rounded(value)
    iterations = source.shape[0] - 1
    for vector in range(iterations):
        source[vector + 1] = rounded(saved[:, vector, :])
    for part in range(CHUNKS):
        fetch(part).wait()
        span = range(part * chunk, (part + 1) * chunk)
        add_products(True, rows, columns, count, tiles, span, source, total)
    lines = total.shape[1]
    share = lines // n_row
    me = lax.axis_index("row")
    groups = []
    for part in range(n_row):
        at = pl.ds(pl.multiple_of((me ^ part) * share, share), share)
        sums = total[1:, at, :].reshape(iterations * share, LANES)
        if part % 2:
            groups.append(coded(sums))
        else:
            keep[part // 2] = sums
    write_payload(out, lines, total[0], groups)


def dual_body(
    step, n_col, rows, columns, count, sizes, tiles, mask, image, received, before, anchor, *refs
):
    last = step == 0
    if last:
        demand, images, terms, term, anchor_out, out, _, source, total = refs
    else:
        saved, term, anchor_out, out, _, source, total = refs
    weight = weight_of(step)
    adjoint = before[...] + sizes[0] * (image[...] + received[...])
    anchor_out[...] = anchor[...] + (1.0 - weight) * adjoint
    value = mask[:, step, :].astype(jnp.float32) * weight * adjoint
    term[...] = value
    source[...] = rounded(value)
    total[...] = jnp.zeros_like(total)
    add_products(True, rows, columns, count, tiles, range(tiles.shape[0]), source, total)
    lines = total.shape[0]
    groups = []
    if last:
        share = demand[...] * (1.0 / n_col)
        found = value * (share - images[0])
        for other, earlier in enumerate(terms):
            found += earlier[...] * (share - images[other + 1])
        groups.append(coded_fine(fold(found)))
    elif saved is not None:
        groups.append(coded(saved[...]))
    write_payload(out, lines, total[...], groups)


def primal_body(
    kind, step, n_row, n_col,
    rows, columns, count, sizes, tiles, mask, mine, received, before, anchor, *refs
):
    last = kind == "sums"
    if last:
        reduced, terms, final, keep, send, _, source, out = refs
    elif kind == "scatter":
        kept, term, adjoint_out, anchor_out, out, saved, _, source = refs
    elif kind == "gather":
        cost, upper, primal, term, adjoint_out, anchor_out, out, reduced, images, _, source, total = refs
    else:
        term, adjoint_out, anchor_out, out, _, source = refs
    sigma = sizes[1]
    weight = weight_of(step)
    lines = mask.shape[0]
    back = both(lines, mine, received)
    adjoint = before[...]
    anchored = (1.0 - weight) * adjoint
    if anchor is not None:
        anchored = anchor[...] + anchored
    value = mask[:, step, :].astype(jnp.float32) * (weight * adjoint - 2.0 * sigma * back)
    after = value + sigma * back
    if last:
        final[...] = after + anchored
    else:
        term[...] = value
        adjoint_out[...] = after
        anchor_out[...] = anchored
    all_slots = range(tiles.shape[0])
    if kind == "gather":
        iterations = reduced.shape[0]
        share = lines // n_row
        size = iterations * share
        me = lax.axis_index("row")
        owners = gather_order(n_row)
        held = n_row // 2
        codes = [codes_of(mine), codes_of(received)]
        for spot, owner in enumerate(owners):
            part, where = (mine, received)[spot // held], spot % held
            at = pl.ds(pl.multiple_of((me ^ owner) * share, share), share)
            code = codes[spot // held][where + 1 : where + 2]
            sums = long(group(part, lines, size, where)) * from_units(code)
            reduced[:, at, :] = cost[at, :][None] - sums.reshape(iterations, share, LANES)
        source[0] = rounded(value)
        for vector in range(iterations):
            saved = primal[:, vector, :]
            half = jnp.minimum(jnp.maximum(saved - sizes[0] * reduced[vector], 0.0), upper[...])
            source[vector + 1] = rounded(2.0 * half - saved)
        total[...] = jnp.zeros_like(total)
        add_products(False, columns, rows, count, tiles, all_slots, source, total)
        out[...] = total[0]
        images[...] = total[1:]
        return
    source[...] = rounded(value)
    out[...] = jnp.zeros_like(out)
    add_products(False, columns, rows, count, tiles, all_slots, source, out)
    if kind == "scatter":
        size = saved.shape[0]
        code = codes_of(received)[1:2]
        saved[...] = kept[0] + long(group(received, lines, size, 0)) * from_units(code)
    if last:
        sums = both_fine(lines, mine, received)
        found = value * reduced[0]
        for other_step, later in enumerate(terms):
            found += later[...] * reduced[other_step + 1]
        tail = jnp.concatenate([sums, -fold(found)], axis=0)
        share = out.shape[0] // n_col
        me = lax.axis_index("col")
        for part in range(n_col):
            at = pl.ds((me ^ part) * share, share)
            (send if part % 2 else keep)[part // 2, :share, :] = out[at, :]
        for half in (keep, send):
            half[n_col // 2, :EXTRA, :] = tail


def last_body(scales, sizes, kept, received, term, anchor, adjoint, gradients):
    share = adjoint.shape[0]
    image = kept[0, :share, :] + received[0, :share, :]
    sums = kept[1, :EXTRA, :] + received[1, :EXTRA, :]
    at = pl.ds(lax.axis_index("col") * share, share)
    adjoint[...] = term[at, :] + sizes[0] * image + anchor[at, :]
    gradients[0] = jnp.sum(sums[8:]) * scales[0]
    gradients[1] = jnp.sum(sums[:8]) * scales[1]


def far(array):
    return pltpu.with_memory_space_constraint(array, pltpu.HBM)


def run(body, out_shape, groups, scratch, name, cost=None, tiles=None):
    flat, specs, widths, aliases = [], [], [], {}
    for spec, value in groups:
        if value is None:
            widths.append(None)
            continue
        many = isinstance(value, (list, tuple))
        widths.append(len(value) if many else 0)
        for array in value if many else [value]:
            if array is tiles:
                aliases[len(flat)] = len(out_shape)
                array = pltpu.with_memory_space_constraint(array, pltpu.VMEM)
            flat.append(array)
            specs.append(spec)

    def kernel(*refs):
        given = list(refs)
        taken = []
        for width in widths:
            if width is None:
                taken.append(None)
            elif width == 0:
                taken.append(given.pop(0))
            else:
                taken.append([given.pop(0) for _ in range(width)])
        body(*taken, *given)

    in_smem = [isinstance(shape, tuple) for shape in out_shape]
    shapes = [shape[1] if isinstance(shape, tuple) else shape for shape in out_shape]
    if tiles is not None:
        shapes.append(pltpu.VMEM(tiles.shape, tiles.dtype))
        in_smem.append(False)
    return pl.pallas_call(
        kernel,
        out_shape=shapes,
        in_specs=specs,
        out_specs=[SMEM if smem else VMEM for smem in in_smem],
        scratch_shapes=scratch,
        input_output_aliases=aliases,
        compiler_params=pltpu.CompilerParams(vmem_limit_bytes=GRANT),
        cost_estimate=cost,
        name=name,
    )(*flat)


def gather_order(size):
    order, stride = [0], size // 2
    while stride:
        order += [owner ^ stride for owner in order]
        stride //= 2
    return order


def swap(array, axis, stride):
    size = lax.axis_size(axis)
    return lax.ppermute(array, axis, [(i, i ^ stride) for i in range(size)])


def strides(size):
    return [1 << bit for bit in range(size.bit_length() - 1)]


def local(
    tile_data,
    tile_row_block,
    tile_column_block,
    tile_count,
    saved_primal,
    saved_dual,
    primal_mask,
    dual_mask,
    cost_vector,
    demand,
    upper_bound,
    step_sizes,
    primal_cotangent,
    dual_cotangent,
):
    slots, width = tile_data.shape[2], tile_data.shape[-1]
    iterations, row_length = saved_dual.shape
    column_length = saved_primal.shape[1]
    n_row, n_col = lax.axis_size("row"), lax.axis_size("col")
    lines_y, lines_x = row_length // LANES, column_length // LANES
    share_y, share_x = lines_y // n_col, lines_x // n_row
    saved_lines = iterations * share_x
    last = iterations - 1
    cost = pl.CostEstimate(
        flops=2 * tile_data.size, bytes_accessed=2 * tile_data.size, transcendentals=0
    )

    def lines(array):
        if array.ndim == 1:
            return array.reshape(-1, LANES)
        return array.reshape(iterations, -1, LANES).transpose(1, 0, 2)

    def f32(*shape):
        return jax.ShapeDtypeStruct(shape, jnp.float32)

    def payload(size, count):
        return jax.ShapeDtypeStruct((lines_x + size * count + SCALES, LANES), jnp.int16)

    def row_rounds(kind, part, size, kept):
        order = strides(n_row)
        if kind == "gather":
            order = order[::-1]
        for spot, stride in enumerate(order):
            received = swap(part, "row", stride)
            if spot == len(order) - 1:
                return part, received, kept
            outs, count = [], 1
            if kind == "scatter":
                count = kept.shape[0] // 2
                outs = [f32(count, size, LANES)]
            elif kind == "gather":
                count = 2 << spot
            elif kind == "plain":
                count = 0
            part, *more = run(
                functools.partial(middle_body, kind, lines_x, size),
                [payload(size, count)] + outs,
                [(VMEM, part), (VMEM, received), (VMEM, kept)],
                [],
                f"{kind}_{spot}",
            )
            if kind == "scatter":
                (kept,) = more

    def col_rounds(part):
        order = strides(n_col)
        for stride in order[:-1]:
            part = part + swap(part, "col", stride)
        return part, swap(part, "col", order[-1])

    def scratch(*shape):
        return pltpu.VMEM(shape, jnp.float32)

    mask_x, mask_y = lines(primal_mask), lines(dual_mask)
    full_x, full_y = f32(lines_x, LANES), f32(lines_y, LANES)
    where = [(SMEM, tile_row_block), (SMEM, tile_column_block), (SMEM, tile_count)]
    saved = lines(saved_dual)
    tiles, term_y, anchor_y, part, kept = run(
        functools.partial(first_body, last, n_row),
        [pltpu.VMEM((slots, width, width), jnp.bfloat16), full_y, full_y]
        + [payload(saved_lines, n_row // 2), f32(n_row // 2, saved_lines, LANES)],
        [(ANY, far(tile_row_block)), (ANY, far(tile_column_block)), (SMEM, tile_count)]
        + [(ANY, far(tile_data)), (ANY, far(mask_y)), (ANY, far(lines(dual_cotangent)))]
        + [(ANY, far(saved))],
        [
            scratch(iterations + 1, lines_y, LANES),
            scratch(iterations + 1, lines_x, LANES),
            pltpu.SMEM(tile_row_block.shape, jnp.int32),
            pltpu.SMEM(tile_row_block.shape, jnp.int32),
            pltpu.VMEM(mask_y.shape, jnp.int32),
            scratch(lines_y, LANES),
            scratch(*saved.shape),
            pltpu.SemaphoreType.DMA((CHUNKS,)),
            pltpu.SemaphoreType.DMA((5,)),
        ],
        "first",
        cost,
    )
    adjoint_x, anchor_x = lines(primal_cotangent), None
    terms_x, terms_y = [], [term_y]
    reduced = images = saved_sums = None
    for step in reversed(range(iterations)):
        kind = {0: "sums", last: "scatter", last - 1: "gather"}.get(step, "plain")
        size = EXTRA if kind == "sums" else saved_lines
        mine, received, kept = row_rounds(kind, part, size, kept)
        groups = where + [(SMEM, step_sizes), (VMEM, tiles), (VMEM, mask_x)]
        groups += [(VMEM, mine), (VMEM, received), (VMEM, adjoint_x), (VMEM, anchor_x)]
        body = functools.partial(primal_body, kind, step, n_row, n_col)
        if step == 0:
            break
        outs = [full_x, full_x, full_x, full_y]
        extra = [scratch(lines_x, LANES)]
        if kind == "scatter":
            groups += [(VMEM, kept)]
            outs.append(f32(saved_lines, LANES))
        if kind == "gather":
            outs += [f32(iterations, lines_x, LANES), f32(iterations, lines_y, LANES)]
            groups += [(VMEM, lines(cost_vector)), (VMEM, lines(upper_bound))]
            groups += [(VMEM, lines(saved_primal))]
            extra = [
                scratch(iterations + 1, lines_x, LANES),
                scratch(iterations + 1, lines_y, LANES),
            ]
        term_x, adjoint_x, anchor_x, partial, *more, tiles = run(
            body, outs, groups, extra, f"primal_{step}", cost, tiles
        )
        kept = saved_sums = None
        if kind == "scatter":
            (saved_sums,) = more
        elif kind == "gather":
            reduced, images = more
        terms_x.insert(0, term_x)
        image, received = col_rounds(partial)
        groups = where + [(SMEM, step_sizes), (VMEM, tiles), (VMEM, mask_y)]
        groups += [(VMEM, image), (VMEM, received), (VMEM, term_y), (VMEM, anchor_y)]
        if step == 1:
            groups += [(VMEM, lines(demand)), (VMEM, images), (VMEM, list(terms_y))]
            out = payload(EXTRA, 1)
        else:
            groups += [(VMEM, saved_sums)]
            out = payload(saved_lines, 0 if saved_sums is None else 1)
        term_y, anchor_y, part, tiles = run(
            functools.partial(dual_body, step - 1, n_col),
            [full_y, full_y, out],
            groups,
            [scratch(lines_y, LANES), scratch(lines_x, LANES)],
            f"dual_{step - 1}",
            cost,
            tiles,
        )
        terms_y.insert(0, term_y)

    def halves(count):
        return [f32(count + 1, max(share_y, EXTRA), LANES)] * 2

    primal_adjoint, kept, sent, tiles = run(
        body,
        [full_x] + halves(n_col // 2),
        groups + [(VMEM, reduced), (VMEM, terms_x)],
        [scratch(lines_x, LANES), scratch(lines_y, LANES)],
        "primal_0",
        cost,
        tiles,
    )
    for stride in strides(n_col):
        received = swap(sent, "col", stride)
        count = kept.shape[0] - 1
        if count > 1:
            kept, sent = run(
                halve_body, halves(count // 2), [(VMEM, kept), (VMEM, received)], [], f"halve_{count}"
            )
    scales = (1.0 / math.sqrt(column_length * n_col), 1.0 / math.sqrt(row_length * n_row))
    dual_adjoint, gradients = run(
        functools.partial(last_body, scales),
        [f32(share_y, LANES), ("smem", f32(2))],
        [(SMEM, step_sizes), (VMEM, kept), (VMEM, received), (VMEM, term_y), (VMEM, anchor_y)],
        [],
        "last",
    )
    return (primal_adjoint.reshape(-1), dual_adjoint.reshape(-1), gradients)


def solution(mesh):
    placed = (
        P("row", "col", None, None, None),
        P("row", "col", None),
        P("row", "col", None),
        P("row", "col"),
        P(None, "col"),
        P(None, "row"),
        P(None, "col"),
        P(None, "row"),
        P("col"),
        P("row"),
        P("col"),
        P(),
        P("col"),
        P("row"),
    )
    return jax.shard_map(
        local,
        mesh=mesh,
        in_specs=placed,
        out_specs=(P("col"), P(("row", "col")), P()),
        check_vma=False,
    )
```

```python
import functools
import math

import jax
import jax.numpy as jnp
from jax import lax
from jax.experimental import pallas as pl
from jax.experimental.pallas import tpu as pltpu
from jax.sharding import PartitionSpec as P

LANES = 128
EXTRA = 16
CHUNKS = 8
SCALES = 16
STEPS = 64.0
LIMIT = 32760.0
FINE = 65000.0
LN2 = math.log(2.0)
VMEM = pl.BlockSpec(memory_space=pltpu.VMEM)
SMEM = pl.BlockSpec(memory_space=pltpu.SMEM)
ANY = pl.BlockSpec(memory_space=pl.ANY)
GRANT = 16 * 1024 * 1024


def weight_of(step):
    return (step + 1.0) / (step + 2.0)


def tree_sum(parts):
    while len(parts) > 1:
        parts = [parts[i] + parts[i + 1] for i in range(0, len(parts), 2)]
    return parts[0]


def fold(lines):
    return lines.reshape(-1, 8, LANES).sum(axis=0)


def rounded(values):
    return values.astype(jnp.bfloat16).astype(jnp.float32)


def add_products(in_index, out_index, count, tiles, slots, source, total):
    per_block = tiles.shape[-1] // LANES
    several = len(total.shape) == 3
    live_count = count[0, 0]
    for slot in slots:
        start = in_index[0, 0, slot] * per_block
        place = out_index[0, 0, slot] * per_block
        live = (live_count > slot).astype(jnp.float32)
        halves = []
        for half in range(per_block):
            if not several:
                halves.append(source[pl.ds(start + half, 1), :])
                continue
            vectors = source.shape[0]
            rows = -(-vectors // 8) * 8
            which = lax.broadcasted_iota(jnp.int32, (rows, LANES), 0)
            stacked = jnp.zeros((rows, LANES), jnp.float32)
            for vector in range(vectors):
                line = source[vector, pl.ds(start + half, 1), :]
                stacked = jnp.where(which == vector, line, stacked)
            halves.append(stacked)
        block = (jnp.concatenate(halves, axis=1) * live).astype(jnp.bfloat16)
        product = jnp.dot(block, tiles[slot], preferred_element_type=jnp.float32)
        for half in range(per_block):
            at = pl.ds(place + half, 1)
            lanes = slice(half * LANES, (half + 1) * LANES)
            if several:
                for vector in range(total.shape[0]):
                    total[vector, at, :] += product[vector : vector + 1, lanes]
            else:
                total[at, :] += product[:, lanes]


def whole_scale(lines):
    largest = jnp.maximum(jnp.max(jnp.abs(lines), axis=0, keepdims=True), 1e-30)
    return jnp.floor(jnp.log(largest) * (STEPS / LN2) + 1.0)


def to_units(code):
    return jnp.exp(code * (-LN2 / STEPS)) * LIMIT


def from_units(code):
    return jnp.exp(code * (LN2 / STEPS)) * (1.0 / LIMIT)


def nearest(values):
    return jnp.floor(values + 0.5)


def short(values):
    return values.astype(jnp.int32).astype(jnp.int16)


def long(values):
    return values.astype(jnp.int32).astype(jnp.float32)


def encode(lines):
    code = whole_scale(lines)
    return nearest(lines * to_units(code)), code


def encode_fine(lines):
    code = whole_scale(lines)
    units = lines * to_units(code)
    coarse = nearest(units)
    return coarse, nearest((units - coarse) * FINE), code


def scale_rows(codes):
    which = lax.broadcasted_iota(jnp.int32, (SCALES, LANES), 0)
    rows = jnp.zeros((SCALES, LANES), jnp.float32)
    for spot, code in enumerate(codes):
        rows = jnp.where(which == spot, code, rows)
    return short(rows)


def scales_of(part):
    codes = long(part[part.shape[0] - SCALES :, :])
    return [from_units(codes[spot : spot + 1]) for spot in range(2)]


def first_body(
    step, n_row, rows_far, columns_far, count, tile_data, mask_far, cotangent_far, saved_far,
    tiles, term, anchor, *refs
):
    outs = refs[:n_row]
    source, total, rows, columns, mask, cotangent, saved, arrived, ready = refs[n_row:]
    slots = tiles.shape[0]
    chunk = slots // CHUNKS
    pairs = [(mask_far, mask), (cotangent_far, cotangent), (saved_far, saved)]
    pairs += [(rows_far, rows), (columns_far, columns)]
    small = [
        pltpu.make_async_copy(far_ref, near, ready.at[spot])
        for spot, (far_ref, near) in enumerate(pairs)
    ]
    for copy in small:
        copy.start()

    def fetch(part):
        span = pl.ds(part * chunk, chunk)
        return pltpu.make_async_copy(tile_data.at[0, 0, span], tiles.at[span], arrived.at[part])

    for part in range(CHUNKS):
        fetch(part).start()
    total[...] = jnp.zeros_like(total)
    for copy in small:
        copy.wait()
    weight = weight_of(step)
    adjoint = cotangent[...]
    anchor[...] = (1.0 - weight) * adjoint
    value = mask[:, step, :].astype(jnp.float32) * weight * adjoint
    term[...] = value
    source[0] = rounded(value)
    iterations = source.shape[0] - 1
    for vector in range(iterations):
        source[vector + 1] = rounded(saved[:, vector, :])
    for part in range(CHUNKS):
        fetch(part).wait()
        span = range(part * chunk, (part + 1) * chunk)
        add_products(rows, columns, count, tiles, span, source, total)
    lines = total.shape[1]
    share = lines // n_row
    me = lax.axis_index("row")
    units, code = encode(total[0])
    units = short(units)
    for part, out in enumerate(outs):
        at = pl.ds(pl.multiple_of((me ^ part) * share, share), share)
        out[:lines, :] = units
        saved_units, saved_code = encode(total[1:, at, :].reshape(iterations * share, LANES))
        out[lines : lines + iterations * share, :] = short(saved_units)
        out[lines + iterations * share :, :] = scale_rows([code, saved_code])


def turn_body(tiles, turned, _):
    for slot in range(tiles.shape[0]):
        turned[slot] = tiles[slot].T


def dual_body(step, n_col, rows, columns, count, sizes, tiles, mask, parts, before, anchor, *refs):
    last = step == 0
    if last:
        demand, images, terms, term, anchor_out, out, _, source, total = refs
    else:
        saved, term, anchor_out, out, _, source, total = refs
    weight = weight_of(step)
    rows_y = before.shape[0]
    image = tree_sum([long(part[:rows_y, :]) * scales_of(part)[0] for part in parts])
    adjoint = before[...] + sizes[0] * image
    anchor_out[...] = anchor[...] + (1.0 - weight) * adjoint
    value = mask[:, step, :].astype(jnp.float32) * weight * adjoint
    term[...] = value
    source[...] = rounded(value)
    total[...] = jnp.zeros_like(total)
    add_products(rows, columns, count, tiles, range(tiles.shape[0]), source, total)
    lines = total.shape[0]
    units, code = encode(total[...])
    out[:lines, :] = short(units)
    if last:
        share = demand[...] * (1.0 / n_col)
        found = value * (share - images[0])
        for other, earlier in enumerate(terms):
            found += earlier[...] * (share - images[other + 1])
        coarse, fine, found_code = encode_fine(fold(found))
        out[lines : lines + EXTRA, :] = short(jnp.concatenate([coarse, fine], axis=0))
        out[lines + EXTRA :, :] = scale_rows([code, found_code])
    elif saved is None:
        out[lines:, :] = scale_rows([code])
    else:
        size = saved.shape[0]
        saved_units, saved_code = encode(saved[...])
        out[lines : lines + size, :] = short(saved_units)
        out[lines + size :, :] = scale_rows([code, saved_code])


def primal_body(kind, step, n_row, n_col, rows, columns, count, sizes, tiles, mask, parts, before, anchor, *refs):
    last = kind == "last"
    if last:
        reduced, terms, final, mine, other, _, source, out = refs
    elif kind == "sums":
        term, adjoint_out, anchor_out, out, saved, _, source = refs
    elif kind == "shares":
        cost, upper, primal, term, adjoint_out, anchor_out, out, reduced, images, _, source, total = refs
    else:
        term, adjoint_out, anchor_out, out, _, source = refs
    sigma = sizes[1]
    weight = weight_of(step)
    lines = mask.shape[0]
    scales = [scales_of(part) for part in parts]
    back = tree_sum([long(part[:lines, :]) * scale[0] for part, scale in zip(parts, scales)])
    adjoint = before[...]
    anchored = (1.0 - weight) * adjoint
    if anchor is not None:
        anchored = anchor[...] + anchored
    value = mask[:, step, :].astype(jnp.float32) * (weight * adjoint - 2.0 * sigma * back)
    after = value + sigma * back
    if last:
        final[...] = after + anchored
    else:
        term[...] = value
        adjoint_out[...] = after
        anchor_out[...] = anchored
    all_slots = range(tiles.shape[0])
    if kind == "shares":
        iterations = reduced.shape[0]
        share = lines // n_row
        size = iterations * share
        me = lax.axis_index("row")
        for part, (held, scale) in enumerate(zip(parts, scales)):
            at = pl.ds(pl.multiple_of((me ^ part) * share, share), share)
            sums = (long(held[lines : lines + size, :]) * scale[1]).reshape(iterations, share, LANES)
            reduced[:, at, :] = cost[at, :][None] - sums
        source[0] = rounded(value)
        for vector in range(iterations):
            saved = primal[:, vector, :]
            half = jnp.minimum(jnp.maximum(saved - sizes[0] * reduced[vector], 0.0), upper[...])
            source[vector + 1] = rounded(2.0 * half - saved)
        total[...] = jnp.zeros_like(total)
        add_products(columns, rows, count, tiles, all_slots, source, total)
        out[...] = total[0]
        images[...] = total[1:]
        return
    source[...] = rounded(value)
    out[...] = jnp.zeros_like(out)
    add_products(columns, rows, count, tiles, all_slots, source, out)
    if kind == "sums":
        size = saved.shape[0]
        saved[...] = tree_sum(
            [long(part[lines : lines + size, :]) * scale[1] for part, scale in zip(parts, scales)]
        )
    if last:
        sums = 0.0
        for part, scale in zip(parts, scales):
            units = long(part[lines : lines + EXTRA, :])
            sums += (units[:8] + units[8:] * (1.0 / FINE)) * scale[1]
        found = value * reduced[0]
        for other_step, later in enumerate(terms):
            found += later[...] * reduced[other_step + 1]
        tail = jnp.concatenate([sums, -fold(found)], axis=0)
        share = out.shape[0] // n_col
        core = lax.axis_index("col") % 2
        for chip in range(n_col // 2):
            span = slice(chip * share, (chip + 1) * share)
            mine[span, :] = out[pl.ds((2 * chip + core) * share, share), :]
            other[span, :] = out[pl.ds((2 * chip + 1 - core) * share, share), :]
        mine[n_col // 2 * share :, :] = tail
        other[n_col // 2 * share :, :] = tail


def pair_body(mine, received, out):
    lines = mine.shape[0]
    units, code = encode(mine[...] + received[...])
    out[:lines, :] = short(units)
    out[lines:, :] = scale_rows([code])


def split_body(n_chip, mine, received, *outs):
    share = (mine.shape[0] - EXTRA) // n_chip
    chip = lax.axis_index("col") // 2
    tail = mine[n_chip * share :, :] + received[n_chip * share :, :]
    for part, out in enumerate(outs):
        at = pl.ds((chip ^ part) * share, share)
        out[:share, :] = mine[at, :] + received[at, :]
        out[share:, :] = tail


def last_body(scales, sizes, parts, term, anchor, adjoint, gradients):
    share = adjoint.shape[0]
    total = tree_sum([part[...] for part in parts])
    at = pl.ds(lax.axis_index("col") * share, share)
    adjoint[...] = term[at, :] + sizes[0] * total[:share] + anchor[at, :]
    gradients[0] = jnp.sum(total[share + 8 : share + 16]) * scales[0]
    gradients[1] = jnp.sum(total[share : share + 8]) * scales[1]


def far(array):
    return pltpu.with_memory_space_constraint(array, pltpu.HBM)


def run(body, out_shape, groups, scratch, name, cost=None, tiles=None):
    flat, specs, widths, aliases = [], [], [], {}
    for spec, value in groups:
        if value is None:
            widths.append(None)
            continue
        many = isinstance(value, (list, tuple))
        widths.append(len(value) if many else 0)
        for array in value if many else [value]:
            if array is tiles:
                aliases[len(flat)] = len(out_shape)
                array = pltpu.with_memory_space_constraint(array, pltpu.VMEM)
            flat.append(array)
            specs.append(spec)

    def kernel(*refs):
        given = list(refs)
        taken = []
        for width in widths:
            if width is None:
                taken.append(None)
            elif width == 0:
                taken.append(given.pop(0))
            else:
                taken.append([given.pop(0) for _ in range(width)])
        body(*taken, *given)

    in_smem = [isinstance(shape, tuple) for shape in out_shape]
    shapes = [shape[1] if isinstance(shape, tuple) else shape for shape in out_shape]
    if tiles is not None:
        shapes.append(pltpu.VMEM(tiles.shape, tiles.dtype))
        in_smem.append(False)
    return pl.pallas_call(
        kernel,
        out_shape=shapes,
        in_specs=specs,
        out_specs=[SMEM if smem else VMEM for smem in in_smem],
        scratch_shapes=scratch,
        input_output_aliases=aliases,
        compiler_params=pltpu.CompilerParams(vmem_limit_bytes=GRANT),
        cost_estimate=cost,
        name=name,
    )(*flat)


def swap(array, axis, stride):
    size = lax.axis_size(axis)
    return lax.ppermute(array, axis, [(i, i ^ stride) for i in range(size)])


def exchange(parts, axis, stride=1):
    size = lax.axis_size(axis) // stride
    return [parts[0]] + [swap(parts[k], axis, k * stride) for k in range(1, size)]


def local(
    tile_data,
    tile_row_block,
    tile_column_block,
    tile_count,
    saved_primal,
    saved_dual,
    primal_mask,
    dual_mask,
    cost_vector,
    demand,
    upper_bound,
    step_sizes,
    primal_cotangent,
    dual_cotangent,
):
    slots, width = tile_data.shape[2], tile_data.shape[-1]
    iterations, row_length = saved_dual.shape
    column_length = saved_primal.shape[1]
    n_row, n_col = lax.axis_size("row"), lax.axis_size("col")
    n_chip = n_col // 2
    lines_y, lines_x = row_length // LANES, column_length // LANES
    share_y, share_x = lines_y // n_col, lines_x // n_row
    saved_lines = iterations * share_x
    last = iterations - 1
    cost = pl.CostEstimate(
        flops=2 * tile_data.size, bytes_accessed=2 * tile_data.size, transcendentals=0
    )

    def lines(array):
        if array.ndim == 1:
            return array.reshape(-1, LANES)
        return array.reshape(iterations, -1, LANES).transpose(1, 0, 2)

    def f32(*shape):
        return jax.ShapeDtypeStruct(shape, jnp.float32)

    def row_part(more):
        return jax.ShapeDtypeStruct((lines_x + more + SCALES, LANES), jnp.int16)

    def scratch(*shape):
        return pltpu.VMEM(shape, jnp.float32)

    mask_x, mask_y = lines(primal_mask), lines(dual_mask)
    full_x, full_y = f32(lines_x, LANES), f32(lines_y, LANES)
    where = [(SMEM, tile_row_block), (SMEM, tile_column_block), (SMEM, tile_count)]
    saved = lines(saved_dual)
    tiles, term_y, anchor_y, *parts = run(
        functools.partial(first_body, last, n_row),
        [pltpu.VMEM((slots, width, width), jnp.bfloat16), full_y, full_y]
        + [row_part(saved_lines)] * n_row,
        [(ANY, far(tile_row_block)), (ANY, far(tile_column_block)), (SMEM, tile_count)]
        + [(ANY, far(tile_data)), (ANY, far(mask_y)), (ANY, far(lines(dual_cotangent)))]
        + [(ANY, far(saved))],
        [
            scratch(iterations + 1, lines_y, LANES),
            scratch(iterations + 1, lines_x, LANES),
            pltpu.SMEM(tile_row_block.shape, jnp.int32),
            pltpu.SMEM(tile_row_block.shape, jnp.int32),
            pltpu.VMEM(mask_y.shape, jnp.int32),
            scratch(lines_y, LANES),
            scratch(*saved.shape),
            pltpu.SemaphoreType.DMA((CHUNKS,)),
            pltpu.SemaphoreType.DMA((5,)),
        ],
        "first",
        cost,
    )
    turned, tiles = run(
        turn_body,
        [pltpu.VMEM(tiles.shape, tiles.dtype)],
        [(VMEM, tiles)],
        [],
        "turn",
        cost,
        tiles,
    )
    adjoint_x, anchor_x = lines(primal_cotangent), None
    terms_x, terms_y = [], [term_y]
    reduced = images = saved_sums = None
    for step in reversed(range(iterations)):
        parts = exchange(parts, "row")
        kind = {0: "last", last: "sums", last - 1: "shares"}.get(step, "plain")
        groups = where + [(SMEM, step_sizes), (VMEM, turned), (VMEM, mask_x), (VMEM, parts)]
        groups += [(VMEM, adjoint_x), (VMEM, anchor_x)]
        body = functools.partial(primal_body, kind, step, n_row, n_col)
        if step == 0:
            break
        outs = [full_x, full_x, full_x, full_y]
        extra = [scratch(lines_x, LANES)]
        if kind == "sums":
            outs.append(f32(saved_lines, LANES))
        if kind == "shares":
            outs += [f32(iterations, lines_x, LANES), f32(iterations, lines_y, LANES)]
            groups += [(VMEM, lines(cost_vector)), (VMEM, lines(upper_bound))]
            groups += [(VMEM, lines(saved_primal))]
            extra = [
                scratch(iterations + 1, lines_x, LANES),
                scratch(iterations + 1, lines_y, LANES),
            ]
        term_x, adjoint_x, anchor_x, partial, *more, turned = run(
            body, outs, groups, extra, f"primal_{step}", cost, turned
        )
        if kind == "sums":
            (saved_sums,) = more
        elif kind == "shares":
            reduced, images = more
            saved_sums = None
        terms_x.insert(0, term_x)
        part = run(
            pair_body,
            [jax.ShapeDtypeStruct((lines_y + SCALES, LANES), jnp.int16)],
            [(VMEM, partial), (VMEM, swap(partial, "col", 1))],
            [],
            f"pair_{step}",
        )[0]
        parts = exchange([part] * n_chip, "col", 2)
        groups = where + [(SMEM, step_sizes), (VMEM, tiles), (VMEM, mask_y), (VMEM, parts)]
        groups += [(VMEM, term_y), (VMEM, anchor_y)]
        if step == 1:
            groups += [(VMEM, lines(demand)), (VMEM, images), (VMEM, list(terms_y))]
            out = row_part(EXTRA)
        else:
            groups += [(VMEM, saved_sums)]
            out = row_part(saved_lines if saved_sums is not None else 0)
        term_y, anchor_y, part, tiles = run(
            functools.partial(dual_body, step - 1, n_col),
            [full_y, full_y, out],
            groups,
            [scratch(lines_y, LANES), scratch(lines_x, LANES)],
            f"dual_{step - 1}",
            cost,
            tiles,
        )
        parts = [part] * n_row
        terms_y.insert(0, term_y)
    half_y = f32(n_chip * share_y + EXTRA, LANES)
    primal_adjoint, mine, other, turned = run(
        body,
        [pltpu.VMEM((lines_x, LANES), jnp.float32), half_y, half_y],
        groups + [(VMEM, reduced), (VMEM, terms_x)],
        [scratch(lines_x, LANES), scratch(lines_y, LANES)],
        "primal_0",
        cost,
        turned,
    )
    received = swap(other, "col", 1)
    parts = run(
        functools.partial(split_body, n_chip),
        [f32(share_y + EXTRA, LANES)] * n_chip,
        [(VMEM, mine), (VMEM, received)],
        [],
        "split",
    )
    parts = exchange(parts, "col", 2)
    scales = (1.0 / math.sqrt(column_length * n_col), 1.0 / math.sqrt(row_length * n_row))
    dual_adjoint, gradients = run(
        functools.partial(last_body, scales),
        [f32(share_y, LANES), ("smem", f32(2))],
        [(SMEM, step_sizes), (VMEM, parts), (VMEM, term_y), (VMEM, anchor_y)],
        [],
        "last",
    )
    return (primal_adjoint.reshape(-1), dual_adjoint.reshape(-1), gradients)


def solution(mesh):
    placed = (
        P("row", "col", None, None, None),
        P("row", "col", None),
        P("row", "col", None),
        P("row", "col"),
        P(None, "col"),
        P(None, "row"),
        P(None, "col"),
        P(None, "row"),
        P("col"),
        P("row"),
        P("col"),
        P(),
        P("col"),
        P("row"),
    )
    return jax.shard_map(
        local,
        mesh=mesh,
        in_specs=placed,
        out_specs=(P("col"), P(("row", "col")), P()),
        check_vma=False,
    )
```

```python
import functools
import math

import jax
import jax.numpy as jnp
from jax import lax
from jax.experimental import pallas as pl
from jax.experimental.pallas import tpu as pltpu
from jax.sharding import PartitionSpec as P

LANES = 128
EXTRA = 16
CHUNKS = 4
SCALES = 16
STEPS = 64.0
LIMIT = 32760.0
FINE = 65000.0
LN2 = math.log(2.0)
VMEM = pl.BlockSpec(memory_space=pltpu.VMEM)
SMEM = pl.BlockSpec(memory_space=pltpu.SMEM)
ANY = pl.BlockSpec(memory_space=pl.ANY)
GRANT = 16 * 1024 * 1024


def weight_of(step):
    return (step + 1.0) / (step + 2.0)


def tree_sum(parts):
    while len(parts) > 1:
        parts = [parts[i] + parts[i + 1] for i in range(0, len(parts), 2)]
    return parts[0]


def fold(lines):
    return lines.reshape(-1, 8, LANES).sum(axis=0)


def rounded(values):
    return values.astype(jnp.bfloat16).astype(jnp.float32)


def add_products(in_index, out_index, count, tiles, slots, source, total):
    per_block = tiles.shape[-1] // LANES
    several = len(total.shape) == 3
    live_count = count[0, 0]
    for slot in slots:
        start = in_index[0, 0, slot] * per_block
        place = out_index[0, 0, slot] * per_block
        live = (live_count > slot).astype(jnp.float32)
        halves = []
        for half in range(per_block):
            if not several:
                halves.append(source[pl.ds(start + half, 1), :])
                continue
            vectors = source.shape[0]
            rows = -(-vectors // 8) * 8
            which = lax.broadcasted_iota(jnp.int32, (rows, LANES), 0)
            stacked = jnp.zeros((rows, LANES), jnp.float32)
            for vector in range(vectors):
                line = source[vector, pl.ds(start + half, 1), :]
                stacked = jnp.where(which == vector, line, stacked)
            halves.append(stacked)
        block = (jnp.concatenate(halves, axis=1) * live).astype(jnp.bfloat16)
        product = jnp.dot(block, tiles[slot], preferred_element_type=jnp.float32)
        for half in range(per_block):
            at = pl.ds(place + half, 1)
            lanes = slice(half * LANES, (half + 1) * LANES)
            if several:
                for vector in range(total.shape[0]):
                    total[vector, at, :] += product[vector : vector + 1, lanes]
            else:
                total[at, :] += product[:, lanes]


def whole_scale(lines):
    largest = jnp.maximum(jnp.max(jnp.abs(lines), axis=0, keepdims=True), 1e-30)
    return jnp.floor(jnp.log(largest) * (STEPS / LN2) + 1.0)


def to_units(code):
    return jnp.exp(code * (-LN2 / STEPS)) * LIMIT


def from_units(code):
    return jnp.exp(code * (LN2 / STEPS)) * (1.0 / LIMIT)


def nearest(values):
    return jnp.floor(values + 0.5)


def short(values):
    return values.astype(jnp.int32).astype(jnp.int16)


def long(values):
    return values.astype(jnp.int32).astype(jnp.float32)


def encode(lines):
    code = whole_scale(lines)
    return nearest(lines * to_units(code)), code


def encode_fine(lines):
    code = whole_scale(lines)
    units = lines * to_units(code)
    coarse = nearest(units)
    return coarse, nearest((units - coarse) * FINE), code


def scale_rows(codes):
    which = lax.broadcasted_iota(jnp.int32, (SCALES, LANES), 0)
    rows = jnp.zeros((SCALES, LANES), jnp.float32)
    for spot, code in enumerate(codes):
        rows = jnp.where(which == spot, code, rows)
    return short(rows)


def scales_of(part):
    codes = long(part[part.shape[0] - SCALES :, :])
    return [from_units(codes[spot : spot + 1]) for spot in range(2)]


def first_body(
    step, n_row, rows_far, columns_far, count, tile_data, mask_far, cotangent_far, saved_far,
    tiles, term, anchor, *refs
):
    outs = refs[:n_row]
    source, total, rows, columns, mask, cotangent, saved, arrived, ready = refs[n_row:]
    slots = tiles.shape[0]
    chunk = slots // CHUNKS
    pairs = [(mask_far, mask), (cotangent_far, cotangent), (saved_far, saved)]
    pairs += [(rows_far, rows), (columns_far, columns)]
    small = [
        pltpu.make_async_copy(far_ref, near, ready.at[spot])
        for spot, (far_ref, near) in enumerate(pairs)
    ]
    for copy in small:
        copy.start()

    def fetch(part):
        span = pl.ds(part * chunk, chunk)
        return pltpu.make_async_copy(tile_data.at[0, 0, span], tiles.at[span], arrived.at[part])

    for part in range(CHUNKS):
        fetch(part).start(priority=part % 2)
    total[...] = jnp.zeros_like(total)
    for copy in small:
        copy.wait()
    weight = weight_of(step)
    adjoint = cotangent[...]
    anchor[...] = (1.0 - weight) * adjoint
    value = mask[:, step, :].astype(jnp.float32) * weight * adjoint
    term[...] = value
    source[0] = rounded(value)
    iterations = source.shape[0] - 1
    for vector in range(iterations):
        source[vector + 1] = rounded(saved[:, vector, :])
    for part in range(CHUNKS):
        fetch(part).wait()
        span = range(part * chunk, (part + 1) * chunk)
        add_products(rows, columns, count, tiles, span, source, total)
    lines = total.shape[1]
    share = lines // n_row
    me = lax.axis_index("row")
    units, code = encode(total[0])
    units = short(units)
    for part, out in enumerate(outs):
        at = pl.ds(pl.multiple_of((me ^ part) * share, share), share)
        out[:lines, :] = units
        saved_units, saved_code = encode(total[1:, at, :].reshape(iterations * share, LANES))
        out[lines : lines + iterations * share, :] = short(saved_units)
        out[lines + iterations * share :, :] = scale_rows([code, saved_code])


def turn_body(tiles, turned, _):
    for slot in range(tiles.shape[0]):
        turned[slot] = tiles[slot].T


def dual_body(step, n_col, rows, columns, count, sizes, tiles, mask, parts, before, anchor, *refs):
    last = step == 0
    if last:
        demand, images, terms, term, anchor_out, out, _, source, total = refs
    else:
        saved, term, anchor_out, out, _, source, total = refs
    weight = weight_of(step)
    rows_y = before.shape[0]
    image = tree_sum([long(part[:rows_y, :]) * scales_of(part)[0] for part in parts])
    adjoint = before[...] + sizes[0] * image
    anchor_out[...] = anchor[...] + (1.0 - weight) * adjoint
    value = mask[:, step, :].astype(jnp.float32) * weight * adjoint
    term[...] = value
    source[...] = rounded(value)
    total[...] = jnp.zeros_like(total)
    add_products(rows, columns, count, tiles, range(tiles.shape[0]), source, total)
    lines = total.shape[0]
    units, code = encode(total[...])
    out[:lines, :] = short(units)
    if last:
        share = demand[...] * (1.0 / n_col)
        found = value * (share - images[0])
        for other, earlier in enumerate(terms):
            found += earlier[...] * (share - images[other + 1])
        coarse, fine, found_code = encode_fine(fold(found))
        out[lines : lines + EXTRA, :] = short(jnp.concatenate([coarse, fine], axis=0))
        out[lines + EXTRA :, :] = scale_rows([code, found_code])
    elif saved is None:
        out[lines:, :] = scale_rows([code])
    else:
        size = saved.shape[0]
        saved_units, saved_code = encode(saved[...])
        out[lines : lines + size, :] = short(saved_units)
        out[lines + size :, :] = scale_rows([code, saved_code])


def primal_body(kind, step, n_row, n_col, rows, columns, count, sizes, tiles, mask, parts, before, anchor, *refs):
    last = kind == "last"
    if last:
        reduced, terms, final, mine, other, _, source, out = refs
    elif kind == "sums":
        term, adjoint_out, anchor_out, out, saved, _, source = refs
    elif kind == "shares":
        cost, upper, primal, term, adjoint_out, anchor_out, out, reduced, images, _, source, total = refs
    else:
        term, adjoint_out, anchor_out, out, _, source = refs
    sigma = sizes[1]
    weight = weight_of(step)
    lines = mask.shape[0]
    scales = [scales_of(part) for part in parts]
    back = tree_sum([long(part[:lines, :]) * scale[0] for part, scale in zip(parts, scales)])
    adjoint = before[...]
    anchored = (1.0 - weight) * adjoint
    if anchor is not None:
        anchored = anchor[...] + anchored
    value = mask[:, step, :].astype(jnp.float32) * (weight * adjoint - 2.0 * sigma * back)
    after = value + sigma * back
    if last:
        final[...] = after + anchored
    else:
        term[...] = value
        adjoint_out[...] = after
        anchor_out[...] = anchored
    all_slots = range(tiles.shape[0])
    if kind == "shares":
        iterations = reduced.shape[0]
        share = lines // n_row
        size = iterations * share
        me = lax.axis_index("row")
        for part, (held, scale) in enumerate(zip(parts, scales)):
            at = pl.ds(pl.multiple_of((me ^ part) * share, share), share)
            sums = (long(held[lines : lines + size, :]) * scale[1]).reshape(iterations, share, LANES)
            reduced[:, at, :] = cost[at, :][None] - sums
        source[0] = rounded(value)
        for vector in range(iterations):
            saved = primal[:, vector, :]
            half = jnp.minimum(jnp.maximum(saved - sizes[0] * reduced[vector], 0.0), upper[...])
            source[vector + 1] = rounded(2.0 * half - saved)
        total[...] = jnp.zeros_like(total)
        add_products(columns, rows, count, tiles, all_slots, source, total)
        out[...] = total[0]
        images[...] = total[1:]
        return
    source[...] = rounded(value)
    out[...] = jnp.zeros_like(out)
    add_products(columns, rows, count, tiles, all_slots, source, out)
    if kind == "sums":
        size = saved.shape[0]
        saved[...] = tree_sum(
            [long(part[lines : lines + size, :]) * scale[1] for part, scale in zip(parts, scales)]
        )
    if last:
        sums = 0.0
        for part, scale in zip(parts, scales):
            units = long(part[lines : lines + EXTRA, :])
            sums += (units[:8] + units[8:] * (1.0 / FINE)) * scale[1]
        found = value * reduced[0]
        for other_step, later in enumerate(terms):
            found += later[...] * reduced[other_step + 1]
        tail = jnp.concatenate([sums, -fold(found)], axis=0)
        share = out.shape[0] // n_col
        core = lax.axis_index("col") % 2
        for chip in range(n_col // 2):
            span = slice(chip * share, (chip + 1) * share)
            mine[span, :] = out[pl.ds((2 * chip + core) * share, share), :]
            other[span, :] = out[pl.ds((2 * chip + 1 - core) * share, share), :]
        mine[n_col // 2 * share :, :] = tail
        other[n_col // 2 * share :, :] = tail


def pair_body(mine, received, out):
    lines = mine.shape[0]
    units, code = encode(mine[...] + received[...])
    out[:lines, :] = short(units)
    out[lines:, :] = scale_rows([code])


def split_body(n_chip, mine, received, *outs):
    share = (mine.shape[0] - EXTRA) // n_chip
    chip = lax.axis_index("col") // 2
    tail = mine[n_chip * share :, :] + received[n_chip * share :, :]
    for part, out in enumerate(outs):
        at = pl.ds((chip ^ part) * share, share)
        out[:share, :] = mine[at, :] + received[at, :]
        out[share:, :] = tail


def last_body(
    scales, sizes, parts, term, anchor, adjoint_far, gradients_far, adjoint, gradients, sent
):
    share = adjoint.shape[0]
    total = tree_sum([part[...] for part in parts])
    at = pl.ds(lax.axis_index("col") * share, share)
    adjoint[...] = term[at, :] + sizes[0] * total[:share] + anchor[at, :]
    first = pltpu.make_async_copy(adjoint, adjoint_far, sent.at[0])
    first.start()
    gradients[0] = jnp.sum(total[share + 8 : share + 16]) * scales[0]
    gradients[1] = jnp.sum(total[share : share + 8]) * scales[1]
    second = pltpu.make_async_copy(gradients, gradients_far, sent.at[1])
    second.start()
    first.wait()
    second.wait()


def far(array):
    return pltpu.with_memory_space_constraint(array, pltpu.HBM)


def run(body, out_shape, groups, scratch, name, cost=None, tiles=None):
    flat, specs, widths, aliases = [], [], [], {}
    for spec, value in groups:
        if value is None:
            widths.append(None)
            continue
        many = isinstance(value, (list, tuple))
        widths.append(len(value) if many else 0)
        for array in value if many else [value]:
            if array is tiles:
                aliases[len(flat)] = len(out_shape)
                array = pltpu.with_memory_space_constraint(array, pltpu.VMEM)
            flat.append(array)
            specs.append(spec)

    def kernel(*refs):
        given = list(refs)
        taken = []
        for width in widths:
            if width is None:
                taken.append(None)
            elif width == 0:
                taken.append(given.pop(0))
            else:
                taken.append([given.pop(0) for _ in range(width)])
        body(*taken, *given)

    out_specs = [shape[0] if isinstance(shape, tuple) else VMEM for shape in out_shape]
    shapes = [shape[1] if isinstance(shape, tuple) else shape for shape in out_shape]
    if tiles is not None:
        shapes.append(pltpu.VMEM(tiles.shape, tiles.dtype))
        out_specs.append(VMEM)
    return pl.pallas_call(
        kernel,
        out_shape=shapes,
        in_specs=specs,
        out_specs=out_specs,
        scratch_shapes=scratch,
        input_output_aliases=aliases,
        compiler_params=pltpu.CompilerParams(vmem_limit_bytes=GRANT),
        cost_estimate=cost,
        name=name,
    )(*flat)


def swap(array, axis, stride):
    size = lax.axis_size(axis)
    return lax.ppermute(array, axis, [(i, i ^ stride) for i in range(size)])


def exchange(parts, axis, stride=1):
    size = lax.axis_size(axis) // stride
    return [parts[0]] + [swap(parts[k], axis, k * stride) for k in range(1, size)]


def local(
    tile_data,
    tile_row_block,
    tile_column_block,
    tile_count,
    saved_primal,
    saved_dual,
    primal_mask,
    dual_mask,
    cost_vector,
    demand,
    upper_bound,
    step_sizes,
    primal_cotangent,
    dual_cotangent,
):
    slots, width = tile_data.shape[2], tile_data.shape[-1]
    iterations, row_length = saved_dual.shape
    column_length = saved_primal.shape[1]
    n_row, n_col = lax.axis_size("row"), lax.axis_size("col")
    n_chip = n_col // 2
    lines_y, lines_x = row_length // LANES, column_length // LANES
    share_y, share_x = lines_y // n_col, lines_x // n_row
    saved_lines = iterations * share_x
    last = iterations - 1
    cost = pl.CostEstimate(
        flops=2 * tile_data.size, bytes_accessed=2 * tile_data.size, transcendentals=0
    )

    def lines(array):
        if array.ndim == 1:
            return array.reshape(-1, LANES)
        return array.reshape(iterations, -1, LANES).transpose(1, 0, 2)

    def f32(*shape):
        return jax.ShapeDtypeStruct(shape, jnp.float32)

    def row_part(more):
        return jax.ShapeDtypeStruct((lines_x + more + SCALES, LANES), jnp.int16)

    def scratch(*shape):
        return pltpu.VMEM(shape, jnp.float32)

    mask_x, mask_y = lines(primal_mask), lines(dual_mask)
    full_x, full_y = f32(lines_x, LANES), f32(lines_y, LANES)
    where = [(SMEM, tile_row_block), (SMEM, tile_column_block), (SMEM, tile_count)]
    saved = lines(saved_dual)
    tiles, term_y, anchor_y, *parts = run(
        functools.partial(first_body, last, n_row),
        [pltpu.VMEM((slots, width, width), jnp.bfloat16), full_y, full_y]
        + [row_part(saved_lines)] * n_row,
        [(ANY, far(tile_row_block)), (ANY, far(tile_column_block)), (SMEM, tile_count)]
        + [(ANY, far(tile_data)), (ANY, far(mask_y)), (ANY, far(lines(dual_cotangent)))]
        + [(ANY, far(saved))],
        [
            scratch(iterations + 1, lines_y, LANES),
            scratch(iterations + 1, lines_x, LANES),
            pltpu.SMEM(tile_row_block.shape, jnp.int32),
            pltpu.SMEM(tile_row_block.shape, jnp.int32),
            pltpu.VMEM(mask_y.shape, jnp.int32),
            scratch(lines_y, LANES),
            scratch(*saved.shape),
            pltpu.SemaphoreType.DMA((CHUNKS,)),
            pltpu.SemaphoreType.DMA((5,)),
        ],
        "first",
        cost,
    )
    turned, tiles = run(
        turn_body,
        [pltpu.VMEM(tiles.shape, tiles.dtype)],
        [(VMEM, tiles)],
        [],
        "turn",
        cost,
        tiles,
    )
    adjoint_x, anchor_x = lines(primal_cotangent), None
    terms_x, terms_y = [], [term_y]
    reduced = images = saved_sums = None
    for step in reversed(range(iterations)):
        parts = exchange(parts, "row")
        kind = {0: "last", last: "sums", last - 1: "shares"}.get(step, "plain")
        groups = where + [(SMEM, step_sizes), (VMEM, turned), (VMEM, mask_x), (VMEM, parts)]
        groups += [(VMEM, adjoint_x), (VMEM, anchor_x)]
        body = functools.partial(primal_body, kind, step, n_row, n_col)
        if step == 0:
            break
        outs = [full_x, full_x, full_x, full_y]
        extra = [scratch(lines_x, LANES)]
        if kind == "sums":
            outs.append(f32(saved_lines, LANES))
        if kind == "shares":
            outs += [f32(iterations, lines_x, LANES), f32(iterations, lines_y, LANES)]
            groups += [(VMEM, lines(cost_vector)), (VMEM, lines(upper_bound))]
            groups += [(VMEM, lines(saved_primal))]
            extra = [
                scratch(iterations + 1, lines_x, LANES),
                scratch(iterations + 1, lines_y, LANES),
            ]
        term_x, adjoint_x, anchor_x, partial, *more, turned = run(
            body, outs, groups, extra, f"primal_{step}", cost, turned
        )
        if kind == "sums":
            (saved_sums,) = more
        elif kind == "shares":
            reduced, images = more
            saved_sums = None
        terms_x.insert(0, term_x)
        part = run(
            pair_body,
            [jax.ShapeDtypeStruct((lines_y + SCALES, LANES), jnp.int16)],
            [(VMEM, partial), (VMEM, swap(partial, "col", 1))],
            [],
            f"pair_{step}",
        )[0]
        parts = exchange([part] * n_chip, "col", 2)
        groups = where + [(SMEM, step_sizes), (VMEM, tiles), (VMEM, mask_y), (VMEM, parts)]
        groups += [(VMEM, term_y), (VMEM, anchor_y)]
        if step == 1:
            groups += [(VMEM, lines(demand)), (VMEM, images), (VMEM, list(terms_y))]
            out = row_part(EXTRA)
        else:
            groups += [(VMEM, saved_sums)]
            out = row_part(saved_lines if saved_sums is not None else 0)
        term_y, anchor_y, part, tiles = run(
            functools.partial(dual_body, step - 1, n_col),
            [full_y, full_y, out],
            groups,
            [scratch(lines_y, LANES), scratch(lines_x, LANES)],
            f"dual_{step - 1}",
            cost,
            tiles,
        )
        parts = [part] * n_row
        terms_y.insert(0, term_y)
    half_y = f32(n_chip * share_y + EXTRA, LANES)
    primal_adjoint, mine, other, turned = run(
        body,
        [pltpu.VMEM((lines_x, LANES), jnp.float32), half_y, half_y],
        groups + [(VMEM, reduced), (VMEM, terms_x)],
        [scratch(lines_x, LANES), scratch(lines_y, LANES)],
        "primal_0",
        cost,
        turned,
    )
    received = swap(other, "col", 1)
    parts = run(
        functools.partial(split_body, n_chip),
        [f32(share_y + EXTRA, LANES)] * n_chip,
        [(VMEM, mine), (VMEM, received)],
        [],
        "split",
    )
    parts = exchange(parts, "col", 2)
    scales = (1.0 / math.sqrt(column_length * n_col), 1.0 / math.sqrt(row_length * n_row))
    dual_adjoint, gradients = run(
        functools.partial(last_body, scales),
        [(ANY, f32(share_y, LANES)), (ANY, f32(2))],
        [(SMEM, step_sizes), (VMEM, parts), (VMEM, term_y), (VMEM, anchor_y)],
        [
            scratch(share_y, LANES),
            pltpu.SMEM((2,), jnp.float32),
            pltpu.SemaphoreType.DMA((2,)),
        ],
        "last",
    )
    return (primal_adjoint.reshape(-1), dual_adjoint.reshape(-1), gradients)


def solution(mesh):
    placed = (
        P("row", "col", None, None, None),
        P("row", "col", None),
        P("row", "col", None),
        P("row", "col"),
        P(None, "col"),
        P(None, "row"),
        P(None, "col"),
        P(None, "row"),
        P("col"),
        P("row"),
        P("col"),
        P(),
        P("col"),
        P("row"),
    )
    return jax.shard_map(
        local,
        mesh=mesh,
        in_specs=placed,
        out_specs=(P("col"), P(("row", "col")), P()),
        check_vma=False,
    )
```

```python
import functools
import math

import jax
import jax.numpy as jnp
from jax import lax
from jax.experimental import pallas as pl
from jax.experimental.pallas import tpu as pltpu
from jax.sharding import PartitionSpec as P

LANES = 128
EXTRA = 16
CHUNKS = 4
SCALES = 16
STEPS = 64.0
LIMIT = 32760.0
FINE = 65000.0
LN2 = math.log(2.0)
VMEM = pl.BlockSpec(memory_space=pltpu.VMEM)
SMEM = pl.BlockSpec(memory_space=pltpu.SMEM)
ANY = pl.BlockSpec(memory_space=pl.ANY)
GRANT = 16 * 1024 * 1024


def weight_of(step):
    return (step + 1.0) / (step + 2.0)


def tree_sum(parts):
    while len(parts) > 1:
        parts = [parts[i] + parts[i + 1] for i in range(0, len(parts), 2)]
    return parts[0]


def fold(lines):
    return lines.reshape(-1, 8, LANES).sum(axis=0)


def rounded(values):
    return values.astype(jnp.bfloat16).astype(jnp.float32)


def add_products(in_index, out_index, count, tiles, slots, source, total):
    per_block = tiles.shape[-1] // LANES
    several = len(total.shape) == 3
    live_count = count[0, 0]
    for slot in slots:
        start = in_index[0, 0, slot] * per_block
        place = out_index[0, 0, slot] * per_block
        live = (live_count > slot).astype(jnp.float32)
        halves = []
        for half in range(per_block):
            if not several:
                halves.append(source[pl.ds(start + half, 1), :])
                continue
            vectors = source.shape[0]
            rows = -(-vectors // 8) * 8
            which = lax.broadcasted_iota(jnp.int32, (rows, LANES), 0)
            stacked = jnp.zeros((rows, LANES), jnp.float32)
            for vector in range(vectors):
                line = source[vector, pl.ds(start + half, 1), :]
                stacked = jnp.where(which == vector, line, stacked)
            halves.append(stacked)
        block = (jnp.concatenate(halves, axis=1) * live).astype(jnp.bfloat16)
        product = jnp.dot(block, tiles[slot], preferred_element_type=jnp.float32)
        for half in range(per_block):
            at = pl.ds(place + half, 1)
            lanes = slice(half * LANES, (half + 1) * LANES)
            if several:
                for vector in range(total.shape[0]):
                    total[vector, at, :] += product[vector : vector + 1, lanes]
            else:
                total[at, :] += product[:, lanes]


def whole_scale(lines):
    largest = jnp.maximum(jnp.max(jnp.abs(lines), axis=0, keepdims=True), 1e-30)
    return jnp.floor(jnp.log(largest) * (STEPS / LN2) + 1.0)


def to_units(code):
    return jnp.exp(code * (-LN2 / STEPS)) * LIMIT


def from_units(code):
    return jnp.exp(code * (LN2 / STEPS)) * (1.0 / LIMIT)


def nearest(values):
    return jnp.floor(values + 0.5)


def short(values):
    return values.astype(jnp.int32).astype(jnp.int16)


def long(values):
    return values.astype(jnp.int32).astype(jnp.float32)


def encode(lines):
    code = whole_scale(lines)
    return nearest(lines * to_units(code)), code


def encode_fine(lines):
    code = whole_scale(lines)
    units = lines * to_units(code)
    coarse = nearest(units)
    return coarse, nearest((units - coarse) * FINE), code


def scale_rows(codes):
    which = lax.broadcasted_iota(jnp.int32, (SCALES, LANES), 0)
    rows = jnp.zeros((SCALES, LANES), jnp.float32)
    for spot, code in enumerate(codes):
        rows = jnp.where(which == spot, code, rows)
    return short(rows)


def write_payload(out, lines):
    units, code = encode(lines)
    out[: lines.shape[0], :] = short(units)
    out[lines.shape[0] :, :] = scale_rows([code])


def scales_of(part):
    codes = long(part[part.shape[0] - SCALES :, :])
    return [from_units(codes[spot : spot + 1]) for spot in range(2)]


def first_body(
    step, rows_far, columns_far, count, tile_data, mask_far, cotangent_far, saved_far,
    tiles, term, anchor, *refs
):
    out, saved_out, source, total, rows, columns, mask, cotangent, saved, arrived, ready = refs
    slots = tiles.shape[0]
    chunk = slots // CHUNKS
    pairs = [(mask_far, mask), (cotangent_far, cotangent), (saved_far, saved)]
    pairs += [(rows_far, rows), (columns_far, columns)]
    small = [
        pltpu.make_async_copy(far_ref, near, ready.at[spot])
        for spot, (far_ref, near) in enumerate(pairs)
    ]
    for copy in small:
        copy.start()

    def fetch(part):
        span = pl.ds(part * chunk, chunk)
        return pltpu.make_async_copy(tile_data.at[0, 0, span], tiles.at[span], arrived.at[part])

    for part in range(CHUNKS):
        fetch(part).start(priority=part % 2)
    total[...] = jnp.zeros_like(total)
    for copy in small:
        copy.wait()
    weight = weight_of(step)
    adjoint = cotangent[...]
    anchor[...] = (1.0 - weight) * adjoint
    value = mask[:, step, :].astype(jnp.float32) * weight * adjoint
    term[...] = value
    source[0] = rounded(value)
    iterations = source.shape[0] - 1
    for vector in range(iterations):
        source[vector + 1] = rounded(saved[:, vector, :])
    for part in range(CHUNKS):
        fetch(part).wait()
        span = range(part * chunk, (part + 1) * chunk)
        add_products(rows, columns, count, tiles, span, source, total)
    lines = total.shape[1]
    write_payload(out, total[0])
    saved_out[...] = total[1:].reshape(iterations * lines, LANES)


def turn_body(tiles, turned, _):
    for slot in range(tiles.shape[0]):
        turned[slot] = tiles[slot].T


def dual_body(step, n_col, rows, columns, count, sizes, tiles, mask, parts, before, anchor, *refs):
    last = step == 0
    if last:
        demand, images, terms, term, anchor_out, out, _, source, total = refs
    else:
        term, anchor_out, out, _, source, total = refs
    weight = weight_of(step)
    rows_y = before.shape[0]
    image = tree_sum([long(part[:rows_y, :]) * scales_of(part)[0] for part in parts])
    adjoint = before[...] + sizes[0] * image
    anchor_out[...] = anchor[...] + (1.0 - weight) * adjoint
    value = mask[:, step, :].astype(jnp.float32) * weight * adjoint
    term[...] = value
    source[...] = rounded(value)
    total[...] = jnp.zeros_like(total)
    add_products(rows, columns, count, tiles, range(tiles.shape[0]), source, total)
    lines = total.shape[0]
    units, code = encode(total[...])
    out[:lines, :] = short(units)
    if last:
        share = demand[...] * (1.0 / n_col)
        found = value * (share - images[0])
        for other, earlier in enumerate(terms):
            found += earlier[...] * (share - images[other + 1])
        coarse, fine, found_code = encode_fine(fold(found))
        out[lines : lines + EXTRA, :] = short(jnp.concatenate([coarse, fine], axis=0))
        out[lines + EXTRA :, :] = scale_rows([code, found_code])
    else:
        out[lines:, :] = scale_rows([code])


def primal_body(kind, step, n_row, n_col, rows, columns, count, sizes, tiles, mask, parts, before, anchor, *refs):
    last = kind == "last"
    if last:
        reduced, terms, final, mine, other, _, source, out = refs
    elif kind == "saved":
        gathered, cost, upper, primal, term, adjoint_out, anchor_out, out, reduced, images, _, source, total = refs
    else:
        term, adjoint_out, anchor_out, out, _, source = refs
    sigma = sizes[1]
    weight = weight_of(step)
    lines = mask.shape[0]
    scales = [scales_of(part) for part in parts]
    back = tree_sum([long(part[:lines, :]) * scale[0] for part, scale in zip(parts, scales)])
    adjoint = before[...]
    anchored = (1.0 - weight) * adjoint
    if anchor is not None:
        anchored = anchor[...] + anchored
    value = mask[:, step, :].astype(jnp.float32) * (weight * adjoint - 2.0 * sigma * back)
    after = value + sigma * back
    if last:
        final[...] = after + anchored
    else:
        term[...] = value
        adjoint_out[...] = after
        anchor_out[...] = anchored
    all_slots = range(tiles.shape[0])
    if kind == "saved":
        iterations = reduced.shape[0]
        size = iterations * lines
        for vector in range(iterations):
            at = slice(vector * lines, (vector + 1) * lines)
            sums = [gathered[part, at, :] for part in range(n_row)]
            reduced[vector] = cost[...] - tree_sum(sums)
        source[0] = rounded(value)
        for vector in range(iterations):
            saved = primal[:, vector, :]
            half = jnp.minimum(jnp.maximum(saved - sizes[0] * reduced[vector], 0.0), upper[...])
            source[vector + 1] = rounded(2.0 * half - saved)
        total[...] = jnp.zeros_like(total)
        add_products(columns, rows, count, tiles, all_slots, source, total)
        out[...] = total[0]
        images[...] = total[1:]
        return
    source[...] = rounded(value)
    out[...] = jnp.zeros_like(out)
    add_products(columns, rows, count, tiles, all_slots, source, out)
    if last:
        sums = 0.0
        for part, scale in zip(parts, scales):
            units = long(part[lines : lines + EXTRA, :])
            sums += (units[:8] + units[8:] * (1.0 / FINE)) * scale[1]
        found = value * reduced[0]
        for other_step, later in enumerate(terms):
            found += later[...] * reduced[other_step + 1]
        tail = jnp.concatenate([sums, -fold(found)], axis=0)
        share = out.shape[0] // n_col
        core = lax.axis_index("col") % 2
        for chip in range(n_col // 2):
            span = slice(chip * share, (chip + 1) * share)
            mine[span, :] = out[pl.ds((2 * chip + core) * share, share), :]
            other[span, :] = out[pl.ds((2 * chip + 1 - core) * share, share), :]
        mine[n_col // 2 * share :, :] = tail
        other[n_col // 2 * share :, :] = tail


def pair_body(mine, received, out):
    lines = mine.shape[0]
    units, code = encode(mine[...] + received[...])
    out[:lines, :] = short(units)
    out[lines:, :] = scale_rows([code])


def split_body(n_chip, mine, received, *outs):
    share = (mine.shape[0] - EXTRA) // n_chip
    chip = lax.axis_index("col") // 2
    tail = mine[n_chip * share :, :] + received[n_chip * share :, :]
    for part, out in enumerate(outs):
        at = pl.ds((chip ^ part) * share, share)
        out[:share, :] = mine[at, :] + received[at, :]
        out[share:, :] = tail


def last_body(
    scales, sizes, parts, term, anchor, adjoint_far, gradients_far, adjoint, gradients, sent
):
    share = adjoint.shape[0]
    total = tree_sum([part[...] for part in parts])
    at = pl.ds(lax.axis_index("col") * share, share)
    adjoint[...] = term[at, :] + sizes[0] * total[:share] + anchor[at, :]
    first = pltpu.make_async_copy(adjoint, adjoint_far, sent.at[0])
    first.start()
    gradients[0] = jnp.sum(total[share + 8 : share + 16]) * scales[0]
    gradients[1] = jnp.sum(total[share : share + 8]) * scales[1]
    second = pltpu.make_async_copy(gradients, gradients_far, sent.at[1])
    second.start()
    first.wait()
    second.wait()


def far(array):
    return pltpu.with_memory_space_constraint(array, pltpu.HBM)


def run(body, out_shape, groups, scratch, name, cost=None, tiles=None):
    flat, specs, widths, aliases = [], [], [], {}
    for spec, value in groups:
        if value is None:
            widths.append(None)
            continue
        many = isinstance(value, (list, tuple))
        widths.append(len(value) if many else 0)
        for array in value if many else [value]:
            if array is tiles:
                aliases[len(flat)] = len(out_shape)
                array = pltpu.with_memory_space_constraint(array, pltpu.VMEM)
            flat.append(array)
            specs.append(spec)

    def kernel(*refs):
        given = list(refs)
        taken = []
        for width in widths:
            if width is None:
                taken.append(None)
            elif width == 0:
                taken.append(given.pop(0))
            else:
                taken.append([given.pop(0) for _ in range(width)])
        body(*taken, *given)

    out_specs = [shape[0] if isinstance(shape, tuple) else VMEM for shape in out_shape]
    shapes = [shape[1] if isinstance(shape, tuple) else shape for shape in out_shape]
    if tiles is not None:
        shapes.append(pltpu.VMEM(tiles.shape, tiles.dtype))
        out_specs.append(VMEM)
    return pl.pallas_call(
        kernel,
        out_shape=shapes,
        in_specs=specs,
        out_specs=out_specs,
        scratch_shapes=scratch,
        input_output_aliases=aliases,
        compiler_params=pltpu.CompilerParams(vmem_limit_bytes=GRANT),
        cost_estimate=cost,
        name=name,
    )(*flat)


def swap(array, axis, stride):
    size = lax.axis_size(axis)
    return lax.ppermute(array, axis, [(i, i ^ stride) for i in range(size)])


def exchange(parts, axis, stride=1):
    size = lax.axis_size(axis) // stride
    return [parts[0]] + [swap(parts[k], axis, k * stride) for k in range(1, size)]


def local(
    tile_data,
    tile_row_block,
    tile_column_block,
    tile_count,
    saved_primal,
    saved_dual,
    primal_mask,
    dual_mask,
    cost_vector,
    demand,
    upper_bound,
    step_sizes,
    primal_cotangent,
    dual_cotangent,
):
    slots, width = tile_data.shape[2], tile_data.shape[-1]
    iterations, row_length = saved_dual.shape
    column_length = saved_primal.shape[1]
    n_row, n_col = lax.axis_size("row"), lax.axis_size("col")
    n_chip = n_col // 2
    lines_y, lines_x = row_length // LANES, column_length // LANES
    share_y = lines_y // n_col
    last = iterations - 1
    cost = pl.CostEstimate(
        flops=2 * tile_data.size, bytes_accessed=2 * tile_data.size, transcendentals=0
    )

    def lines(array):
        if array.ndim == 1:
            return array.reshape(-1, LANES)
        return array.reshape(iterations, -1, LANES).transpose(1, 0, 2)

    def f32(*shape):
        return jax.ShapeDtypeStruct(shape, jnp.float32)

    def row_part(more):
        return jax.ShapeDtypeStruct((lines_x + more + SCALES, LANES), jnp.int16)

    def scratch(*shape):
        return pltpu.VMEM(shape, jnp.float32)

    mask_x, mask_y = lines(primal_mask), lines(dual_mask)
    full_x, full_y = f32(lines_x, LANES), f32(lines_y, LANES)
    where = [(SMEM, tile_row_block), (SMEM, tile_column_block), (SMEM, tile_count)]
    saved = lines(saved_dual)
    tiles, term_y, anchor_y, part, saved_part = run(
        functools.partial(first_body, last),
        [pltpu.VMEM((slots, width, width), jnp.bfloat16), full_y, full_y]
        + [row_part(0), scratch(iterations * lines_x, LANES)],
        [(ANY, far(tile_row_block)), (ANY, far(tile_column_block)), (SMEM, tile_count)]
        + [(ANY, far(tile_data)), (ANY, far(mask_y)), (ANY, far(lines(dual_cotangent)))]
        + [(ANY, far(saved))],
        [
            scratch(iterations + 1, lines_y, LANES),
            scratch(iterations + 1, lines_x, LANES),
            pltpu.SMEM(tile_row_block.shape, jnp.int32),
            pltpu.SMEM(tile_row_block.shape, jnp.int32),
            pltpu.VMEM(mask_y.shape, jnp.int32),
            scratch(lines_y, LANES),
            scratch(*saved.shape),
            pltpu.SemaphoreType.DMA((CHUNKS,)),
            pltpu.SemaphoreType.DMA((5,)),
        ],
        "first",
        cost,
    )
    turned, tiles = run(
        turn_body,
        [pltpu.VMEM(tiles.shape, tiles.dtype)],
        [(VMEM, tiles)],
        [],
        "turn",
        cost,
        tiles,
    )
    adjoint_x, anchor_x = lines(primal_cotangent), None
    terms_x, terms_y = [], [term_y]
    parts = [part] * n_row
    gathered = lax.all_gather(saved_part, "row")
    reduced = images = None
    for step in reversed(range(iterations)):
        parts = exchange(parts, "row")
        kind = {0: "last", last - 1: "saved"}.get(step, "plain")
        groups = where + [(SMEM, step_sizes), (VMEM, turned), (VMEM, mask_x), (VMEM, parts)]
        groups += [(VMEM, adjoint_x), (VMEM, anchor_x)]
        body = functools.partial(primal_body, kind, step, n_row, n_col)
        if step == 0:
            break
        outs = [full_x, full_x, full_x, full_y]
        extra = [scratch(lines_x, LANES)]
        if kind == "saved":
            outs += [f32(iterations, lines_x, LANES), f32(iterations, lines_y, LANES)]
            groups += [(VMEM, gathered), (VMEM, lines(cost_vector)), (VMEM, lines(upper_bound))]
            groups += [(VMEM, lines(saved_primal))]
            extra = [
                scratch(iterations + 1, lines_x, LANES),
                scratch(iterations + 1, lines_y, LANES),
            ]
        term_x, adjoint_x, anchor_x, partial, *more, turned = run(
            body, outs, groups, extra, f"primal_{step}", cost, turned
        )
        if kind == "saved":
            reduced, images = more
        terms_x.insert(0, term_x)
        part = run(
            pair_body,
            [jax.ShapeDtypeStruct((lines_y + SCALES, LANES), jnp.int16)],
            [(VMEM, partial), (VMEM, swap(partial, "col", 1))],
            [],
            f"pair_{step}",
        )[0]
        parts = exchange([part] * n_chip, "col", 2)
        groups = where + [(SMEM, step_sizes), (VMEM, tiles), (VMEM, mask_y), (VMEM, parts)]
        groups += [(VMEM, term_y), (VMEM, anchor_y)]
        if step == 1:
            groups += [(VMEM, lines(demand)), (VMEM, images), (VMEM, list(terms_y))]
            out = row_part(EXTRA)
        else:
            out = row_part(0)
        term_y, anchor_y, part, tiles = run(
            functools.partial(dual_body, step - 1, n_col),
            [full_y, full_y, out],
            groups,
            [scratch(lines_y, LANES), scratch(lines_x, LANES)],
            f"dual_{step - 1}",
            cost,
            tiles,
        )
        parts = [part] * n_row
        terms_y.insert(0, term_y)
    half_y = f32(n_chip * share_y + EXTRA, LANES)
    primal_adjoint, mine, other, turned = run(
        body,
        [pltpu.VMEM((lines_x, LANES), jnp.float32), half_y, half_y],
        groups + [(VMEM, reduced), (VMEM, terms_x)],
        [scratch(lines_x, LANES), scratch(lines_y, LANES)],
        "primal_0",
        cost,
        turned,
    )
    received = swap(other, "col", 1)
    parts = run(
        functools.partial(split_body, n_chip),
        [f32(share_y + EXTRA, LANES)] * n_chip,
        [(VMEM, mine), (VMEM, received)],
        [],
        "split",
    )
    parts = exchange(parts, "col", 2)
    scales = (1.0 / math.sqrt(column_length * n_col), 1.0 / math.sqrt(row_length * n_row))
    dual_adjoint, gradients = run(
        functools.partial(last_body, scales),
        [(ANY, f32(share_y, LANES)), (ANY, f32(2))],
        [(SMEM, step_sizes), (VMEM, parts), (VMEM, term_y), (VMEM, anchor_y)],
        [
            scratch(share_y, LANES),
            pltpu.SMEM((2,), jnp.float32),
            pltpu.SemaphoreType.DMA((2,)),
        ],
        "last",
    )
    return (primal_adjoint.reshape(-1), dual_adjoint.reshape(-1), gradients)


def solution(mesh):
    placed = (
        P("row", "col", None, None, None),
        P("row", "col", None),
        P("row", "col", None),
        P("row", "col"),
        P(None, "col"),
        P(None, "row"),
        P(None, "col"),
        P(None, "row"),
        P("col"),
        P("row"),
        P("col"),
        P(),
        P("col"),
        P("row"),
    )
    return jax.shard_map(
        local,
        mesh=mesh,
        in_specs=placed,
        out_specs=(P("col"), P(("row", "col")), P()),
        check_vma=False,
    )
```

```python
import functools
import math

import jax
import jax.numpy as jnp
from jax import lax
from jax.experimental import pallas as pl
from jax.experimental.pallas import tpu as pltpu
from jax.sharding import PartitionSpec as P

LANES = 128
EXTRA = 16
BOUNDS = (0, 5, 11, 16)
SCALES = 16
STEPS = 64.0
LIMIT = 32760.0
FINE = 65000.0
LN2 = math.log(2.0)
VMEM = pl.BlockSpec(memory_space=pltpu.VMEM)
SMEM = pl.BlockSpec(memory_space=pltpu.SMEM)
ANY = pl.BlockSpec(memory_space=pl.ANY)
GRANT = 16 * 1024 * 1024


def weight_of(step):
    return (step + 1.0) / (step + 2.0)


def tree_sum(parts):
    while len(parts) > 1:
        parts = [parts[i] + parts[i + 1] for i in range(0, len(parts), 2)]
    return parts[0]


def fold(lines):
    return lines.reshape(-1, 8, LANES).sum(axis=0)


def rounded(values):
    return values.astype(jnp.bfloat16).astype(jnp.float32)


def add_products(in_index, out_index, count, tiles, slots, source, total):
    per_block = tiles.shape[-1] // LANES
    several = len(total.shape) == 3
    live_count = count[0, 0]
    for slot in slots:
        start = in_index[0, 0, slot] * per_block
        place = out_index[0, 0, slot] * per_block
        live = (live_count > slot).astype(jnp.float32)
        halves = []
        for half in range(per_block):
            if not several:
                halves.append(source[pl.ds(start + half, 1), :])
                continue
            vectors = source.shape[0]
            rows = -(-vectors // 8) * 8
            which = lax.broadcasted_iota(jnp.int32, (rows, LANES), 0)
            stacked = jnp.zeros((rows, LANES), jnp.float32)
            for vector in range(vectors):
                line = source[vector, pl.ds(start + half, 1), :]
                stacked = jnp.where(which == vector, line, stacked)
            halves.append(stacked)
        block = (jnp.concatenate(halves, axis=1) * live).astype(jnp.bfloat16)
        product = jnp.dot(block, tiles[slot], preferred_element_type=jnp.float32)
        for half in range(per_block):
            at = pl.ds(place + half, 1)
            lanes = slice(half * LANES, (half + 1) * LANES)
            if several:
                for vector in range(total.shape[0]):
                    total[vector, at, :] += product[vector : vector + 1, lanes]
            else:
                total[at, :] += product[:, lanes]


def whole_scale(lines):
    largest = jnp.maximum(jnp.max(jnp.abs(lines), axis=0, keepdims=True), 1e-30)
    return jnp.floor(jnp.log(largest) * (STEPS / LN2) + 1.0)


def to_units(code):
    return jnp.exp(code * (-LN2 / STEPS)) * LIMIT


def from_units(code):
    return jnp.exp(code * (LN2 / STEPS)) * (1.0 / LIMIT)


def nearest(values):
    return jnp.floor(values + 0.5)


def short(values):
    return values.astype(jnp.int32).astype(jnp.int16)


def long(values):
    return values.astype(jnp.int32).astype(jnp.float32)


def encode(lines):
    code = whole_scale(lines)
    return nearest(lines * to_units(code)), code


def encode_fine(lines):
    code = whole_scale(lines)
    units = lines * to_units(code)
    coarse = nearest(units)
    return coarse, nearest((units - coarse) * FINE), code


def scale_rows(codes):
    which = lax.broadcasted_iota(jnp.int32, (SCALES, LANES), 0)
    rows = jnp.zeros((SCALES, LANES), jnp.float32)
    for spot, code in enumerate(codes):
        rows = jnp.where(which == spot, code, rows)
    return short(rows)


def scales_of(part):
    codes = long(part[part.shape[0] - SCALES :, :])
    return [from_units(codes[spot : spot + 1]) for spot in range(2)]


def first_body(
    step, n_row, rows_far, columns_far, count, sizes_far, tile_data, mask_far, cotangent_far, saved_far,
    tiles, term, anchor, rows, columns, count_out, sizes, *refs
):
    outs = refs[:n_row]
    source, total, mask, cotangent, saved, arrived, ready = refs[n_row:]
    count_out[0, 0] = count[0, 0]
    slots = tiles.shape[0]
    bounds = [slots * part // 16 for part in BOUNDS]
    pairs = [(mask_far, mask), (cotangent_far, cotangent), (saved_far, saved)]
    pairs += [(rows_far, rows), (columns_far, columns), (sizes_far, sizes)]
    small = [
        pltpu.make_async_copy(far_ref, near, ready.at[spot])
        for spot, (far_ref, near) in enumerate(pairs)
    ]
    for copy in small:
        copy.start()

    def fetch(part):
        span = pl.ds(bounds[part], bounds[part + 1] - bounds[part])
        return pltpu.make_async_copy(tile_data.at[0, 0, span], tiles.at[span], arrived.at[part])

    for part in range(len(BOUNDS) - 1):
        fetch(part).start()
    total[...] = jnp.zeros_like(total)
    for copy in small:
        copy.wait()
    weight = weight_of(step)
    adjoint = cotangent[...]
    anchor[...] = (1.0 - weight) * adjoint
    value = mask[:, step, :].astype(jnp.float32) * weight * adjoint
    term[...] = value
    source[0] = rounded(value)
    iterations = source.shape[0] - 1
    for vector in range(iterations):
        source[vector + 1] = rounded(saved[:, vector, :])
    for part in range(len(BOUNDS) - 1):
        fetch(part).wait()
        span = range(bounds[part], bounds[part + 1])
        add_products(rows, columns, count, tiles, span, source, total)
    lines = total.shape[1]
    share = lines // n_row
    me = lax.axis_index("row")
    units, code = encode(total[0])
    units = short(units)
    for part, out in enumerate(outs):
        at = pl.ds(pl.multiple_of((me ^ part) * share, share), share)
        out[:lines, :] = units
        saved_units, saved_code = encode(total[1:, at, :].reshape(iterations * share, LANES))
        out[lines : lines + iterations * share, :] = short(saved_units)
        out[lines + iterations * share :, :] = scale_rows([code, saved_code])


def turn_body(tiles, turned, _):
    for slot in range(tiles.shape[0]):
        turned[slot] = tiles[slot].T


def dual_body(step, n_col, rows, columns, count, sizes, tiles, mask, parts, before, anchor, *refs):
    last = step == 0
    if last:
        demand, images, terms, term, anchor_out, out, _, source, total = refs
    else:
        saved, term, anchor_out, out, _, source, total = refs
    weight = weight_of(step)
    rows_y = before.shape[0]
    image = tree_sum([long(part[:rows_y, :]) * scales_of(part)[0] for part in parts])
    adjoint = before[...] + sizes[0] * image
    anchor_out[...] = anchor[...] + (1.0 - weight) * adjoint
    value = mask[:, step, :].astype(jnp.float32) * weight * adjoint
    term[...] = value
    source[...] = rounded(value)
    total[...] = jnp.zeros_like(total)
    add_products(rows, columns, count, tiles, range(tiles.shape[0]), source, total)
    lines = total.shape[0]
    units, code = encode(total[...])
    out[:lines, :] = short(units)
    if last:
        share = demand[...] * (1.0 / n_col)
        found = value * (share - images[0])
        for other, earlier in enumerate(terms):
            found += earlier[...] * (share - images[other + 1])
        coarse, fine, found_code = encode_fine(fold(found))
        out[lines : lines + EXTRA, :] = short(jnp.concatenate([coarse, fine], axis=0))
        out[lines + EXTRA :, :] = scale_rows([code, found_code])
    elif saved is None:
        out[lines:, :] = scale_rows([code])
    else:
        size = saved.shape[0]
        saved_units, saved_code = encode(saved[...])
        out[lines : lines + size, :] = short(saved_units)
        out[lines + size :, :] = scale_rows([code, saved_code])


def primal_body(kind, step, n_row, n_col, rows, columns, count, sizes, tiles, mask, parts, before, anchor, *refs):
    last = kind == "last"
    if last:
        reduced, terms, final, mine, other, _, source, out = refs
    elif kind == "sums":
        term, adjoint_out, anchor_out, out, saved, _, source = refs
    elif kind == "shares":
        cost, upper, primal, term, adjoint_out, anchor_out, out, reduced, images, _, source, total = refs
    else:
        term, adjoint_out, anchor_out, out, _, source = refs
    sigma = sizes[1]
    weight = weight_of(step)
    lines = mask.shape[0]
    scales = [scales_of(part) for part in parts]
    back = tree_sum([long(part[:lines, :]) * scale[0] for part, scale in zip(parts, scales)])
    adjoint = before[...]
    anchored = (1.0 - weight) * adjoint
    if anchor is not None:
        anchored = anchor[...] + anchored
    value = mask[:, step, :].astype(jnp.float32) * (weight * adjoint - 2.0 * sigma * back)
    after = value + sigma * back
    if last:
        final[...] = after + anchored
    else:
        term[...] = value
        adjoint_out[...] = after
        anchor_out[...] = anchored
    all_slots = range(tiles.shape[0])
    if kind == "shares":
        iterations = reduced.shape[0]
        share = lines // n_row
        size = iterations * share
        me = lax.axis_index("row")
        for part, (held, scale) in enumerate(zip(parts, scales)):
            at = pl.ds(pl.multiple_of((me ^ part) * share, share), share)
            sums = (long(held[lines : lines + size, :]) * scale[1]).reshape(iterations, share, LANES)
            reduced[:, at, :] = cost[at, :][None] - sums
        source[0] = rounded(value)
        for vector in range(iterations):
            saved = primal[:, vector, :]
            half = jnp.minimum(jnp.maximum(saved - sizes[0] * reduced[vector], 0.0), upper[...])
            source[vector + 1] = rounded(2.0 * half - saved)
        total[...] = jnp.zeros_like(total)
        add_products(columns, rows, count, tiles, all_slots, source, total)
        out[...] = total[0]
        images[...] = total[1:]
        return
    source[...] = rounded(value)
    out[...] = jnp.zeros_like(out)
    add_products(columns, rows, count, tiles, all_slots, source, out)
    if kind == "sums":
        size = saved.shape[0]
        saved[...] = tree_sum(
            [long(part[lines : lines + size, :]) * scale[1] for part, scale in zip(parts, scales)]
        )
    if last:
        sums = 0.0
        for part, scale in zip(parts, scales):
            units = long(part[lines : lines + EXTRA, :])
            sums += (units[:8] + units[8:] * (1.0 / FINE)) * scale[1]
        found = value * reduced[0]
        for other_step, later in enumerate(terms):
            found += later[...] * reduced[other_step + 1]
        tail = jnp.concatenate([sums, -fold(found)], axis=0)
        share = out.shape[0] // n_col
        core = lax.axis_index("col") % 2
        for chip in range(n_col // 2):
            span = slice(chip * share, (chip + 1) * share)
            mine[span, :] = out[pl.ds((2 * chip + core) * share, share), :]
            other[span, :] = out[pl.ds((2 * chip + 1 - core) * share, share), :]
        mine[n_col // 2 * share :, :] = tail
        other[n_col // 2 * share :, :] = tail


def pair_body(mine, received, out):
    lines = mine.shape[0]
    units, code = encode(mine[...] + received[...])
    out[:lines, :] = short(units)
    out[lines:, :] = scale_rows([code])


def split_body(n_chip, mine, received, *outs):
    share = (mine.shape[0] - EXTRA) // n_chip
    chip = lax.axis_index("col") // 2
    tail = mine[n_chip * share :, :] + received[n_chip * share :, :]
    for part, out in enumerate(outs):
        at = pl.ds((chip ^ part) * share, share)
        out[:share, :] = mine[at, :] + received[at, :]
        out[share:, :] = tail


def last_body(
    scales, sizes, parts, term, anchor, adjoint_far, gradients_far, adjoint, gradients, sent
):
    share = adjoint.shape[0]
    total = tree_sum([part[...] for part in parts])
    at = pl.ds(lax.axis_index("col") * share, share)
    adjoint[...] = term[at, :] + sizes[0] * total[:share] + anchor[at, :]
    first = pltpu.make_async_copy(adjoint, adjoint_far, sent.at[0])
    first.start()
    gradients[0] = jnp.sum(total[share + 8 : share + 16]) * scales[0]
    gradients[1] = jnp.sum(total[share : share + 8]) * scales[1]
    second = pltpu.make_async_copy(gradients, gradients_far, sent.at[1])
    second.start()
    first.wait()
    second.wait()


def far(array):
    return pltpu.with_memory_space_constraint(array, pltpu.HBM)


def run(body, out_shape, groups, scratch, name, cost=None, tiles=None):
    flat, specs, widths, aliases = [], [], [], {}
    for spec, value in groups:
        if value is None:
            widths.append(None)
            continue
        many = isinstance(value, (list, tuple))
        widths.append(len(value) if many else 0)
        for array in value if many else [value]:
            if array is tiles:
                aliases[len(flat)] = len(out_shape)
                array = pltpu.with_memory_space_constraint(array, pltpu.VMEM)
            flat.append(array)
            specs.append(spec)

    def kernel(*refs):
        given = list(refs)
        taken = []
        for width in widths:
            if width is None:
                taken.append(None)
            elif width == 0:
                taken.append(given.pop(0))
            else:
                taken.append([given.pop(0) for _ in range(width)])
        body(*taken, *given)

    out_specs = [shape[0] if isinstance(shape, tuple) else VMEM for shape in out_shape]
    shapes = [shape[1] if isinstance(shape, tuple) else shape for shape in out_shape]
    if tiles is not None:
        shapes.append(pltpu.VMEM(tiles.shape, tiles.dtype))
        out_specs.append(VMEM)
    return pl.pallas_call(
        kernel,
        out_shape=shapes,
        in_specs=specs,
        out_specs=out_specs,
        scratch_shapes=scratch,
        input_output_aliases=aliases,
        compiler_params=pltpu.CompilerParams(vmem_limit_bytes=GRANT),
        cost_estimate=cost,
        name=name,
    )(*flat)


def swap(array, axis, stride):
    size = lax.axis_size(axis)
    return lax.ppermute(array, axis, [(i, i ^ stride) for i in range(size)])


def exchange(parts, axis, stride=1):
    size = lax.axis_size(axis) // stride
    return [parts[0]] + [swap(parts[k], axis, k * stride) for k in range(1, size)]


def local(
    tile_data,
    tile_row_block,
    tile_column_block,
    tile_count,
    saved_primal,
    saved_dual,
    primal_mask,
    dual_mask,
    cost_vector,
    demand,
    upper_bound,
    step_sizes,
    primal_cotangent,
    dual_cotangent,
):
    slots, width = tile_data.shape[2], tile_data.shape[-1]
    iterations, row_length = saved_dual.shape
    column_length = saved_primal.shape[1]
    n_row, n_col = lax.axis_size("row"), lax.axis_size("col")
    n_chip = n_col // 2
    lines_y, lines_x = row_length // LANES, column_length // LANES
    share_y, share_x = lines_y // n_col, lines_x // n_row
    saved_lines = iterations * share_x
    last = iterations - 1
    cost = pl.CostEstimate(
        flops=2 * tile_data.size, bytes_accessed=2 * tile_data.size, transcendentals=0
    )

    def lines(array):
        if array.ndim == 1:
            return array.reshape(-1, LANES)
        return array.reshape(iterations, -1, LANES).transpose(1, 0, 2)

    def f32(*shape):
        return jax.ShapeDtypeStruct(shape, jnp.float32)

    def row_part(more):
        return jax.ShapeDtypeStruct((lines_x + more + SCALES, LANES), jnp.int16)

    def scratch(*shape):
        return pltpu.VMEM(shape, jnp.float32)

    mask_x, mask_y = lines(primal_mask), lines(dual_mask)
    full_x, full_y = f32(lines_x, LANES), f32(lines_y, LANES)
    saved = lines(saved_dual)
    index = (SMEM, pltpu.SMEM(tile_row_block.shape, jnp.int32))
    tiles, term_y, anchor_y, *parts = run(
        functools.partial(first_body, last, n_row),
        [pltpu.VMEM((slots, width, width), jnp.bfloat16), full_y, full_y, index, index]
        + [(SMEM, pltpu.SMEM((1, 1), jnp.int32)), (SMEM, pltpu.SMEM((2,), jnp.float32))]
        + [row_part(saved_lines)] * n_row,
        [(ANY, far(tile_row_block)), (ANY, far(tile_column_block)), (SMEM, tile_count)]
        + [(ANY, far(step_sizes)), (ANY, far(tile_data)), (ANY, far(mask_y)), (ANY, far(lines(dual_cotangent)))]
        + [(ANY, far(saved))],
        [
            scratch(iterations + 1, lines_y, LANES),
            scratch(iterations + 1, lines_x, LANES),
            pltpu.VMEM(mask_y.shape, jnp.int32),
            scratch(lines_y, LANES),
            scratch(*saved.shape),
            pltpu.SemaphoreType.DMA((len(BOUNDS) - 1,)),
            pltpu.SemaphoreType.DMA((6,)),
        ],
        "first",
        cost,
    )
    *where, sizes = [
        (SMEM, pltpu.with_memory_space_constraint(held, pltpu.SMEM)) for held in parts[:4]
    ]
    parts = parts[4:]
    turned, tiles = run(
        turn_body,
        [pltpu.VMEM(tiles.shape, tiles.dtype)],
        [(VMEM, tiles)],
        [],
        "turn",
        cost,
        tiles,
    )
    adjoint_x, anchor_x = lines(primal_cotangent), None
    terms_x, terms_y = [], [term_y]
    reduced = images = saved_sums = None
    for step in reversed(range(iterations)):
        parts = exchange(parts, "row")
        kind = {0: "last", last: "sums", last - 1: "shares"}.get(step, "plain")
        groups = where + [sizes, (VMEM, turned), (VMEM, mask_x), (VMEM, parts)]
        groups += [(VMEM, adjoint_x), (VMEM, anchor_x)]
        body = functools.partial(primal_body, kind, step, n_row, n_col)
        if step == 0:
            break
        outs = [full_x, full_x, full_x, full_y]
        extra = [scratch(lines_x, LANES)]
        if kind == "sums":
            outs.append(f32(saved_lines, LANES))
        if kind == "shares":
            outs += [f32(iterations, lines_x, LANES), f32(iterations, lines_y, LANES)]
            groups += [(VMEM, lines(cost_vector)), (VMEM, lines(upper_bound))]
            groups += [(VMEM, lines(saved_primal))]
            extra = [
                scratch(iterations + 1, lines_x, LANES),
                scratch(iterations + 1, lines_y, LANES),
            ]
        term_x, adjoint_x, anchor_x, partial, *more, turned = run(
            body, outs, groups, extra, f"primal_{step}", cost, turned
        )
        if kind == "sums":
            (saved_sums,) = more
        elif kind == "shares":
            reduced, images = more
            saved_sums = None
        terms_x.insert(0, term_x)
        part = run(
            pair_body,
            [jax.ShapeDtypeStruct((lines_y + SCALES, LANES), jnp.int16)],
            [(VMEM, partial), (VMEM, swap(partial, "col", 1))],
            [],
            f"pair_{step}",
        )[0]
        parts = exchange([part] * n_chip, "col", 2)
        groups = where + [sizes, (VMEM, tiles), (VMEM, mask_y), (VMEM, parts)]
        groups += [(VMEM, term_y), (VMEM, anchor_y)]
        if step == 1:
            groups += [(VMEM, lines(demand)), (VMEM, images), (VMEM, list(terms_y))]
            out = row_part(EXTRA)
        else:
            groups += [(VMEM, saved_sums)]
            out = row_part(saved_lines if saved_sums is not None else 0)
        term_y, anchor_y, part, tiles = run(
            functools.partial(dual_body, step - 1, n_col),
            [full_y, full_y, out],
            groups,
            [scratch(lines_y, LANES), scratch(lines_x, LANES)],
            f"dual_{step - 1}",
            cost,
            tiles,
        )
        parts = [part] * n_row
        terms_y.insert(0, term_y)
    half_y = f32(n_chip * share_y + EXTRA, LANES)
    primal_adjoint, mine, other, turned = run(
        body,
        [pltpu.VMEM((lines_x, LANES), jnp.float32), half_y, half_y],
        groups + [(VMEM, reduced), (VMEM, terms_x)],
        [scratch(lines_x, LANES), scratch(lines_y, LANES)],
        "primal_0",
        cost,
        turned,
    )
    received = swap(other, "col", 1)
    parts = run(
        functools.partial(split_body, n_chip),
        [f32(share_y + EXTRA, LANES)] * n_chip,
        [(VMEM, mine), (VMEM, received)],
        [],
        "split",
    )
    parts = exchange(parts, "col", 2)
    scales = (1.0 / math.sqrt(column_length * n_col), 1.0 / math.sqrt(row_length * n_row))
    dual_adjoint, gradients = run(
        functools.partial(last_body, scales),
        [(ANY, f32(share_y, LANES)), (ANY, f32(2))],
        [sizes, (VMEM, parts), (VMEM, term_y), (VMEM, anchor_y)],
        [
            scratch(share_y, LANES),
            pltpu.SMEM((2,), jnp.float32),
            pltpu.SemaphoreType.DMA((2,)),
        ],
        "last",
    )
    return (primal_adjoint.reshape(-1), dual_adjoint.reshape(-1), gradients)


def solution(mesh):
    placed = (
        P("row", "col", None, None, None),
        P("row", "col", None),
        P("row", "col", None),
        P("row", "col"),
        P(None, "col"),
        P(None, "row"),
        P(None, "col"),
        P(None, "row"),
        P("col"),
        P("row"),
        P("col"),
        P(),
        P("col"),
        P("row"),
    )
    return jax.shard_map(
        local,
        mesh=mesh,
        in_specs=placed,
        out_specs=(P("col"), P(("row", "col")), P()),
        check_vma=False,
    )
```

```python
import functools
import math

import jax
import jax.numpy as jnp
from jax import lax
from jax.experimental import pallas as pl
from jax.experimental.pallas import tpu as pltpu
from jax.sharding import PartitionSpec as P

LANES = 128
EXTRA = 16
BOUNDS = (0, 6, 12, 16)
SCALES = 16
STEPS = 64.0
LIMIT = 32760.0
FINE = 65000.0
LN2 = math.log(2.0)
VMEM = pl.BlockSpec(memory_space=pltpu.VMEM)
SMEM = pl.BlockSpec(memory_space=pltpu.SMEM)
ANY = pl.BlockSpec(memory_space=pl.ANY)
GRANT = 16 * 1024 * 1024


def weight_of(step):
    return (step + 1.0) / (step + 2.0)


def tree_sum(parts):
    while len(parts) > 1:
        parts = [parts[i] + parts[i + 1] for i in range(0, len(parts), 2)]
    return parts[0]


def fold(lines):
    return lines.reshape(-1, 8, LANES).sum(axis=0)


def rounded(values):
    return values.astype(jnp.bfloat16).astype(jnp.float32)


def add_products(in_index, out_index, count, tiles, slots, source, total):
    per_block = tiles.shape[-1] // LANES
    several = len(total.shape) == 3
    live_count = count[0, 0]
    for slot in slots:
        start = in_index[0, 0, slot] * per_block
        place = out_index[0, 0, slot] * per_block
        live = (live_count > slot).astype(jnp.float32)
        halves = []
        for half in range(per_block):
            if not several:
                halves.append(source[pl.ds(start + half, 1), :])
                continue
            vectors = source.shape[0]
            rows = -(-vectors // 8) * 8
            which = lax.broadcasted_iota(jnp.int32, (rows, LANES), 0)
            stacked = jnp.zeros((rows, LANES), jnp.float32)
            for vector in range(vectors):
                line = source[vector, pl.ds(start + half, 1), :]
                stacked = jnp.where(which == vector, line, stacked)
            halves.append(stacked)
        block = (jnp.concatenate(halves, axis=1) * live).astype(jnp.bfloat16)
        product = jnp.dot(block, tiles[slot], preferred_element_type=jnp.float32)
        for half in range(per_block):
            at = pl.ds(place + half, 1)
            lanes = slice(half * LANES, (half + 1) * LANES)
            if several:
                for vector in range(total.shape[0]):
                    total[vector, at, :] += product[vector : vector + 1, lanes]
            else:
                total[at, :] += product[:, lanes]


def whole_scale(lines):
    largest = jnp.maximum(jnp.max(jnp.abs(lines), axis=0, keepdims=True), 1e-30)
    return jnp.floor(jnp.log(largest) * (STEPS / LN2) + 1.0)


def to_units(code):
    return jnp.exp(code * (-LN2 / STEPS)) * LIMIT


def from_units(code):
    return jnp.exp(code * (LN2 / STEPS)) * (1.0 / LIMIT)


def nearest(values):
    return jnp.floor(values + 0.5)


def short(values):
    return values.astype(jnp.int32).astype(jnp.int16)


def long(values):
    return values.astype(jnp.int32).astype(jnp.float32)


def encode(lines):
    code = whole_scale(lines)
    return nearest(lines * to_units(code)), code


def encode_fine(lines):
    code = whole_scale(lines)
    units = lines * to_units(code)
    coarse = nearest(units)
    return coarse, nearest((units - coarse) * FINE), code


def scale_rows(codes):
    which = lax.broadcasted_iota(jnp.int32, (SCALES, LANES), 0)
    rows = jnp.zeros((SCALES, LANES), jnp.float32)
    for spot, code in enumerate(codes):
        rows = jnp.where(which == spot, code, rows)
    return short(rows)


def scales_of(part):
    codes = long(part[part.shape[0] - SCALES :, :])
    return [from_units(codes[spot : spot + 1]) for spot in range(2)]


def first_body(
    step, n_row, rows_far, columns_far, count, sizes_far, tile_data, mask_far, cotangent_far, saved_far,
    tiles, term, anchor, rows, columns, count_out, sizes, *refs
):
    outs = refs[:n_row]
    source, total, mask, cotangent, saved, arrived, ready = refs[n_row:]
    count_out[0, 0] = count[0, 0]
    slots = tiles.shape[0]
    bounds = [slots * part // 16 for part in BOUNDS]
    pairs = [(mask_far, mask), (cotangent_far, cotangent), (saved_far, saved)]
    pairs += [(rows_far, rows), (columns_far, columns), (sizes_far, sizes)]
    small = [
        pltpu.make_async_copy(far_ref, near, ready.at[spot])
        for spot, (far_ref, near) in enumerate(pairs)
    ]
    for copy in small:
        copy.start()

    def fetch(part):
        span = pl.ds(bounds[part], bounds[part + 1] - bounds[part])
        return pltpu.make_async_copy(tile_data.at[0, 0, span], tiles.at[span], arrived.at[part])

    for part in range(len(BOUNDS) - 1):
        fetch(part).start()
    total[...] = jnp.zeros_like(total)
    for copy in small:
        copy.wait()
    weight = weight_of(step)
    adjoint = cotangent[...]
    anchor[...] = (1.0 - weight) * adjoint
    value = mask[:, step, :].astype(jnp.float32) * weight * adjoint
    term[...] = value
    source[0] = rounded(value)
    iterations = source.shape[0] - 1
    for vector in range(iterations):
        source[vector + 1] = rounded(saved[:, vector, :])
    for part in range(len(BOUNDS) - 1):
        fetch(part).wait()
        span = range(bounds[part], bounds[part + 1])
        add_products(rows, columns, count, tiles, span, source, total)
    lines = total.shape[1]
    share = lines // n_row
    me = lax.axis_index("row")
    units, code = encode(total[0])
    units = short(units)
    for part, out in enumerate(outs):
        at = pl.ds(pl.multiple_of((me ^ part) * share, share), share)
        out[:lines, :] = units
        saved_units, saved_code = encode(total[1:, at, :].reshape(iterations * share, LANES))
        out[lines : lines + iterations * share, :] = short(saved_units)
        out[lines + iterations * share :, :] = scale_rows([code, saved_code])


def turn_body(tiles, turned, _):
    for slot in range(tiles.shape[0]):
        turned[slot] = tiles[slot].T


def dual_body(step, n_col, rows, columns, count, sizes, tiles, mask, parts, before, anchor, *refs):
    last = step == 0
    if last:
        demand, images, terms, term, anchor_out, out, _, source, total = refs
    else:
        saved, term, anchor_out, out, _, source, total = refs
    weight = weight_of(step)
    rows_y = before.shape[0]
    image = tree_sum([long(part[:rows_y, :]) * scales_of(part)[0] for part in parts])
    adjoint = before[...] + sizes[0] * image
    anchor_out[...] = anchor[...] + (1.0 - weight) * adjoint
    value = mask[:, step, :].astype(jnp.float32) * weight * adjoint
    term[...] = value
    source[...] = rounded(value)
    total[...] = jnp.zeros_like(total)
    add_products(rows, columns, count, tiles, range(tiles.shape[0]), source, total)
    lines = total.shape[0]
    units, code = encode(total[...])
    out[:lines, :] = short(units)
    if last:
        share = demand[...] * (1.0 / n_col)
        found = value * (share - images[0])
        for other, earlier in enumerate(terms):
            found += earlier[...] * (share - images[other + 1])
        coarse, fine, found_code = encode_fine(fold(found))
        out[lines : lines + EXTRA, :] = short(jnp.concatenate([coarse, fine], axis=0))
        out[lines + EXTRA :, :] = scale_rows([code, found_code])
    elif saved is None:
        out[lines:, :] = scale_rows([code])
    else:
        size = saved.shape[0]
        saved_units, saved_code = encode(saved[...])
        out[lines : lines + size, :] = short(saved_units)
        out[lines + size :, :] = scale_rows([code, saved_code])


def primal_body(kind, step, n_row, n_col, rows, columns, count, sizes, tiles, mask, parts, before, anchor, *refs):
    last = kind == "last"
    if last:
        reduced, terms, final, mine, other, _, source, out = refs
    elif kind == "sums":
        term, adjoint_out, anchor_out, out, saved, _, source = refs
    elif kind == "shares":
        cost, upper, primal, term, adjoint_out, anchor_out, out, reduced, images, _, source, total = refs
    else:
        term, adjoint_out, anchor_out, out, _, source = refs
    sigma = sizes[1]
    weight = weight_of(step)
    lines = mask.shape[0]
    scales = [scales_of(part) for part in parts]
    back = tree_sum([long(part[:lines, :]) * scale[0] for part, scale in zip(parts, scales)])
    adjoint = before[...]
    anchored = (1.0 - weight) * adjoint
    if anchor is not None:
        anchored = anchor[...] + anchored
    value = mask[:, step, :].astype(jnp.float32) * (weight * adjoint - 2.0 * sigma * back)
    after = value + sigma * back
    if last:
        final[...] = after + anchored
    else:
        term[...] = value
        adjoint_out[...] = after
        anchor_out[...] = anchored
    all_slots = range(tiles.shape[0])
    if kind == "shares":
        iterations = reduced.shape[0]
        share = lines // n_row
        size = iterations * share
        me = lax.axis_index("row")
        for part, (held, scale) in enumerate(zip(parts, scales)):
            at = pl.ds(pl.multiple_of((me ^ part) * share, share), share)
            sums = (long(held[lines : lines + size, :]) * scale[1]).reshape(iterations, share, LANES)
            reduced[:, at, :] = cost[at, :][None] - sums
        source[0] = rounded(value)
        for vector in range(iterations):
            saved = primal[:, vector, :]
            half = jnp.minimum(jnp.maximum(saved - sizes[0] * reduced[vector], 0.0), upper[...])
            source[vector + 1] = rounded(2.0 * half - saved)
        total[...] = jnp.zeros_like(total)
        add_products(columns, rows, count, tiles, all_slots, source, total)
        out[...] = total[0]
        images[...] = total[1:]
        return
    source[...] = rounded(value)
    out[...] = jnp.zeros_like(out)
    add_products(columns, rows, count, tiles, all_slots, source, out)
    if kind == "sums":
        size = saved.shape[0]
        saved[...] = tree_sum(
            [long(part[lines : lines + size, :]) * scale[1] for part, scale in zip(parts, scales)]
        )
    if last:
        sums = 0.0
        for part, scale in zip(parts, scales):
            units = long(part[lines : lines + EXTRA, :])
            sums += (units[:8] + units[8:] * (1.0 / FINE)) * scale[1]
        found = value * reduced[0]
        for other_step, later in enumerate(terms):
            found += later[...] * reduced[other_step + 1]
        tail = jnp.concatenate([sums, -fold(found)], axis=0)
        share = out.shape[0] // n_col
        core = lax.axis_index("col") % 2
        for chip in range(n_col // 2):
            span = slice(chip * share, (chip + 1) * share)
            mine[span, :] = out[pl.ds((2 * chip + core) * share, share), :]
            other[span, :] = out[pl.ds((2 * chip + 1 - core) * share, share), :]
        mine[n_col // 2 * share :, :] = tail
        other[n_col // 2 * share :, :] = tail


def pair_body(mine, received, out):
    lines = mine.shape[0]
    units, code = encode(mine[...] + received[...])
    out[:lines, :] = short(units)
    out[lines:, :] = scale_rows([code])


def split_body(n_chip, mine, received, *outs):
    share = (mine.shape[0] - EXTRA) // n_chip
    chip = lax.axis_index("col") // 2
    tail = mine[n_chip * share :, :] + received[n_chip * share :, :]
    for part, out in enumerate(outs):
        at = pl.ds((chip ^ part) * share, share)
        out[:share, :] = mine[at, :] + received[at, :]
        out[share:, :] = tail


def last_body(
    scales, sizes, parts, term, anchor, adjoint_far, gradients_far, adjoint, gradients, sent
):
    share = adjoint.shape[0]
    total = tree_sum([part[...] for part in parts])
    at = pl.ds(lax.axis_index("col") * share, share)
    adjoint[...] = term[at, :] + sizes[0] * total[:share] + anchor[at, :]
    first = pltpu.make_async_copy(adjoint, adjoint_far, sent.at[0])
    first.start()
    gradients[0] = jnp.sum(total[share + 8 : share + 16]) * scales[0]
    gradients[1] = jnp.sum(total[share : share + 8]) * scales[1]
    second = pltpu.make_async_copy(gradients, gradients_far, sent.at[1])
    second.start()
    first.wait()
    second.wait()


def far(array):
    return pltpu.with_memory_space_constraint(array, pltpu.HBM)


def run(body, out_shape, groups, scratch, name, cost=None, tiles=None):
    flat, specs, widths, aliases = [], [], [], {}
    for spec, value in groups:
        if value is None:
            widths.append(None)
            continue
        many = isinstance(value, (list, tuple))
        widths.append(len(value) if many else 0)
        for array in value if many else [value]:
            if array is tiles:
                aliases[len(flat)] = len(out_shape)
                array = pltpu.with_memory_space_constraint(array, pltpu.VMEM)
            flat.append(array)
            specs.append(spec)

    def kernel(*refs):
        given = list(refs)
        taken = []
        for width in widths:
            if width is None:
                taken.append(None)
            elif width == 0:
                taken.append(given.pop(0))
            else:
                taken.append([given.pop(0) for _ in range(width)])
        body(*taken, *given)

    out_specs = [shape[0] if isinstance(shape, tuple) else VMEM for shape in out_shape]
    shapes = [shape[1] if isinstance(shape, tuple) else shape for shape in out_shape]
    if tiles is not None:
        shapes.append(pltpu.VMEM(tiles.shape, tiles.dtype))
        out_specs.append(VMEM)
    return pl.pallas_call(
        kernel,
        out_shape=shapes,
        in_specs=specs,
        out_specs=out_specs,
        scratch_shapes=scratch,
        input_output_aliases=aliases,
        compiler_params=pltpu.CompilerParams(vmem_limit_bytes=GRANT),
        cost_estimate=cost,
        name=name,
    )(*flat)


def swap(array, axis, stride):
    size = lax.axis_size(axis)
    return lax.ppermute(array, axis, [(i, i ^ stride) for i in range(size)])


def exchange(parts, axis, stride=1):
    size = lax.axis_size(axis) // stride
    return [parts[0]] + [swap(parts[k], axis, k * stride) for k in range(1, size)]


def local(
    tile_data,
    tile_row_block,
    tile_column_block,
    tile_count,
    saved_primal,
    saved_dual,
    primal_mask,
    dual_mask,
    cost_vector,
    demand,
    upper_bound,
    step_sizes,
    primal_cotangent,
    dual_cotangent,
):
    slots, width = tile_data.shape[2], tile_data.shape[-1]
    iterations, row_length = saved_dual.shape
    column_length = saved_primal.shape[1]
    n_row, n_col = lax.axis_size("row"), lax.axis_size("col")
    n_chip = n_col // 2
    lines_y, lines_x = row_length // LANES, column_length // LANES
    share_y, share_x = lines_y // n_col, lines_x // n_row
    saved_lines = iterations * share_x
    last = iterations - 1
    cost = pl.CostEstimate(
        flops=2 * tile_data.size, bytes_accessed=2 * tile_data.size, transcendentals=0
    )

    def lines(array):
        if array.ndim == 1:
            return array.reshape(-1, LANES)
        return array.reshape(iterations, -1, LANES).transpose(1, 0, 2)

    def f32(*shape):
        return jax.ShapeDtypeStruct(shape, jnp.float32)

    def row_part(more):
        return jax.ShapeDtypeStruct((lines_x + more + SCALES, LANES), jnp.int16)

    def scratch(*shape):
        return pltpu.VMEM(shape, jnp.float32)

    mask_x, mask_y = lines(primal_mask), lines(dual_mask)
    full_x, full_y = f32(lines_x, LANES), f32(lines_y, LANES)
    saved = lines(saved_dual)
    index = (SMEM, pltpu.SMEM(tile_row_block.shape, jnp.int32))
    tiles, term_y, anchor_y, *parts = run(
        functools.partial(first_body, last, n_row),
        [pltpu.VMEM((slots, width, width), jnp.bfloat16), full_y, full_y, index, index]
        + [(SMEM, pltpu.SMEM((1, 1), jnp.int32)), (SMEM, pltpu.SMEM((2,), jnp.float32))]
        + [row_part(saved_lines)] * n_row,
        [(ANY, far(tile_row_block)), (ANY, far(tile_column_block)), (SMEM, tile_count)]
        + [(ANY, far(step_sizes)), (ANY, far(tile_data)), (ANY, far(mask_y)), (ANY, far(lines(dual_cotangent)))]
        + [(ANY, far(saved))],
        [
            scratch(iterations + 1, lines_y, LANES),
            scratch(iterations + 1, lines_x, LANES),
            pltpu.VMEM(mask_y.shape, jnp.int32),
            scratch(lines_y, LANES),
            scratch(*saved.shape),
            pltpu.SemaphoreType.DMA((len(BOUNDS) - 1,)),
            pltpu.SemaphoreType.DMA((6,)),
        ],
        "first",
        cost,
    )
    *where, sizes = [
        (SMEM, pltpu.with_memory_space_constraint(held, pltpu.SMEM)) for held in parts[:4]
    ]
    parts = parts[4:]
    turned, tiles = run(
        turn_body,
        [pltpu.VMEM(tiles.shape, tiles.dtype)],
        [(VMEM, tiles)],
        [],
        "turn",
        cost,
        tiles,
    )
    adjoint_x, anchor_x = lines(primal_cotangent), None
    terms_x, terms_y = [], [term_y]
    reduced = images = saved_sums = None
    for step in reversed(range(iterations)):
        parts = exchange(parts, "row")
        kind = {0: "last", last: "sums", last - 1: "shares"}.get(step, "plain")
        if kind == "sums":
            parts = parts[::-1]
        groups = where + [sizes, (VMEM, turned), (VMEM, mask_x), (VMEM, parts)]
        groups += [(VMEM, adjoint_x), (VMEM, anchor_x)]
        body = functools.partial(primal_body, kind, step, n_row, n_col)
        if step == 0:
            break
        outs = [full_x, full_x, full_x, full_y]
        extra = [scratch(lines_x, LANES)]
        if kind == "sums":
            outs.append(f32(saved_lines, LANES))
        if kind == "shares":
            outs += [f32(iterations, lines_x, LANES), f32(iterations, lines_y, LANES)]
            groups += [(VMEM, lines(cost_vector)), (VMEM, lines(upper_bound))]
            groups += [(VMEM, lines(saved_primal))]
            extra = [
                scratch(iterations + 1, lines_x, LANES),
                scratch(iterations + 1, lines_y, LANES),
            ]
        term_x, adjoint_x, anchor_x, partial, *more, turned = run(
            body, outs, groups, extra, f"primal_{step}", cost, turned
        )
        if kind == "sums":
            (saved_sums,) = more
        elif kind == "shares":
            reduced, images = more
            saved_sums = None
        terms_x.insert(0, term_x)
        part = run(
            pair_body,
            [jax.ShapeDtypeStruct((lines_y + SCALES, LANES), jnp.int16)],
            [(VMEM, partial), (VMEM, swap(partial, "col", 1))],
            [],
            f"pair_{step}",
        )[0]
        parts = exchange([part] * n_chip, "col", 2)
        groups = where + [sizes, (VMEM, tiles), (VMEM, mask_y), (VMEM, parts)]
        groups += [(VMEM, term_y), (VMEM, anchor_y)]
        if step == 1:
            groups += [(VMEM, lines(demand)), (VMEM, images), (VMEM, list(terms_y))]
            out = row_part(EXTRA)
        else:
            groups += [(VMEM, saved_sums)]
            out = row_part(saved_lines if saved_sums is not None else 0)
        term_y, anchor_y, part, tiles = run(
            functools.partial(dual_body, step - 1, n_col),
            [full_y, full_y, out],
            groups,
            [scratch(lines_y, LANES), scratch(lines_x, LANES)],
            f"dual_{step - 1}",
            cost,
            tiles,
        )
        parts = [part] * n_row
        terms_y.insert(0, term_y)
    half_y = f32(n_chip * share_y + EXTRA, LANES)
    primal_adjoint, mine, other, turned = run(
        body,
        [pltpu.VMEM((lines_x, LANES), jnp.float32), half_y, half_y],
        groups + [(VMEM, reduced), (VMEM, terms_x)],
        [scratch(lines_x, LANES), scratch(lines_y, LANES)],
        "primal_0",
        cost,
        turned,
    )
    received = swap(other, "col", 1)
    parts = run(
        functools.partial(split_body, n_chip),
        [f32(share_y + EXTRA, LANES)] * n_chip,
        [(VMEM, mine), (VMEM, received)],
        [],
        "split",
    )
    parts = exchange(parts, "col", 2)
    scales = (1.0 / math.sqrt(column_length * n_col), 1.0 / math.sqrt(row_length * n_row))
    dual_adjoint, gradients = run(
        functools.partial(last_body, scales),
        [(ANY, f32(share_y, LANES)), (ANY, f32(2))],
        [sizes, (VMEM, parts[::-1]), (VMEM, term_y), (VMEM, anchor_y)],
        [
            scratch(share_y, LANES),
            pltpu.SMEM((2,), jnp.float32),
            pltpu.SemaphoreType.DMA((2,)),
        ],
        "last",
    )
    return (primal_adjoint.reshape(-1), dual_adjoint.reshape(-1), gradients)


def solution(mesh):
    placed = (
        P("row", "col", None, None, None),
        P("row", "col", None),
        P("row", "col", None),
        P("row", "col"),
        P(None, "col"),
        P(None, "row"),
        P(None, "col"),
        P(None, "row"),
        P("col"),
        P("row"),
        P("col"),
        P(),
        P("col"),
        P("row"),
    )
    return jax.shard_map(
        local,
        mesh=mesh,
        in_specs=placed,
        out_specs=(P("col"), P(("row", "col")), P()),
        check_vma=False,
    )
```

```python
import functools
import math

import jax
import jax.numpy as jnp
from jax import lax
from jax.experimental import pallas as pl
from jax.experimental.pallas import tpu as pltpu
from jax.sharding import PartitionSpec as P

LANES = 128
EXTRA = 16
BOUNDS = (0, 6, 12, 16)
SCALES = 16
STEPS = 64.0
LIMIT = 32760.0
FINE = 65000.0
LN2 = math.log(2.0)
VMEM = pl.BlockSpec(memory_space=pltpu.VMEM)
SMEM = pl.BlockSpec(memory_space=pltpu.SMEM)
ANY = pl.BlockSpec(memory_space=pl.ANY)
GRANT = 16 * 1024 * 1024


def weight_of(step):
    return (step + 1.0) / (step + 2.0)


def tree_sum(parts):
    while len(parts) > 1:
        parts = [parts[i] + parts[i + 1] for i in range(0, len(parts), 2)]
    return parts[0]


def fold(lines):
    return lines.reshape(-1, 8, LANES).sum(axis=0)


def rounded(values):
    return values.astype(jnp.bfloat16).astype(jnp.float32)


def add_products(in_index, out_index, count, tiles, slots, source, total):
    per_block = tiles.shape[-1] // LANES
    several = len(total.shape) == 3
    live_count = count[0, 0]
    for slot in slots:
        start = in_index[0, 0, slot] * per_block
        place = out_index[0, 0, slot] * per_block
        live = (live_count > slot).astype(jnp.float32)
        halves = []
        for half in range(per_block):
            if not several:
                halves.append(source[pl.ds(start + half, 1), :])
                continue
            vectors = source.shape[0]
            rows = -(-vectors // 8) * 8
            which = lax.broadcasted_iota(jnp.int32, (rows, LANES), 0)
            stacked = jnp.zeros((rows, LANES), jnp.float32)
            for vector in range(vectors):
                line = source[vector, pl.ds(start + half, 1), :]
                stacked = jnp.where(which == vector, line, stacked)
            halves.append(stacked)
        block = (jnp.concatenate(halves, axis=1) * live).astype(jnp.bfloat16)
        product = jnp.dot(block, tiles[slot], preferred_element_type=jnp.float32)
        for half in range(per_block):
            at = pl.ds(place + half, 1)
            lanes = slice(half * LANES, (half + 1) * LANES)
            if several:
                for vector in range(total.shape[0]):
                    total[vector, at, :] += product[vector : vector + 1, lanes]
            else:
                total[at, :] += product[:, lanes]


def whole_scale(lines):
    largest = jnp.maximum(jnp.max(jnp.abs(lines), axis=0, keepdims=True), 1e-30)
    return jnp.floor(jnp.log(largest) * (STEPS / LN2) + 1.0)


def to_units(code):
    return jnp.exp(code * (-LN2 / STEPS)) * LIMIT


def from_units(code):
    return jnp.exp(code * (LN2 / STEPS)) * (1.0 / LIMIT)


def nearest(values):
    return jnp.floor(values + 0.5)


def short(values):
    return values.astype(jnp.int32).astype(jnp.int16)


def long(values):
    return values.astype(jnp.int32).astype(jnp.float32)


def encode(lines):
    code = whole_scale(lines)
    return nearest(lines * to_units(code)), code


def encode_fine(lines):
    code = whole_scale(lines)
    units = lines * to_units(code)
    coarse = nearest(units)
    return coarse, nearest((units - coarse) * FINE), code


def scale_rows(codes):
    which = lax.broadcasted_iota(jnp.int32, (SCALES, LANES), 0)
    rows = jnp.zeros((SCALES, LANES), jnp.float32)
    for spot, code in enumerate(codes):
        rows = jnp.where(which == spot, code, rows)
    return short(rows)


def write_payload(out, lines):
    units, code = encode(lines)
    out[: lines.shape[0], :] = short(units)
    out[lines.shape[0] :, :] = scale_rows([code])


def scales_of(part):
    codes = long(part[part.shape[0] - SCALES :, :])
    return [from_units(codes[spot : spot + 1]) for spot in range(2)]


def first_body(
    step, rows_far, columns_far, count, sizes_far, tile_data, mask_far, cotangent_far,
    tiles, term, anchor, rows, columns, count_out, sizes, out,
    source, total, mask, cotangent, arrived, ready,
):
    count_out[0, 0] = count[0, 0]
    slots = tiles.shape[0]
    bounds = [slots * part // 16 for part in BOUNDS]
    pairs = [(mask_far, mask), (cotangent_far, cotangent)]
    pairs += [(rows_far, rows), (columns_far, columns), (sizes_far, sizes)]
    small = [
        pltpu.make_async_copy(far_ref, near, ready.at[spot])
        for spot, (far_ref, near) in enumerate(pairs)
    ]
    for copy in small:
        copy.start()

    def fetch(part):
        span = pl.ds(bounds[part], bounds[part + 1] - bounds[part])
        return pltpu.make_async_copy(tile_data.at[0, 0, span], tiles.at[span], arrived.at[part])

    for part in range(len(BOUNDS) - 1):
        fetch(part).start()
    total[...] = jnp.zeros_like(total)
    for copy in small:
        copy.wait()
    weight = weight_of(step)
    adjoint = cotangent[...]
    anchor[...] = (1.0 - weight) * adjoint
    value = mask[:, step, :].astype(jnp.float32) * weight * adjoint
    term[...] = value
    source[...] = rounded(value)
    for part in range(len(BOUNDS) - 1):
        fetch(part).wait()
        span = range(bounds[part], bounds[part + 1])
        add_products(rows, columns, count, tiles, span, source, total)
    write_payload(out, total[...])


def saved_back_body(rows, columns, count, tiles, saved, out, _, source, total):
    for vector in range(source.shape[0]):
        source[vector] = rounded(saved[:, vector, :])
    total[...] = jnp.zeros_like(total)
    add_products(rows, columns, count, tiles, range(tiles.shape[0]), source, total)
    write_payload(out, total[...].reshape(-1, LANES))


def saved_image_body(
    rows, columns, count, sizes, tiles, parts, cost, upper, primal, reduced, images, _, source
):
    vectors, lines, _ = reduced.shape
    scales = [scales_of(part)[0] for part in parts]
    for vector in range(vectors):
        at = slice(vector * lines, (vector + 1) * lines)
        sums = tree_sum([long(part[at, :]) * scale for part, scale in zip(parts, scales)])
        reduced[vector] = cost[...] - sums
        saved = primal[:, vector, :]
        half = jnp.minimum(jnp.maximum(saved - sizes[0] * reduced[vector], 0.0), upper[...])
        source[vector] = rounded(2.0 * half - saved)
    images[...] = jnp.zeros_like(images)
    add_products(columns, rows, count, tiles, range(tiles.shape[0]), source, images)


def turn_body(tiles, turned, _):
    for slot in range(tiles.shape[0]):
        turned[slot] = tiles[slot].T


def dual_body(step, n_col, rows, columns, count, sizes, tiles, mask, parts, before, anchor, *refs):
    last = step == 0
    if last:
        demand, images, terms, term, anchor_out, out, _, source, total = refs
    else:
        term, anchor_out, out, _, source, total = refs
    weight = weight_of(step)
    rows_y = before.shape[0]
    image = tree_sum([long(part[:rows_y, :]) * scales_of(part)[0] for part in parts])
    adjoint = before[...] + sizes[0] * image
    anchor_out[...] = anchor[...] + (1.0 - weight) * adjoint
    value = mask[:, step, :].astype(jnp.float32) * weight * adjoint
    term[...] = value
    source[...] = rounded(value)
    total[...] = jnp.zeros_like(total)
    add_products(rows, columns, count, tiles, range(tiles.shape[0]), source, total)
    lines = total.shape[0]
    units, code = encode(total[...])
    out[:lines, :] = short(units)
    if last:
        share = demand[...] * (1.0 / n_col)
        found = value * (share - images[0])
        for other, earlier in enumerate(terms):
            found += earlier[...] * (share - images[other + 1])
        coarse, fine, found_code = encode_fine(fold(found))
        out[lines : lines + EXTRA, :] = short(jnp.concatenate([coarse, fine], axis=0))
        out[lines + EXTRA :, :] = scale_rows([code, found_code])
    else:
        out[lines:, :] = scale_rows([code])


def primal_body(step, n_col, rows, columns, count, sizes, tiles, mask, parts, before, anchor, *refs):
    last = step == 0
    if last:
        reduced, terms, final, mine, other, _, source, out = refs
    else:
        term, adjoint_out, anchor_out, out, _, source = refs
    sigma = sizes[1]
    weight = weight_of(step)
    lines = mask.shape[0]
    scales = [scales_of(part) for part in parts]
    back = tree_sum([long(part[:lines, :]) * scale[0] for part, scale in zip(parts, scales)])
    adjoint = before[...]
    anchored = (1.0 - weight) * adjoint
    if anchor is not None:
        anchored = anchor[...] + anchored
    value = mask[:, step, :].astype(jnp.float32) * (weight * adjoint - 2.0 * sigma * back)
    after = value + sigma * back
    if last:
        final[...] = after + anchored
    else:
        term[...] = value
        adjoint_out[...] = after
        anchor_out[...] = anchored
    all_slots = range(tiles.shape[0])
    source[...] = rounded(value)
    out[...] = jnp.zeros_like(out)
    add_products(columns, rows, count, tiles, all_slots, source, out)
    if last:
        sums = 0.0
        for part, scale in zip(parts, scales):
            units = long(part[lines : lines + EXTRA, :])
            sums += (units[:8] + units[8:] * (1.0 / FINE)) * scale[1]
        found = value * reduced[0]
        for other_step, later in enumerate(terms):
            found += later[...] * reduced[other_step + 1]
        tail = jnp.concatenate([sums, -fold(found)], axis=0)
        share = out.shape[0] // n_col
        core = lax.axis_index("col") % 2
        for chip in range(n_col // 2):
            span = slice(chip * share, (chip + 1) * share)
            mine[span, :] = out[pl.ds((2 * chip + core) * share, share), :]
            other[span, :] = out[pl.ds((2 * chip + 1 - core) * share, share), :]
        mine[n_col // 2 * share :, :] = tail
        other[n_col // 2 * share :, :] = tail


def pair_body(mine, received, out):
    lines = mine.shape[0]
    units, code = encode(mine[...] + received[...])
    out[:lines, :] = short(units)
    out[lines:, :] = scale_rows([code])


def split_body(n_chip, mine, received, *outs):
    share = (mine.shape[0] - EXTRA) // n_chip
    chip = lax.axis_index("col") // 2
    tail = mine[n_chip * share :, :] + received[n_chip * share :, :]
    for part, out in enumerate(outs):
        at = pl.ds((chip ^ part) * share, share)
        out[:share, :] = mine[at, :] + received[at, :]
        out[share:, :] = tail


def last_body(
    scales, sizes, parts, term, anchor, adjoint_far, gradients_far, adjoint, gradients, sent
):
    share = adjoint.shape[0]
    total = tree_sum([part[...] for part in parts])
    at = pl.ds(lax.axis_index("col") * share, share)
    adjoint[...] = term[at, :] + sizes[0] * total[:share] + anchor[at, :]
    first = pltpu.make_async_copy(adjoint, adjoint_far, sent.at[0])
    first.start()
    gradients[0] = jnp.sum(total[share + 8 : share + 16]) * scales[0]
    gradients[1] = jnp.sum(total[share : share + 8]) * scales[1]
    second = pltpu.make_async_copy(gradients, gradients_far, sent.at[1])
    second.start()
    first.wait()
    second.wait()


def far(array):
    return pltpu.with_memory_space_constraint(array, pltpu.HBM)


def run(body, out_shape, groups, scratch, name, cost=None, tiles=None):
    flat, specs, widths, aliases = [], [], [], {}
    for spec, value in groups:
        if value is None:
            widths.append(None)
            continue
        many = isinstance(value, (list, tuple))
        widths.append(len(value) if many else 0)
        for array in value if many else [value]:
            if array is tiles:
                aliases[len(flat)] = len(out_shape)
                array = pltpu.with_memory_space_constraint(array, pltpu.VMEM)
            flat.append(array)
            specs.append(spec)

    def kernel(*refs):
        given = list(refs)
        taken = []
        for width in widths:
            if width is None:
                taken.append(None)
            elif width == 0:
                taken.append(given.pop(0))
            else:
                taken.append([given.pop(0) for _ in range(width)])
        body(*taken, *given)

    out_specs = [shape[0] if isinstance(shape, tuple) else VMEM for shape in out_shape]
    shapes = [shape[1] if isinstance(shape, tuple) else shape for shape in out_shape]
    if tiles is not None:
        shapes.append(pltpu.VMEM(tiles.shape, tiles.dtype))
        out_specs.append(VMEM)
    return pl.pallas_call(
        kernel,
        out_shape=shapes,
        in_specs=specs,
        out_specs=out_specs,
        scratch_shapes=scratch,
        input_output_aliases=aliases,
        compiler_params=pltpu.CompilerParams(vmem_limit_bytes=GRANT),
        cost_estimate=cost,
        name=name,
    )(*flat)


def swap(array, axis, stride):
    size = lax.axis_size(axis)
    return lax.ppermute(array, axis, [(i, i ^ stride) for i in range(size)])


def exchange(parts, axis, stride=1):
    size = lax.axis_size(axis) // stride
    return [parts[0]] + [swap(parts[k], axis, k * stride) for k in range(1, size)]


def local(
    tile_data,
    tile_row_block,
    tile_column_block,
    tile_count,
    saved_primal,
    saved_dual,
    primal_mask,
    dual_mask,
    cost_vector,
    demand,
    upper_bound,
    step_sizes,
    primal_cotangent,
    dual_cotangent,
):
    slots, width = tile_data.shape[2], tile_data.shape[-1]
    iterations, row_length = saved_dual.shape
    column_length = saved_primal.shape[1]
    n_row, n_col = lax.axis_size("row"), lax.axis_size("col")
    n_chip = n_col // 2
    lines_y, lines_x = row_length // LANES, column_length // LANES
    share_y = lines_y // n_col
    last = iterations - 1
    cost = pl.CostEstimate(
        flops=2 * tile_data.size, bytes_accessed=2 * tile_data.size, transcendentals=0
    )

    def lines(array):
        if array.ndim == 1:
            return array.reshape(-1, LANES)
        return array.reshape(iterations, -1, LANES).transpose(1, 0, 2)

    def f32(*shape):
        return jax.ShapeDtypeStruct(shape, jnp.float32)

    def row_part(more):
        return jax.ShapeDtypeStruct((lines_x + more + SCALES, LANES), jnp.int16)

    def scratch(*shape):
        return pltpu.VMEM(shape, jnp.float32)

    mask_x, mask_y = lines(primal_mask), lines(dual_mask)
    full_x, full_y = f32(lines_x, LANES), f32(lines_y, LANES)
    index = (SMEM, pltpu.SMEM(tile_row_block.shape, jnp.int32))
    tiles, term_y, anchor_y, *held, part = run(
        functools.partial(first_body, last),
        [pltpu.VMEM((slots, width, width), jnp.bfloat16), full_y, full_y, index, index]
        + [(SMEM, pltpu.SMEM((1, 1), jnp.int32)), (SMEM, pltpu.SMEM((2,), jnp.float32))]
        + [row_part(0)],
        [(ANY, far(tile_row_block)), (ANY, far(tile_column_block)), (SMEM, tile_count)]
        + [(ANY, far(step_sizes)), (ANY, far(tile_data))]
        + [(ANY, far(mask_y)), (ANY, far(lines(dual_cotangent)))],
        [
            scratch(lines_y, LANES),
            scratch(lines_x, LANES),
            pltpu.VMEM(mask_y.shape, jnp.int32),
            scratch(lines_y, LANES),
            pltpu.SemaphoreType.DMA((len(BOUNDS) - 1,)),
            pltpu.SemaphoreType.DMA((5,)),
        ],
        "first",
        cost,
    )
    *where, sizes = [
        (SMEM, pltpu.with_memory_space_constraint(array, pltpu.SMEM)) for array in held
    ]
    saved_part, tiles = run(
        saved_back_body,
        [row_part((iterations - 1) * lines_x)],
        where + [(VMEM, tiles), (VMEM, lines(saved_dual))],
        [scratch(iterations, lines_y, LANES), scratch(iterations, lines_x, LANES)],
        "saved_back",
        cost,
        tiles,
    )
    turned, tiles = run(
        turn_body,
        [pltpu.VMEM(tiles.shape, tiles.dtype)],
        [(VMEM, tiles)],
        [],
        "turn",
        cost,
        tiles,
    )
    saved_parts = [saved_part] + [None] * (n_row - 1)
    adjoint_x, anchor_x = lines(primal_cotangent), None
    terms_x, terms_y = [], [term_y]
    parts = [part] * n_row
    reduced = images = None
    pending = list(range(n_row - 1, 0, -1))

    def send_saved(parts, count):
        for _ in range(count):
            parts[-1], own = lax.optimization_barrier((parts[-1], saved_part))
            offset = pending.pop(0)
            saved_parts[offset] = swap(own, "row", offset)

    for step in reversed(range(iterations)):
        parts = exchange(parts, "row")
        if step < last:
            send_saved(parts, len(pending))
        groups = where + [sizes, (VMEM, turned), (VMEM, mask_x), (VMEM, parts[::-1])]
        groups += [(VMEM, adjoint_x), (VMEM, anchor_x)]
        body = functools.partial(primal_body, step, n_col)
        if step == 0:
            break
        term_x, adjoint_x, anchor_x, partial, turned = run(
            body,
            [full_x, full_x, full_x, full_y],
            groups,
            [scratch(lines_x, LANES)],
            f"primal_{step}",
            cost,
            turned,
        )
        terms_x.insert(0, term_x)
        part = run(
            pair_body,
            [jax.ShapeDtypeStruct((lines_y + SCALES, LANES), jnp.int16)],
            [(VMEM, partial), (VMEM, swap(partial, "col", 1))],
            [],
            f"pair_{step}",
        )[0]
        parts = exchange([part] * n_chip, "col", 2)
        if step == last:
            send_saved(parts, 1 + len(pending) // 3)
        if step == 1:
            reduced, images, turned = run(
                saved_image_body,
                [f32(iterations, lines_x, LANES), f32(iterations, lines_y, LANES)],
                where
                + [sizes, (VMEM, turned), (VMEM, saved_parts)]
                + [(VMEM, lines(cost_vector)), (VMEM, lines(upper_bound))]
                + [(VMEM, lines(saved_primal))],
                [scratch(iterations, lines_x, LANES)],
                "saved_image",
                cost,
                turned,
            )
        groups = where + [sizes, (VMEM, tiles), (VMEM, mask_y), (VMEM, parts[::-1])]
        groups += [(VMEM, term_y), (VMEM, anchor_y)]
        if step == 1:
            groups += [(VMEM, lines(demand)), (VMEM, images), (VMEM, list(terms_y))]
            out = row_part(EXTRA)
        else:
            out = row_part(0)
        term_y, anchor_y, part, tiles = run(
            functools.partial(dual_body, step - 1, n_col),
            [full_y, full_y, out],
            groups,
            [scratch(lines_y, LANES), scratch(lines_x, LANES)],
            f"dual_{step - 1}",
            cost,
            tiles,
        )
        parts = [part] * n_row
        terms_y.insert(0, term_y)
    half_y = f32(n_chip * share_y + EXTRA, LANES)
    primal_adjoint, mine, other, turned = run(
        body,
        [pltpu.VMEM((lines_x, LANES), jnp.float32), half_y, half_y],
        groups + [(VMEM, reduced), (VMEM, terms_x)],
        [scratch(lines_x, LANES), scratch(lines_y, LANES)],
        "primal_0",
        cost,
        turned,
    )
    received = swap(other, "col", 1)
    parts = run(
        functools.partial(split_body, n_chip),
        [f32(share_y + EXTRA, LANES)] * n_chip,
        [(VMEM, mine), (VMEM, received)],
        [],
        "split",
    )
    parts = exchange(parts, "col", 2)
    scales = (1.0 / math.sqrt(column_length * n_col), 1.0 / math.sqrt(row_length * n_row))
    dual_adjoint, gradients = run(
        functools.partial(last_body, scales),
        [(ANY, f32(share_y, LANES)), (ANY, f32(2))],
        [sizes, (VMEM, parts[::-1]), (VMEM, term_y), (VMEM, anchor_y)],
        [
            scratch(share_y, LANES),
            pltpu.SMEM((2,), jnp.float32),
            pltpu.SemaphoreType.DMA((2,)),
        ],
        "last",
    )
    return (primal_adjoint.reshape(-1), dual_adjoint.reshape(-1), gradients)


def solution(mesh):
    placed = (
        P("row", "col", None, None, None),
        P("row", "col", None),
        P("row", "col", None),
        P("row", "col"),
        P(None, "col"),
        P(None, "row"),
        P(None, "col"),
        P(None, "row"),
        P("col"),
        P("row"),
        P("col"),
        P(),
        P("col"),
        P("row"),
    )
    return jax.shard_map(
        local,
        mesh=mesh,
        in_specs=placed,
        out_specs=(P("col"), P(("row", "col")), P()),
        check_vma=False,
    )
```

```python
import functools
import math

import jax
import jax.numpy as jnp
from jax import lax
from jax.experimental import pallas as pl
from jax.experimental.pallas import tpu as pltpu
from jax.sharding import PartitionSpec as P

LANES = 128
EXTRA = 16
BOUNDS = (0, 6, 12, 16)
SCALES = 16
STEPS = 64.0
LIMIT = 32760.0
FINE = 65000.0
LN2 = math.log(2.0)
VMEM = pl.BlockSpec(memory_space=pltpu.VMEM)
SMEM = pl.BlockSpec(memory_space=pltpu.SMEM)
ANY = pl.BlockSpec(memory_space=pl.ANY)
GRANT = 16 * 1024 * 1024


def weight_of(step):
    return (step + 1.0) / (step + 2.0)


def tree_sum(parts):
    while len(parts) > 1:
        parts = [parts[i] + parts[i + 1] for i in range(0, len(parts), 2)]
    return parts[0]


def fold(lines):
    return lines.reshape(-1, 8, LANES).sum(axis=0)


def rounded(values):
    return values.astype(jnp.bfloat16).astype(jnp.float32)


def add_products(in_index, out_index, count, tiles, slots, source, total):
    per_block = tiles.shape[-1] // LANES
    several = len(total.shape) == 3
    live_count = count[0, 0]
    for slot in slots:
        start = in_index[0, 0, slot] * per_block
        place = out_index[0, 0, slot] * per_block
        live = (live_count > slot).astype(jnp.float32)
        halves = []
        for half in range(per_block):
            if not several:
                halves.append(source[pl.ds(start + half, 1), :])
                continue
            vectors = source.shape[0]
            rows = -(-vectors // 8) * 8
            which = lax.broadcasted_iota(jnp.int32, (rows, LANES), 0)
            stacked = jnp.zeros((rows, LANES), jnp.float32)
            for vector in range(vectors):
                line = source[vector, pl.ds(start + half, 1), :]
                stacked = jnp.where(which == vector, line, stacked)
            halves.append(stacked)
        block = (jnp.concatenate(halves, axis=1) * live).astype(jnp.bfloat16)
        product = jnp.dot(block, tiles[slot], preferred_element_type=jnp.float32)
        for half in range(per_block):
            at = pl.ds(place + half, 1)
            lanes = slice(half * LANES, (half + 1) * LANES)
            if several:
                for vector in range(total.shape[0]):
                    total[vector, at, :] += product[vector : vector + 1, lanes]
            else:
                total[at, :] += product[:, lanes]


def whole_scale(lines):
    largest = jnp.maximum(jnp.max(jnp.abs(lines), axis=0, keepdims=True), 1e-30)
    return jnp.floor(jnp.log(largest) * (STEPS / LN2) + 1.0)


def to_units(code):
    return jnp.exp(code * (-LN2 / STEPS)) * LIMIT


def from_units(code):
    return jnp.exp(code * (LN2 / STEPS)) * (1.0 / LIMIT)


def nearest(values):
    return jnp.floor(values + 0.5)


def short(values):
    return values.astype(jnp.int32).astype(jnp.int16)


def long(values):
    return values.astype(jnp.int32).astype(jnp.float32)


def encode(lines):
    code = whole_scale(lines)
    return nearest(lines * to_units(code)), code


def encode_fine(lines):
    code = whole_scale(lines)
    units = lines * to_units(code)
    coarse = nearest(units)
    return coarse, nearest((units - coarse) * FINE), code


def scale_rows(codes):
    which = lax.broadcasted_iota(jnp.int32, (SCALES, LANES), 0)
    rows = jnp.zeros((SCALES, LANES), jnp.float32)
    for spot, code in enumerate(codes):
        rows = jnp.where(which == spot, code, rows)
    return short(rows)


def write_payload(out, lines):
    units, code = encode(lines)
    out[: lines.shape[0], :] = short(units)
    out[lines.shape[0] :, :] = scale_rows([code])


def scales_of(part):
    codes = long(part[part.shape[0] - SCALES :, :])
    return [from_units(codes[spot : spot + 1]) for spot in range(2)]


def first_body(
    step, rows_far, columns_far, count, sizes_far, tile_data, mask_far, cotangent_far,
    tiles, term, anchor, rows, columns, count_out, sizes, out,
    source, total, mask, cotangent, arrived, ready,
):
    count_out[0, 0] = count[0, 0]
    slots = tiles.shape[0]
    bounds = [slots * part // 16 for part in BOUNDS]
    pairs = [(mask_far, mask), (cotangent_far, cotangent)]
    pairs += [(rows_far, rows), (columns_far, columns), (sizes_far, sizes)]
    small = [
        pltpu.make_async_copy(far_ref, near, ready.at[spot])
        for spot, (far_ref, near) in enumerate(pairs)
    ]
    for copy in small:
        copy.start()

    def fetch(part):
        span = pl.ds(bounds[part], bounds[part + 1] - bounds[part])
        return pltpu.make_async_copy(tile_data.at[0, 0, span], tiles.at[span], arrived.at[part])

    for part in range(len(BOUNDS) - 1):
        fetch(part).start()
    total[...] = jnp.zeros_like(total)
    for copy in small:
        copy.wait()
    weight = weight_of(step)
    adjoint = cotangent[...]
    anchor[...] = (1.0 - weight) * adjoint
    value = mask[:, step, :].astype(jnp.float32) * weight * adjoint
    term[...] = value
    source[...] = rounded(value)
    for part in range(len(BOUNDS) - 1):
        fetch(part).wait()
        span = range(bounds[part], bounds[part + 1])
        add_products(rows, columns, count, tiles, span, source, total)
    write_payload(out, total[...])


def saved_back_body(rows, columns, count, tiles, saved, out, _, source, total):
    for vector in range(source.shape[0]):
        source[vector] = rounded(saved[:, vector, :])
    total[...] = jnp.zeros_like(total)
    add_products(rows, columns, count, tiles, range(tiles.shape[0]), source, total)
    write_payload(out, total[...].reshape(-1, LANES))


def saved_image_body(
    rows, columns, count, sizes, tiles, parts, cost, upper, primal, reduced, images, _, source
):
    vectors, lines, _ = reduced.shape
    scales = [scales_of(part)[0] for part in parts]
    for vector in range(vectors):
        at = slice(vector * lines, (vector + 1) * lines)
        sums = tree_sum([long(part[at, :]) * scale for part, scale in zip(parts, scales)])
        reduced[vector] = cost[...] - sums
        saved = primal[:, vector, :]
        half = jnp.minimum(jnp.maximum(saved - sizes[0] * reduced[vector], 0.0), upper[...])
        source[vector] = rounded(2.0 * half - saved)
    images[...] = jnp.zeros_like(images)
    add_products(columns, rows, count, tiles, range(tiles.shape[0]), source, images)


def turn_body(tiles, turned, _):
    for slot in range(tiles.shape[0]):
        turned[slot] = tiles[slot].T


def dual_body(step, n_col, rows, columns, count, sizes, tiles, mask, parts, before, anchor, *refs):
    last = step == 0
    if last:
        demand, images, terms, term, anchor_out, out, _, source, total = refs
    else:
        term, anchor_out, out, _, source, total = refs
    weight = weight_of(step)
    rows_y = before.shape[0]
    image = tree_sum([long(part[:rows_y, :]) * scales_of(part)[0] for part in parts])
    adjoint = before[...] + sizes[0] * image
    anchor_out[...] = anchor[...] + (1.0 - weight) * adjoint
    value = mask[:, step, :].astype(jnp.float32) * weight * adjoint
    term[...] = value
    source[...] = rounded(value)
    total[...] = jnp.zeros_like(total)
    add_products(rows, columns, count, tiles, range(tiles.shape[0]), source, total)
    lines = total.shape[0]
    units, code = encode(total[...])
    out[:lines, :] = short(units)
    if last:
        share = demand[...] * (1.0 / n_col)
        found = value * (share - images[0])
        for other, earlier in enumerate(terms):
            found += earlier[...] * (share - images[other + 1])
        coarse, fine, found_code = encode_fine(fold(found))
        out[lines : lines + EXTRA, :] = short(jnp.concatenate([coarse, fine], axis=0))
        out[lines + EXTRA :, :] = scale_rows([code, found_code])
    else:
        out[lines:, :] = scale_rows([code])


def primal_body(step, n_col, rows, columns, count, sizes, tiles, mask, parts, before, anchor, *refs):
    last = step == 0
    if last:
        reduced, terms, final, mine, other, _, source, out = refs
    else:
        term, adjoint_out, anchor_out, out, _, source = refs
    sigma = sizes[1]
    weight = weight_of(step)
    lines = mask.shape[0]
    scales = [scales_of(part) for part in parts]
    back = tree_sum([long(part[:lines, :]) * scale[0] for part, scale in zip(parts, scales)])
    adjoint = before[...]
    anchored = (1.0 - weight) * adjoint
    if anchor is not None:
        anchored = anchor[...] + anchored
    value = mask[:, step, :].astype(jnp.float32) * (weight * adjoint - 2.0 * sigma * back)
    after = value + sigma * back
    if last:
        final[...] = after + anchored
    else:
        term[...] = value
        adjoint_out[...] = after
        anchor_out[...] = anchored
    all_slots = range(tiles.shape[0])
    source[...] = rounded(value)
    out[...] = jnp.zeros_like(out)
    add_products(columns, rows, count, tiles, all_slots, source, out)
    if last:
        sums = 0.0
        for part, scale in zip(parts, scales):
            units = long(part[lines : lines + EXTRA, :])
            sums += (units[:8] + units[8:] * (1.0 / FINE)) * scale[1]
        found = value * reduced[0]
        for other_step, later in enumerate(terms):
            found += later[...] * reduced[other_step + 1]
        tail = jnp.concatenate([sums, -fold(found)], axis=0)
        share = out.shape[0] // n_col
        core = lax.axis_index("col") % 2
        for chip in range(n_col // 2):
            span = slice(chip * share, (chip + 1) * share)
            mine[span, :] = out[pl.ds((2 * chip + core) * share, share), :]
            other[span, :] = out[pl.ds((2 * chip + 1 - core) * share, share), :]
        mine[n_col // 2 * share :, :] = tail
        other[n_col // 2 * share :, :] = tail


def pair_body(mine, received, out):
    lines = mine.shape[0]
    units, code = encode(mine[...] + received[...])
    out[:lines, :] = short(units)
    out[lines:, :] = scale_rows([code])


def split_body(n_chip, mine, received, *outs):
    share = (mine.shape[0] - EXTRA) // n_chip
    chip = lax.axis_index("col") // 2
    tail = mine[n_chip * share :, :] + received[n_chip * share :, :]
    for part, out in enumerate(outs):
        at = pl.ds((chip ^ part) * share, share)
        out[:share, :] = mine[at, :] + received[at, :]
        out[share:, :] = tail


def last_body(
    scales, sizes, parts, term, anchor, adjoint_far, gradients_far, adjoint, gradients, sent
):
    share = adjoint.shape[0]
    total = tree_sum([part[...] for part in parts])
    at = pl.ds(lax.axis_index("col") * share, share)
    adjoint[...] = term[at, :] + sizes[0] * total[:share] + anchor[at, :]
    first = pltpu.make_async_copy(adjoint, adjoint_far, sent.at[0])
    first.start()
    gradients[0] = jnp.sum(total[share + 8 : share + 16]) * scales[0]
    gradients[1] = jnp.sum(total[share : share + 8]) * scales[1]
    second = pltpu.make_async_copy(gradients, gradients_far, sent.at[1])
    second.start()
    first.wait()
    second.wait()


def far(array):
    return pltpu.with_memory_space_constraint(array, pltpu.HBM)


def run(body, out_shape, groups, scratch, name, cost=None, tiles=None, handed=None):
    flat, specs, widths, aliases = [], [], [], {}
    for spec, value in groups:
        if value is None:
            widths.append(None)
            continue
        many = isinstance(value, (list, tuple))
        widths.append(len(value) if many else 0)
        for array in value if many else [value]:
            if array is handed:
                aliases[len(flat)] = 0
            if array is tiles:
                aliases[len(flat)] = len(out_shape)
                array = pltpu.with_memory_space_constraint(array, pltpu.VMEM)
            flat.append(array)
            specs.append(spec)

    def kernel(*refs):
        given = list(refs)
        taken = []
        for width in widths:
            if width is None:
                taken.append(None)
            elif width == 0:
                taken.append(given.pop(0))
            else:
                taken.append([given.pop(0) for _ in range(width)])
        body(*taken, *given)

    out_specs = [shape[0] if isinstance(shape, tuple) else VMEM for shape in out_shape]
    shapes = [shape[1] if isinstance(shape, tuple) else shape for shape in out_shape]
    if tiles is not None:
        shapes.append(pltpu.VMEM(tiles.shape, tiles.dtype))
        out_specs.append(VMEM)
    return pl.pallas_call(
        kernel,
        out_shape=shapes,
        in_specs=specs,
        out_specs=out_specs,
        scratch_shapes=scratch,
        input_output_aliases=aliases,
        compiler_params=pltpu.CompilerParams(vmem_limit_bytes=GRANT),
        cost_estimate=cost,
        name=name,
    )(*flat)


def swap(array, axis, stride):
    size = lax.axis_size(axis)
    return lax.ppermute(array, axis, [(i, i ^ stride) for i in range(size)])


def exchange(parts, axis, stride=1):
    size = lax.axis_size(axis) // stride
    return [parts[0]] + [swap(parts[k], axis, k * stride) for k in range(1, size)]


def local(
    tile_data,
    tile_row_block,
    tile_column_block,
    tile_count,
    saved_primal,
    saved_dual,
    primal_mask,
    dual_mask,
    cost_vector,
    demand,
    upper_bound,
    step_sizes,
    primal_cotangent,
    dual_cotangent,
):
    slots, width = tile_data.shape[2], tile_data.shape[-1]
    iterations, row_length = saved_dual.shape
    column_length = saved_primal.shape[1]
    n_row, n_col = lax.axis_size("row"), lax.axis_size("col")
    n_chip = n_col // 2
    lines_y, lines_x = row_length // LANES, column_length // LANES
    share_y = lines_y // n_col
    last = iterations - 1
    cost = pl.CostEstimate(
        flops=2 * tile_data.size, bytes_accessed=2 * tile_data.size, transcendentals=0
    )

    def lines(array):
        if array.ndim == 1:
            return array.reshape(-1, LANES)
        return array.reshape(iterations, -1, LANES).transpose(1, 0, 2)

    def f32(*shape):
        return jax.ShapeDtypeStruct(shape, jnp.float32)

    def row_part(more):
        return jax.ShapeDtypeStruct((lines_x + more + SCALES, LANES), jnp.int16)

    def scratch(*shape):
        return pltpu.VMEM(shape, jnp.float32)

    mask_x, mask_y = lines(primal_mask), lines(dual_mask)
    full_x, full_y = f32(lines_x, LANES), f32(lines_y, LANES)
    index = (SMEM, pltpu.SMEM(tile_row_block.shape, jnp.int32))
    tiles, term_y, anchor_y, *held, part = run(
        functools.partial(first_body, last),
        [pltpu.VMEM((slots, width, width), jnp.bfloat16), full_y, full_y, index, index]
        + [(SMEM, pltpu.SMEM((1, 1), jnp.int32)), (SMEM, pltpu.SMEM((2,), jnp.float32))]
        + [row_part(0)],
        [(ANY, far(tile_row_block)), (ANY, far(tile_column_block)), (SMEM, tile_count)]
        + [(ANY, far(step_sizes)), (ANY, far(tile_data))]
        + [(ANY, far(mask_y)), (ANY, far(lines(dual_cotangent)))],
        [
            scratch(lines_y, LANES),
            scratch(lines_x, LANES),
            pltpu.VMEM(mask_y.shape, jnp.int32),
            scratch(lines_y, LANES),
            pltpu.SemaphoreType.DMA((len(BOUNDS) - 1,)),
            pltpu.SemaphoreType.DMA((5,)),
        ],
        "first",
        cost,
    )
    *where, sizes = [
        (SMEM, pltpu.with_memory_space_constraint(array, pltpu.SMEM)) for array in held
    ]
    saved_part, tiles = run(
        saved_back_body,
        [row_part((iterations - 1) * lines_x)],
        where + [(VMEM, tiles), (VMEM, lines(saved_dual))],
        [scratch(iterations, lines_y, LANES), scratch(iterations, lines_x, LANES)],
        "saved_back",
        cost,
        tiles,
    )
    turned, tiles = run(
        turn_body,
        [pltpu.VMEM(tiles.shape, tiles.dtype)],
        [(VMEM, tiles)],
        [],
        "turn",
        cost,
        tiles,
    )
    saved_parts = [saved_part] + [None] * (n_row - 1)
    adjoint_x, anchor_x = lines(primal_cotangent), None
    terms_x, terms_y = [], [term_y]
    parts = [part] * n_row
    reduced = images = None
    pending = list(range(n_row - 1, 0, -1))

    def send_saved(own, after, count):
        (own,) = run(
            lambda *refs: None,
            [jax.ShapeDtypeStruct(own.shape, own.dtype)],
            [(VMEM, own), (VMEM, after)],
            [],
            f"after_{len(pending)}",
            handed=own,
        )
        for _ in range(count):
            offset = pending.pop(0)
            saved_parts[offset] = swap(own, "row", offset)
        saved_parts[0] = own

    for step in reversed(range(iterations)):
        parts = exchange(parts, "row")
        if step < last and pending:
            send_saved(saved_parts[0], saved_parts[n_row - 1], len(pending))
        groups = where + [sizes, (VMEM, turned), (VMEM, mask_x), (VMEM, parts)]
        groups += [(VMEM, adjoint_x), (VMEM, anchor_x)]
        body = functools.partial(primal_body, step, n_col)
        if step == 0:
            break
        term_x, adjoint_x, anchor_x, partial, turned = run(
            body,
            [full_x, full_x, full_x, full_y],
            groups,
            [scratch(lines_x, LANES)],
            f"primal_{step}",
            cost,
            turned,
        )
        terms_x.insert(0, term_x)
        part = run(
            pair_body,
            [jax.ShapeDtypeStruct((lines_y + SCALES, LANES), jnp.int16)],
            [(VMEM, partial), (VMEM, swap(partial, "col", 1))],
            [],
            f"pair_{step}",
        )[0]
        parts = exchange([part] * n_chip, "col", 2)
        if step == last:
            saved_parts[pending[0]] = swap(saved_part, "row", pending[0])
            pending = pending[1:]
        if step == 1:
            reduced, images, turned = run(
                saved_image_body,
                [f32(iterations, lines_x, LANES), f32(iterations, lines_y, LANES)],
                where
                + [sizes, (VMEM, turned), (VMEM, saved_parts)]
                + [(VMEM, lines(cost_vector)), (VMEM, lines(upper_bound))]
                + [(VMEM, lines(saved_primal))],
                [scratch(iterations, lines_x, LANES)],
                "saved_image",
                cost,
                turned,
            )
        groups = where + [sizes, (VMEM, tiles), (VMEM, mask_y), (VMEM, parts)]
        groups += [(VMEM, term_y), (VMEM, anchor_y)]
        if step == 1:
            groups += [(VMEM, lines(demand)), (VMEM, images), (VMEM, list(terms_y))]
            out = row_part(EXTRA)
        else:
            out = row_part(0)
        term_y, anchor_y, part, tiles = run(
            functools.partial(dual_body, step - 1, n_col),
            [full_y, full_y, out],
            groups,
            [scratch(lines_y, LANES), scratch(lines_x, LANES)],
            f"dual_{step - 1}",
            cost,
            tiles,
        )
        parts = [part] * n_row
        terms_y.insert(0, term_y)
    half_y = f32(n_chip * share_y + EXTRA, LANES)
    primal_adjoint, mine, other, turned = run(
        body,
        [pltpu.VMEM((lines_x, LANES), jnp.float32), half_y, half_y],
        groups + [(VMEM, reduced), (VMEM, terms_x)],
        [scratch(lines_x, LANES), scratch(lines_y, LANES)],
        "primal_0",
        cost,
        turned,
    )
    received = swap(other, "col", 1)
    parts = run(
        functools.partial(split_body, n_chip),
        [f32(share_y + EXTRA, LANES)] * n_chip,
        [(VMEM, mine), (VMEM, received)],
        [],
        "split",
    )
    parts = exchange(parts, "col", 2)
    scales = (1.0 / math.sqrt(column_length * n_col), 1.0 / math.sqrt(row_length * n_row))
    dual_adjoint, gradients = run(
        functools.partial(last_body, scales),
        [(ANY, f32(share_y, LANES)), (ANY, f32(2))],
        [sizes, (VMEM, parts[::-1]), (VMEM, term_y), (VMEM, anchor_y)],
        [
            scratch(share_y, LANES),
            pltpu.SMEM((2,), jnp.float32),
            pltpu.SemaphoreType.DMA((2,)),
        ],
        "last",
    )
    return (primal_adjoint.reshape(-1), dual_adjoint.reshape(-1), gradients)


def solution(mesh):
    placed = (
        P("row", "col", None, None, None),
        P("row", "col", None),
        P("row", "col", None),
        P("row", "col"),
        P(None, "col"),
        P(None, "row"),
        P(None, "col"),
        P(None, "row"),
        P("col"),
        P("row"),
        P("col"),
        P(),
        P("col"),
        P("row"),
    )
    return jax.shard_map(
        local,
        mesh=mesh,
        in_specs=placed,
        out_specs=(P("col"), P(("row", "col")), P()),
        check_vma=False,
    )
```

```python
import functools
import math

import jax
import jax.numpy as jnp
from jax import lax
from jax.experimental import pallas as pl
from jax.experimental.pallas import tpu as pltpu
from jax.sharding import PartitionSpec as P

LANES = 128
EXTRA = 16
BOUNDS = (0, 6, 12, 16)
SCALES = 16
STEPS = 64.0
LIMIT = 32760.0
FINE = 65000.0
LN2 = math.log(2.0)
VMEM = pl.BlockSpec(memory_space=pltpu.VMEM)
SMEM = pl.BlockSpec(memory_space=pltpu.SMEM)
ANY = pl.BlockSpec(memory_space=pl.ANY)
GRANT = 16 * 1024 * 1024


def weight_of(step):
    return (step + 1.0) / (step + 2.0)


def tree_sum(parts):
    while len(parts) > 1:
        parts = [parts[i] + parts[i + 1] for i in range(0, len(parts), 2)]
    return parts[0]


def fold(lines):
    return lines.reshape(-1, 8, LANES).sum(axis=0)


def rounded(values):
    return values.astype(jnp.bfloat16).astype(jnp.float32)


def add_products(in_index, out_index, count, tiles, slots, source, total):
    per_block = tiles.shape[-1] // LANES
    several = len(total.shape) == 3
    live_count = count[0, 0]
    for slot in slots:
        start = in_index[0, 0, slot] * per_block
        place = out_index[0, 0, slot] * per_block
        live = (live_count > slot).astype(jnp.float32)
        halves = []
        for half in range(per_block):
            if not several:
                halves.append(source[pl.ds(start + half, 1), :])
                continue
            vectors = source.shape[0]
            rows = -(-vectors // 8) * 8
            which = lax.broadcasted_iota(jnp.int32, (rows, LANES), 0)
            stacked = jnp.zeros((rows, LANES), jnp.float32)
            for vector in range(vectors):
                line = source[vector, pl.ds(start + half, 1), :]
                stacked = jnp.where(which == vector, line, stacked)
            halves.append(stacked)
        block = (jnp.concatenate(halves, axis=1) * live).astype(jnp.bfloat16)
        product = jnp.dot(block, tiles[slot], preferred_element_type=jnp.float32)
        for half in range(per_block):
            at = pl.ds(place + half, 1)
            lanes = slice(half * LANES, (half + 1) * LANES)
            if several:
                for vector in range(total.shape[0]):
                    total[vector, at, :] += product[vector : vector + 1, lanes]
            else:
                total[at, :] += product[:, lanes]


def whole_scale(lines):
    largest = jnp.maximum(jnp.max(jnp.abs(lines), axis=0, keepdims=True), 1e-30)
    return jnp.floor(jnp.log(largest) * (STEPS / LN2) + 1.0)


def to_units(code):
    return jnp.exp(code * (-LN2 / STEPS)) * LIMIT


def from_units(code):
    return jnp.exp(code * (LN2 / STEPS)) * (1.0 / LIMIT)


def nearest(values):
    return jnp.floor(values + 0.5)


def short(values):
    return values.astype(jnp.int32).astype(jnp.int16)


def long(values):
    return values.astype(jnp.int32).astype(jnp.float32)


def encode(lines):
    code = whole_scale(lines)
    return nearest(lines * to_units(code)), code


def encode_fine(lines):
    code = whole_scale(lines)
    units = lines * to_units(code)
    coarse = nearest(units)
    return coarse, nearest((units - coarse) * FINE), code


def scale_rows(codes):
    which = lax.broadcasted_iota(jnp.int32, (SCALES, LANES), 0)
    rows = jnp.zeros((SCALES, LANES), jnp.float32)
    for spot, code in enumerate(codes):
        rows = jnp.where(which == spot, code, rows)
    return short(rows)


def write_payload(out, lines):
    units, code = encode(lines)
    out[: lines.shape[0], :] = short(units)
    out[lines.shape[0] :, :] = scale_rows([code])


def scales_of(part):
    codes = long(part[part.shape[0] - SCALES :, :])
    return [from_units(codes[spot : spot + 1]) for spot in range(2)]


def first_body(
    step, rows_far, columns_far, count, sizes_far, tile_data, mask_far, cotangent_far,
    tiles, term, anchor, rows, columns, count_out, sizes, out,
    source, total, mask, cotangent, arrived, ready,
):
    count_out[0, 0] = count[0, 0]
    slots = tiles.shape[0]
    bounds = [slots * part // 16 for part in BOUNDS]
    pairs = [(mask_far, mask), (cotangent_far, cotangent)]
    pairs += [(rows_far, rows), (columns_far, columns), (sizes_far, sizes)]
    small = [
        pltpu.make_async_copy(far_ref, near, ready.at[spot])
        for spot, (far_ref, near) in enumerate(pairs)
    ]
    for copy in small:
        copy.start()

    def fetch(part):
        span = pl.ds(bounds[part], bounds[part + 1] - bounds[part])
        return pltpu.make_async_copy(tile_data.at[0, 0, span], tiles.at[span], arrived.at[part])

    for part in range(len(BOUNDS) - 1):
        fetch(part).start()
    total[...] = jnp.zeros_like(total)
    for copy in small:
        copy.wait()
    weight = weight_of(step)
    adjoint = cotangent[...]
    anchor[...] = (1.0 - weight) * adjoint
    value = mask[:, step, :].astype(jnp.float32) * weight * adjoint
    term[...] = value
    source[...] = rounded(value)
    for part in range(len(BOUNDS) - 1):
        fetch(part).wait()
        span = range(bounds[part], bounds[part + 1])
        add_products(rows, columns, count, tiles, span, source, total)
    write_payload(out, total[...])


def saved_back_body(rows, columns, count, tiles, saved, out, _, source, total):
    for vector in range(source.shape[0]):
        source[vector] = rounded(saved[:, vector, :])
    total[...] = jnp.zeros_like(total)
    add_products(rows, columns, count, tiles, range(tiles.shape[0]), source, total)
    write_payload(out, total[...].reshape(-1, LANES))


def saved_image_body(
    rows, columns, count, sizes, tiles, parts, cost, upper, primal, reduced, images, _, source
):
    vectors, lines, _ = reduced.shape
    scales = [scales_of(part)[0] for part in parts]
    for vector in range(vectors):
        at = slice(vector * lines, (vector + 1) * lines)
        sums = tree_sum([long(part[at, :]) * scale for part, scale in zip(parts, scales)])
        reduced[vector] = cost[...] - sums
        saved = primal[:, vector, :]
        half = jnp.minimum(jnp.maximum(saved - sizes[0] * reduced[vector], 0.0), upper[...])
        source[vector] = rounded(2.0 * half - saved)
    images[...] = jnp.zeros_like(images)
    add_products(columns, rows, count, tiles, range(tiles.shape[0]), source, images)


def turn_body(tiles, turned, _):
    for slot in range(tiles.shape[0]):
        turned[slot] = tiles[slot].T


def dual_body(step, n_col, rows, columns, count, sizes, tiles, mask, parts, before, anchor, *refs):
    last = step == 0
    if last:
        demand, images, terms, term, anchor_out, out, _, source, total = refs
    else:
        term, anchor_out, out, _, source, total = refs
    weight = weight_of(step)
    rows_y = before.shape[0]
    image = tree_sum([long(part[:rows_y, :]) * scales_of(part)[0] for part in parts])
    adjoint = before[...] + sizes[0] * image
    anchor_out[...] = anchor[...] + (1.0 - weight) * adjoint
    value = mask[:, step, :].astype(jnp.float32) * weight * adjoint
    term[...] = value
    source[...] = rounded(value)
    total[...] = jnp.zeros_like(total)
    add_products(rows, columns, count, tiles, range(tiles.shape[0]), source, total)
    lines = total.shape[0]
    units, code = encode(total[...])
    out[:lines, :] = short(units)
    if last:
        share = demand[...] * (1.0 / n_col)
        found = value * (share - images[0])
        for other, earlier in enumerate(terms):
            found += earlier[...] * (share - images[other + 1])
        coarse, fine, found_code = encode_fine(fold(found))
        out[lines : lines + EXTRA, :] = short(jnp.concatenate([coarse, fine], axis=0))
        out[lines + EXTRA :, :] = scale_rows([code, found_code])
    else:
        out[lines:, :] = scale_rows([code])


def primal_body(step, n_col, rows, columns, count, sizes, tiles, mask, parts, before, anchor, *refs):
    last = step == 0
    if last:
        reduced, terms, final, mine, other, _, source, out = refs
    else:
        term, adjoint_out, anchor_out, out, _, source = refs
    sigma = sizes[1]
    weight = weight_of(step)
    lines = mask.shape[0]
    scales = [scales_of(part) for part in parts]
    back = tree_sum([long(part[:lines, :]) * scale[0] for part, scale in zip(parts, scales)])
    adjoint = before[...]
    anchored = (1.0 - weight) * adjoint
    if anchor is not None:
        anchored = anchor[...] + anchored
    value = mask[:, step, :].astype(jnp.float32) * (weight * adjoint - 2.0 * sigma * back)
    after = value + sigma * back
    if last:
        final[...] = after + anchored
    else:
        term[...] = value
        adjoint_out[...] = after
        anchor_out[...] = anchored
    all_slots = range(tiles.shape[0])
    source[...] = rounded(value)
    out[...] = jnp.zeros_like(out)
    add_products(columns, rows, count, tiles, all_slots, source, out)
    if last:
        sums = 0.0
        for part, scale in zip(parts, scales):
            units = long(part[lines : lines + EXTRA, :])
            sums += (units[:8] + units[8:] * (1.0 / FINE)) * scale[1]
        found = value * reduced[0]
        for other_step, later in enumerate(terms):
            found += later[...] * reduced[other_step + 1]
        tail = jnp.concatenate([sums, -fold(found)], axis=0)
        share = out.shape[0] // n_col
        core = lax.axis_index("col") % 2
        for chip in range(n_col // 2):
            span = slice(chip * share, (chip + 1) * share)
            mine[span, :] = out[pl.ds((2 * chip + core) * share, share), :]
            other[span, :] = out[pl.ds((2 * chip + 1 - core) * share, share), :]
        mine[n_col // 2 * share :, :] = tail
        other[n_col // 2 * share :, :] = tail


def pair_body(mine, received, out):
    lines = mine.shape[0]
    units, code = encode(mine[...] + received[...])
    out[:lines, :] = short(units)
    out[lines:, :] = scale_rows([code])


def split_body(n_chip, mine, received, *outs):
    share = (mine.shape[0] - EXTRA) // n_chip
    chip = lax.axis_index("col") // 2
    tail = mine[n_chip * share :, :] + received[n_chip * share :, :]
    for part, out in enumerate(outs):
        at = pl.ds((chip ^ part) * share, share)
        out[:share, :] = mine[at, :] + received[at, :]
        out[share:, :] = tail


def last_body(
    scales, sizes, parts, term, anchor, adjoint_far, gradients_far, adjoint, gradients, sent
):
    share = adjoint.shape[0]
    total = tree_sum([part[...] for part in parts])
    at = pl.ds(lax.axis_index("col") * share, share)
    adjoint[...] = term[at, :] + sizes[0] * total[:share] + anchor[at, :]
    first = pltpu.make_async_copy(adjoint, adjoint_far, sent.at[0])
    first.start()
    gradients[0] = jnp.sum(total[share + 8 : share + 16]) * scales[0]
    gradients[1] = jnp.sum(total[share : share + 8]) * scales[1]
    second = pltpu.make_async_copy(gradients, gradients_far, sent.at[1])
    second.start()
    first.wait()
    second.wait()


def far(array):
    return pltpu.with_memory_space_constraint(array, pltpu.HBM)


def run(body, out_shape, groups, scratch, name, cost=None, tiles=None, handed=None):
    flat, specs, widths, aliases = [], [], [], {}
    for spec, value in groups:
        if value is None:
            widths.append(None)
            continue
        many = isinstance(value, (list, tuple))
        widths.append(len(value) if many else 0)
        for array in value if many else [value]:
            if array is handed:
                aliases[len(flat)] = 0
            if array is tiles:
                aliases[len(flat)] = len(out_shape)
                array = pltpu.with_memory_space_constraint(array, pltpu.VMEM)
            flat.append(array)
            specs.append(spec)

    def kernel(*refs):
        given = list(refs)
        taken = []
        for width in widths:
            if width is None:
                taken.append(None)
            elif width == 0:
                taken.append(given.pop(0))
            else:
                taken.append([given.pop(0) for _ in range(width)])
        body(*taken, *given)

    out_specs = [shape[0] if isinstance(shape, tuple) else VMEM for shape in out_shape]
    shapes = [shape[1] if isinstance(shape, tuple) else shape for shape in out_shape]
    if tiles is not None:
        shapes.append(pltpu.VMEM(tiles.shape, tiles.dtype))
        out_specs.append(VMEM)
    return pl.pallas_call(
        kernel,
        out_shape=shapes,
        in_specs=specs,
        out_specs=out_specs,
        scratch_shapes=scratch,
        input_output_aliases=aliases,
        compiler_params=pltpu.CompilerParams(vmem_limit_bytes=GRANT),
        cost_estimate=cost,
        name=name,
    )(*flat)


def swap(array, axis, stride):
    size = lax.axis_size(axis)
    return lax.ppermute(array, axis, [(i, i ^ stride) for i in range(size)])


def exchange(parts, axis, stride=1):
    size = lax.axis_size(axis) // stride
    return [parts[0]] + [swap(parts[k], axis, k * stride) for k in range(1, size)]


def local(
    tile_data,
    tile_row_block,
    tile_column_block,
    tile_count,
    saved_primal,
    saved_dual,
    primal_mask,
    dual_mask,
    cost_vector,
    demand,
    upper_bound,
    step_sizes,
    primal_cotangent,
    dual_cotangent,
):
    slots, width = tile_data.shape[2], tile_data.shape[-1]
    iterations, row_length = saved_dual.shape
    column_length = saved_primal.shape[1]
    n_row, n_col = lax.axis_size("row"), lax.axis_size("col")
    n_chip = n_col // 2
    lines_y, lines_x = row_length // LANES, column_length // LANES
    share_y = lines_y // n_col
    last = iterations - 1
    cost = pl.CostEstimate(
        flops=2 * tile_data.size, bytes_accessed=2 * tile_data.size, transcendentals=0
    )

    def lines(array):
        if array.ndim == 1:
            return array.reshape(-1, LANES)
        return array.reshape(iterations, -1, LANES).transpose(1, 0, 2)

    def f32(*shape):
        return jax.ShapeDtypeStruct(shape, jnp.float32)

    def row_part(more):
        return jax.ShapeDtypeStruct((lines_x + more + SCALES, LANES), jnp.int16)

    def scratch(*shape):
        return pltpu.VMEM(shape, jnp.float32)

    mask_x, mask_y = lines(primal_mask), lines(dual_mask)
    full_x, full_y = f32(lines_x, LANES), f32(lines_y, LANES)
    index = (SMEM, pltpu.SMEM(tile_row_block.shape, jnp.int32))
    tiles, term_y, anchor_y, *held, part = run(
        functools.partial(first_body, last),
        [pltpu.VMEM((slots, width, width), jnp.bfloat16), full_y, full_y, index, index]
        + [(SMEM, pltpu.SMEM((1, 1), jnp.int32)), (SMEM, pltpu.SMEM((2,), jnp.float32))]
        + [row_part(0)],
        [(ANY, far(tile_row_block)), (ANY, far(tile_column_block)), (SMEM, tile_count)]
        + [(ANY, far(step_sizes)), (ANY, far(tile_data))]
        + [(ANY, far(mask_y)), (ANY, far(lines(dual_cotangent)))],
        [
            scratch(lines_y, LANES),
            scratch(lines_x, LANES),
            pltpu.VMEM(mask_y.shape, jnp.int32),
            scratch(lines_y, LANES),
            pltpu.SemaphoreType.DMA((len(BOUNDS) - 1,)),
            pltpu.SemaphoreType.DMA((5,)),
        ],
        "first",
        cost,
    )
    *where, sizes = [
        (SMEM, pltpu.with_memory_space_constraint(array, pltpu.SMEM)) for array in held
    ]
    saved_part, tiles = run(
        saved_back_body,
        [row_part((iterations - 1) * lines_x)],
        where + [(VMEM, tiles), (VMEM, lines(saved_dual))],
        [scratch(iterations, lines_y, LANES), scratch(iterations, lines_x, LANES)],
        "saved_back",
        cost,
        tiles,
    )
    turned, tiles = run(
        turn_body,
        [pltpu.VMEM(tiles.shape, tiles.dtype)],
        [(VMEM, tiles)],
        [],
        "turn",
        cost,
        tiles,
    )
    saved_parts = [saved_part] + [None] * (n_row - 1)
    adjoint_x, anchor_x = lines(primal_cotangent), None
    terms_x, terms_y = [], [term_y]
    parts = [part] * n_row
    reduced = images = None
    pending = list(range(n_row - 1, 0, -1))

    def send_saved(own, after, count):
        (own,) = run(
            lambda *refs: None,
            [jax.ShapeDtypeStruct(own.shape, own.dtype)],
            [(VMEM, own), (VMEM, after)],
            [],
            f"after_{len(pending)}",
            handed=own,
        )
        for _ in range(count):
            offset = pending.pop(0)
            saved_parts[offset] = swap(own, "row", offset)
        saved_parts[0] = own

    for step in reversed(range(iterations)):
        parts = exchange(parts, "row")
        if step < last and pending:
            send_saved(saved_parts[0], saved_parts[1], len(pending))
        groups = where + [sizes, (VMEM, turned), (VMEM, mask_x), (VMEM, parts)]
        groups += [(VMEM, adjoint_x), (VMEM, anchor_x)]
        body = functools.partial(primal_body, step, n_col)
        if step == 0:
            break
        term_x, adjoint_x, anchor_x, partial, turned = run(
            body,
            [full_x, full_x, full_x, full_y],
            groups,
            [scratch(lines_x, LANES)],
            f"primal_{step}",
            cost,
            turned,
        )
        terms_x.insert(0, term_x)
        part = run(
            pair_body,
            [jax.ShapeDtypeStruct((lines_y + SCALES, LANES), jnp.int16)],
            [(VMEM, partial), (VMEM, swap(partial, "col", 1))],
            [],
            f"pair_{step}",
        )[0]
        parts = exchange([part] * n_chip, "col", 2)
        if step == last:
            saved_parts[1] = swap(saved_part, "row", 1)
            pending = pending[:-1]
        if step == 1:
            reduced, images, turned = run(
                saved_image_body,
                [f32(iterations, lines_x, LANES), f32(iterations, lines_y, LANES)],
                where
                + [sizes, (VMEM, turned), (VMEM, saved_parts)]
                + [(VMEM, lines(cost_vector)), (VMEM, lines(upper_bound))]
                + [(VMEM, lines(saved_primal))],
                [scratch(iterations, lines_x, LANES)],
                "saved_image",
                cost,
                turned,
            )
        groups = where + [sizes, (VMEM, tiles), (VMEM, mask_y), (VMEM, parts)]
        groups += [(VMEM, term_y), (VMEM, anchor_y)]
        if step == 1:
            groups += [(VMEM, lines(demand)), (VMEM, images), (VMEM, list(terms_y))]
            out = row_part(EXTRA)
        else:
            out = row_part(0)
        term_y, anchor_y, part, tiles = run(
            functools.partial(dual_body, step - 1, n_col),
            [full_y, full_y, out],
            groups,
            [scratch(lines_y, LANES), scratch(lines_x, LANES)],
            f"dual_{step - 1}",
            cost,
            tiles,
        )
        parts = [part] * n_row
        terms_y.insert(0, term_y)
    half_y = f32(n_chip * share_y + EXTRA, LANES)
    primal_adjoint, mine, other, turned = run(
        body,
        [pltpu.VMEM((lines_x, LANES), jnp.float32), half_y, half_y],
        groups + [(VMEM, reduced), (VMEM, terms_x)],
        [scratch(lines_x, LANES), scratch(lines_y, LANES)],
        "primal_0",
        cost,
        turned,
    )
    received = swap(other, "col", 1)
    parts = run(
        functools.partial(split_body, n_chip),
        [f32(share_y + EXTRA, LANES)] * n_chip,
        [(VMEM, mine), (VMEM, received)],
        [],
        "split",
    )
    parts = exchange(parts, "col", 2)
    scales = (1.0 / math.sqrt(column_length * n_col), 1.0 / math.sqrt(row_length * n_row))
    dual_adjoint, gradients = run(
        functools.partial(last_body, scales),
        [(ANY, f32(share_y, LANES)), (ANY, f32(2))],
        [sizes, (VMEM, parts[::-1]), (VMEM, term_y), (VMEM, anchor_y)],
        [
            scratch(share_y, LANES),
            pltpu.SMEM((2,), jnp.float32),
            pltpu.SemaphoreType.DMA((2,)),
        ],
        "last",
    )
    return (primal_adjoint.reshape(-1), dual_adjoint.reshape(-1), gradients)


def solution(mesh):
    placed = (
        P("row", "col", None, None, None),
        P("row", "col", None),
        P("row", "col", None),
        P("row", "col"),
        P(None, "col"),
        P(None, "row"),
        P(None, "col"),
        P(None, "row"),
        P("col"),
        P("row"),
        P("col"),
        P(),
        P("col"),
        P("row"),
    )
    return jax.shard_map(
        local,
        mesh=mesh,
        in_specs=placed,
        out_specs=(P("col"), P(("row", "col")), P()),
        check_vma=False,
    )
```
